512 devices in a mesh: dp: 16 (over y, z_lo), ctx: 32 (over x, z_hi, core).
Axes of the slice: x: 4, y: 8, z: 8 (z_hi: 4, z_lo: 2; z = z_hi * 2 + z_lo), core: 2. Of those that a mesh axis runs over, the one named last changes fastest.
Arguments:
- queries: bfloat16 [8192, 12288], P('ctx', 'dp'), may hold values from -48 to 48
- latent: bfloat16 [8192, 576], P('ctx'), may hold values from -20 to 20
- grad_out: bfloat16 [8192, 8192], P('ctx', 'dp'), may hold values from -6 to 6
- doc_ids: int32 [8192], P('ctx'), may hold values from 0 to 31, never falling along the last dimension, each value on 1 to 1024 neighbouring positions
- up_key: bfloat16 [512, 8192], P(None, 'dp'), may hold values from -0.25 to 0.25
- up_value: bfloat16 [512, 8192], P(None, 'dp'), may hold values from -0.25 to 0.25
Outputs:
- grad_queries: bfloat16 [8192, 12288], P('ctx', 'dp')
- grad_latent: float32 [8192, 576], P('ctx')
- grad_up_key: float32 [512, 8192], P('ctx', 'dp')
- grad_up_value: float32 [512, 8192], P('ctx', 'dp')
The draws below stay inside these ranges and needn't reach their ends.
Inputs may be any that keep to these rules, and one draw needn't show every extreme that they name: doc_ids never fall along the sequence; a document holds 1 to 1024 tokens, and one holds exactly 1024.
All inputs are finite; a program needn't handle non-finite values.
Results may differ from the reference program's by a relative error of at most 0.0071.
Values may be sent and summed in bfloat16 or wider, within the bound.
A program may use at most 128 MiB of HBM per device.

```python
import math
import jax
import jax.numpy as jnp
import numpy as np
from jax import lax

LAT = 512
ROPE = 64
NOPE = 128
VDIM = 128
HEADS = 64
TOK_DEV = 256
WIN = 4
TOKENS = 8192
N_CTX = 32


def draw_queries(key, part):
    key = jax.random.fold_in(key, 11)
    base = jnp.clip(jax.random.normal(key, (TOKENS, HEADS, NOPE + ROPE), jnp.float32), -6.0, 6.0)
    return base.reshape(TOKENS, HEADS * (NOPE + ROPE)).astype(jnp.bfloat16)


def draw_latent(key, part):
    key = jax.random.fold_in(key, 23)
    base = jnp.clip(jax.random.normal(key, (TOKENS, LAT + ROPE), jnp.float32), -6.0, 6.0)
    return base.astype(jnp.bfloat16)


def block_scale(stream_key, extent, cuts, smallest, top_value):
    factor_of, own = 1.0, jax.random.fold_in(stream_key, 6)
    for axis_at, parts in cuts:
        steps = jnp.exp(jax.random.uniform(jax.random.fold_in(own, axis_at), (parts,), jnp.float32, smallest / len(cuts), top_value / len(cuts)))
        factor_of = factor_of * jnp.repeat(steps, extent[axis_at] // parts).reshape([-1 if axis == axis_at else 1 for axis in range(len(extent))])
    return factor_of


def split_up(amount, total, limit, skew):
    portions = [(1 << 20) // math.isqrt(grade ** skew) + 1 for grade in range(2, amount + 1)]
    spare, given = total - limit - (amount - 1), [1] * (amount - 1)
    while spare > 0:
        free = [i for i in range(amount - 1) if given[i] < limit]
        pool, remaining = sum([portions[i] for i in free]), spare
        for i in free:
            addition = min(limit - given[i], max(1, remaining * portions[i] // pool), spare)
            given[i] = given[i] + addition
            spare = spare - addition
    return np.array([limit] + given)


def ragged_sizes(rng, number_of, total, limit, lean):
    if number_of == 2:
        one = jax.random.randint(rng, (), max(1, total - limit), min(limit, total - 1) + 1)
        return jnp.stack([one, total - one])
    tallies = jnp.asarray(split_up(number_of, total, limit, lean), jnp.int32)
    pairs = (number_of - 1) // 2
    source_of, taker = tallies[1:1 + 2 * pairs:2], tallies[2:2 + 2 * pairs:2]
    slack = jnp.minimum(source_of - 1, limit - taker)
    moved = jax.random.randint(jax.random.fold_in(rng, 1), (pairs,), 0, 1 << 20) % (slack + 1)
    tallies = tallies.at[1:1 + 2 * pairs:2].set(source_of - moved).at[2:2 + 2 * pairs:2].set(taker + moved)
    return tallies[jax.random.permutation(jax.random.fold_in(rng, 2), number_of)]


def bell_draw(own_key, shape, deviation, bound, shards=(), kind=jnp.bfloat16):
    factor_of = block_scale(own_key, shape, shards, -0.22, 0.18) if shards else 1.0
    result = jax.random.normal(own_key, shape, jnp.float32) * deviation * factor_of
    return jnp.minimum(jnp.maximum(result, -bound), bound).astype(kind)


def setup_inputs(seed: int = 0) -> dict:
    keys = jax.random.split(jax.random.key(seed), 7)
    queries = draw_queries(jax.random.fold_in(keys[6], 71), 0)
    latent = draw_latent(jax.random.fold_in(keys[6], 71), 0)
    grad_out = bell_draw(keys[2], (TOKENS, HEADS * VDIM), 1.0, 6.0, ((0, 32), (1, 16)))
    doc_ids = jnp.searchsorted(jnp.cumsum(ragged_sizes(keys[3], N_CTX, TOKENS, WIN * TOK_DEV, 2)), jnp.arange(TOKENS), side="right").astype(jnp.int32)
    up_key = bell_draw(keys[4], (LAT, HEADS * NOPE), LAT ** -0.5, 0.25, ((1, 16),))
    up_value = bell_draw(keys[5], (LAT, HEADS * VDIM), LAT ** -0.5, 0.25, ((1, 16),))
    return {"queries": queries, "latent": latent, "grad_out": grad_out, "doc_ids": doc_ids, "up_key": up_key, "up_value": up_value}


def reference(queries, latent, grad_out, doc_ids, up_key, up_value):
    tokens = queries.shape[0]
    head_count = up_key.shape[1] // NOPE
    score_scale = (NOPE + ROPE) ** -0.5
    latent_part = latent[:, :LAT]
    rope_key = latent[:, LAT:]
    key_flat = jnp.dot(latent_part, up_key, preferred_element_type=jnp.float32).astype(jnp.bfloat16)
    value_flat = jnp.dot(latent_part, up_value, preferred_element_type=jnp.float32).astype(jnp.bfloat16)
    pad_rows = WIN * TOK_DEV
    window_rows = (WIN + 1) * TOK_DEV
    key_pad = jnp.concatenate([jnp.zeros((pad_rows, head_count * NOPE), jnp.bfloat16), key_flat], axis=0).reshape(-1, head_count, NOPE)
    value_pad = jnp.concatenate([jnp.zeros((pad_rows, head_count * VDIM), jnp.bfloat16), value_flat], axis=0).reshape(-1, head_count, VDIM)
    rope_pad = jnp.concatenate([jnp.zeros((pad_rows, ROPE), jnp.bfloat16), rope_key], axis=0)
    doc_pad = jnp.concatenate([jnp.full((pad_rows,), -1, jnp.int32), doc_ids.astype(jnp.int32)], axis=0)
    pos_pad = jnp.arange(tokens + pad_rows, dtype=jnp.int32) - pad_rows
    query_split = queries.reshape(tokens, head_count, NOPE + ROPE)
    grad_rows = grad_out.reshape(tokens, head_count, VDIM)

    def one_block(running, block_index):
        acc_nope, acc_rope, acc_value = running
        first_row = (block_index * TOK_DEV).astype(jnp.int32)
        query_block = lax.dynamic_slice_in_dim(query_split, first_row, TOK_DEV, 0).astype(jnp.float32)
        query_nope = query_block[:, :, :NOPE]
        query_rope = query_block[:, :, NOPE:]
        grad_block = lax.dynamic_slice_in_dim(grad_rows, first_row, TOK_DEV, 0).astype(jnp.float32)
        my_docs = lax.dynamic_slice_in_dim(doc_ids.astype(jnp.int32), first_row, TOK_DEV, 0)
        my_positions = first_row + jnp.arange(TOK_DEV, dtype=jnp.int32)
        keys_win = lax.dynamic_slice_in_dim(key_pad, first_row, window_rows, 0).astype(jnp.float32)
        values_win = lax.dynamic_slice_in_dim(value_pad, first_row, window_rows, 0).astype(jnp.float32)
        rope_win = lax.dynamic_slice_in_dim(rope_pad, first_row, window_rows, 0).astype(jnp.float32)
        docs_win = lax.dynamic_slice_in_dim(doc_pad, first_row, window_rows, 0)
        pos_win = lax.dynamic_slice_in_dim(pos_pad, first_row, window_rows, 0)
        allowed = (my_docs[:, None] == docs_win[None, :]) & (pos_win[None, :] <= my_positions[:, None])
        scores = score_scale * (jnp.einsum("ihd,jhd->hij", query_nope, keys_win) + jnp.einsum("ihd,jd->hij", query_rope, rope_win))
        masked = jnp.where(allowed[None], scores, -jnp.inf)
        row_max = jnp.max(masked, axis=2)
        row_total = jnp.sum(jnp.where(allowed[None], jnp.exp(masked - row_max[:, :, None]), 0.0), axis=2)
        row_lse = row_max + jnp.log(row_total)
        prob_rows = jnp.where(allowed[None], jnp.exp(scores - row_lse[:, :, None]), 0.0)
        grad_probs = jnp.einsum("ihd,jhd->hij", grad_block, values_win)
        row_delta = jnp.sum(prob_rows * grad_probs, axis=2)
        grad_low = (score_scale * prob_rows * (grad_probs - row_delta[:, :, None])).astype(jnp.bfloat16)
        grad_scores = lax.optimization_barrier(grad_low).astype(jnp.float32)
        prob_low = lax.optimization_barrier(prob_rows.astype(jnp.bfloat16)).astype(jnp.float32)
        dq_nope = jnp.einsum("hij,jhd->ihd", grad_scores, keys_win)
        dq_rope = jnp.einsum("hij,jd->ihd", grad_scores, rope_win)
        dq_block = jnp.concatenate([dq_nope, dq_rope], axis=2).reshape(TOK_DEV, -1).astype(jnp.bfloat16)
        part_nope = jnp.einsum("hij,ihd->jhd", grad_scores, query_nope)
        part_rope = jnp.einsum("hij,ihd->jd", grad_scores, query_rope)
        part_value = jnp.einsum("hij,ihd->jhd", prob_low, grad_block)
        acc_nope = lax.dynamic_update_slice_in_dim(acc_nope, lax.dynamic_slice_in_dim(acc_nope, first_row, window_rows, 0) + part_nope, first_row, 0)
        acc_rope = lax.dynamic_update_slice_in_dim(acc_rope, lax.dynamic_slice_in_dim(acc_rope, first_row, window_rows, 0) + part_rope, first_row, 0)
        acc_value = lax.dynamic_update_slice_in_dim(acc_value, lax.dynamic_slice_in_dim(acc_value, first_row, window_rows, 0) + part_value, first_row, 0)
        return (acc_nope, acc_rope, acc_value), dq_block

    start_state = (jnp.zeros((tokens + pad_rows, head_count, NOPE), jnp.float32),
                   jnp.zeros((tokens + pad_rows, ROPE), jnp.float32),
                   jnp.zeros((tokens + pad_rows, head_count, VDIM), jnp.float32))
    final_state, dq_blocks = lax.scan(one_block, start_state, jnp.arange(N_CTX, dtype=jnp.int32))
    acc_nope, acc_rope, acc_value = final_state
    grad_queries = dq_blocks.reshape(tokens, -1)
    grad_key_nope = acc_nope[pad_rows:].reshape(tokens, -1)
    grad_values = acc_value[pad_rows:].reshape(tokens, -1)
    grad_key_rope = acc_rope[pad_rows:]
    highest = lax.Precision.HIGHEST
    latent_wide = latent_part.astype(jnp.float32)
    grad_up_key = jnp.dot(latent_wide.T, grad_key_nope, precision=highest)
    grad_up_value = jnp.dot(latent_wide.T, grad_values, precision=highest)
    latent_grad = jnp.dot(grad_key_nope, up_key.astype(jnp.float32).T, precision=highest) + jnp.dot(grad_values, up_value.astype(jnp.float32).T, precision=highest)
    grad_latent = jnp.concatenate([latent_grad, grad_key_rope], axis=1)
    return (grad_queries, grad_latent, grad_up_key, grad_up_value)
```

```python
import functools
import jax
import jax.numpy as jnp
from jax import lax
from jax.experimental import pallas as pl
from jax.experimental.pallas import tpu as pltpu
from jax.sharding import PartitionSpec as P

LAT = 512
ROPE = 64
NOPE = 128
ROWS = 256
HEADS_HERE = 4
WIDE = 640
SLOTS = 5
SCALE = (NOPE + ROPE) ** -0.5
LOG2E = 1.4426950408889634
LOW = -1e30
MESH = pl.DeviceIdType.MESH
F32 = jnp.float32
BF16 = jnp.bfloat16
NT = (((1,), (1,)), ((), ()))
NN = (((1,), (0,)), ((), ()))


def mm(a, b, dims=NN):
    return lax.dot_general(a, b, dims, preferred_element_type=F32)


def kernel(
    q_ref, lat_ref, go_ref, doc_ref, upk_ref, upv_ref,
    dq_ref, dlat_ref, dupk_ref, dupv_ref,
    win, qx, ups, kv, kxt, latt, probs, gprobs, stats, bias, dqt, dkv,
    part, sib_out, sib_in, ys_out, ys_own, ys_in, own_out, own_in, own_keep, gather,
    g_out, g_in, g_own, gx_out, gx_in, gz_out, gz_in,
    s_near, r_near, s_y, r_y, s_fw, r_fw, s_sib, r_sib, s_ys, r_ys,
    s_own, r_own, s_ag, r_ag, s_g, r_g, s_gx, r_gx, s_gz, r_gz,
):
    dp = lax.axis_index("dp")
    ctx = lax.axis_index("ctx")
    y, zl = lax.div(dp, 2), lax.rem(dp, 2)
    x, zh, core = lax.div(ctx, 8), lax.rem(lax.div(ctx, 2), 4), lax.rem(ctx, 2)
    sib = (dp, ctx + 1 - 2 * core)

    def at_ctx(by):
        return lax.rem(ctx + by + 32, 32)

    def at_y(by):
        return (lax.rem(y + by + 8, 8) * 2 + zl, ctx)

    def at_dp(by):
        return (lax.rem(dp + by + 16, 16), ctx)

    def at_x(by):
        return (dp, lax.rem(x + by + 4, 4) * 8 + zh * 2 + core)

    def at_zh(by):
        return (dp, x * 8 + lax.rem(zh + by + 4, 4) * 2 + core)

    def owner(by, other):
        mate = dp + 1 - 2 * zl if other else dp
        return (mate, at_ctx(by))

    barrier = pltpu.get_barrier_semaphore()
    senders = [sib, (dp, at_ctx(-2)), (dp, at_ctx(-4))]
    senders += [owner(by, other) for by in (0, 2, 4) for other in (0, 1) if by or other]
    senders += [at_dp(-i) for i in range(1, 16)]
    senders += [at_x(-i) for i in range(1, 4)]
    senders += [at_zh(-i) for i in range(1, 4)]
    for sender in senders:
        pl.semaphore_signal(barrier, inc=1, device_id=sender, device_id_type=MESH)

    def remote(src, dst, send, recv, to):
        return pltpu.make_async_remote_copy(
            src_ref=src, dst_ref=dst, send_sem=send, recv_sem=recv,
            device_id=to, device_id_type=MESH,
        )

    doc_row = doc_ref[...].astype(F32)
    line = lax.broadcasted_iota(jnp.int32, (ROWS, ROWS), 0)
    lane = lax.broadcasted_iota(jnp.int32, (ROWS, ROWS), 1)
    doc_col = jnp.sum(jnp.where(line == lane, doc_row, 0.0), axis=1, keepdims=True)
    win[4, :, :LAT] = lat_ref[:, :LAT]
    tail = jnp.concatenate([lat_ref[:, LAT:].astype(F32), jnp.zeros((ROWS, 64), F32)], axis=1)
    tail_lane = lax.broadcasted_iota(jnp.int32, (ROWS, 128), 1)
    win[4, :, LAT:] = jnp.where(tail_lane == 64, doc_col, tail).astype(BF16)

    pl.semaphore_wait(barrier, len(senders))

    def shares(slot, who):
        return win.at[slot, pl.ds(pl.multiple_of(who * 32, 32), 32), :]

    to_near = remote(shares(4, y), shares(2, y), s_near.at[0], r_near.at[0], (dp, at_ctx(2)))
    to_far = remote(shares(4, y), shares(0, y), s_near.at[1], r_near.at[1], (dp, at_ctx(4)))
    to_far.start()
    to_near.start()

    fw_own = remote(win.at[4], win.at[3], s_fw.at[0], r_fw.at[0], sib)
    fw_mid = remote(win.at[2], win.at[3], s_fw.at[0], r_fw.at[0], sib)
    fw_mid_low = remote(win.at[2], win.at[1], s_fw.at[1], r_fw.at[1], sib)
    fw_far_low = remote(win.at[0], win.at[1], s_fw.at[1], r_fw.at[1], sib)

    @pl.when(core == 0)
    def _():
        fw_own.start()

    def along_y(slot, index, by):
        return remote(
            shares(slot, y), shares(slot, y), s_y.at[index, by - 1], r_y.at[index, by - 1], at_y(by)
        )

    for h in range(HEADS_HERE):
        qx[:, h * 256 : h * 256 + 128] = q_ref[:, h * 192 : h * 192 + 128]
        qx[:, h * 256 + 128 : h * 256 + 256] = jnp.concatenate(
            [q_ref[:, h * 192 + 128 : h * 192 + 192], jnp.zeros((ROWS, 64), BF16)], axis=1
        )
    ups[:, :512] = upk_ref[...]
    ups[:, 512:] = upv_ref[...]
    dqt[...] = jnp.zeros_like(dqt)

    to_far.wait_recv()
    for by in (4, 3, 5, 2, 6, 1, 7):
        along_y(0, 1, by).start()
    to_near.wait_recv()
    for by in (4, 3, 5, 2, 6, 1, 7):
        along_y(2, 0, by).start()

    def scores(t, carry):
        slot = lax.rem(4 + 3 * t, 5)

        @pl.when(t == 1)
        def _():
            for by in range(1, 8):
                along_y(2, 0, by).wait_recv()

            @pl.when(core == 0)
            def _():
                fw_mid_low.start()

            @pl.when(core == 1)
            def _():
                fw_mid.start()

        @pl.when(t == 2)
        def _():
            for by in range(1, 8):
                along_y(0, 1, by).wait_recv()

            @pl.when(core == 1)
            def _():
                fw_far_low.start()

        @pl.when(t == 3)
        def _():
            fw_own.wait_recv()

        @pl.when(t == 4)
        def _():
            fw_mid_low.wait_recv()

        start = pl.multiple_of(slot * ROWS, ROWS)
        block = win[slot]
        latent = block[:, :LAT]
        rope = block[:, LAT:]
        for n in range(4):
            kv[pl.ds(start, ROWS), n * 256 : n * 256 + 256] = mm(
                latent, ups[:, n * 256 : n * 256 + 256]
            ).astype(BF16)
        keys = kv[pl.ds(start, ROWS), :512]
        kxt[slot, :512, :] = keys.T
        kxt[slot, 512:, :] = rope.T
        flipped = latent.T
        for g in range(32):
            row = (g % 2) * 256 + (g // 2) * 16
            latt[row : row + 16, pl.ds(start, ROWS)] = flipped[g * 16 : g * 16 + 16, :]
        docs = rope[:, 64:65].astype(F32)
        past = jnp.logical_or(slot < 4, line <= lane)
        bias[...] = jnp.where(jnp.logical_and(docs == doc_row, past), 0.0, LOW)
        for h in range(HEADS_HERE):
            cols = slice(h * 256, h * 256 + 256)
            key = kv[pl.ds(start, ROWS), h * 128 : h * 128 + 128]
            value = kv[pl.ds(start, ROWS), 512 + h * 128 : 640 + h * 128]
            s = mm(jnp.concatenate([key, rope], axis=1), qx[:, cols], NT) + bias[...]
            top = jnp.max(s, axis=0, keepdims=True)
            p = jnp.exp2((s - top) * (SCALE * LOG2E))
            gp = mm(value, go_ref[:, h * 128 : h * 128 + 128], NT)
            probs[pl.ds(start, ROWS), cols] = p
            gprobs[pl.ds(start, ROWS), cols] = gp
            stats[0, pl.ds(slot, 1), cols] = top
            stats[1, pl.ds(slot, 1), cols] = jnp.sum(p, axis=0, keepdims=True)
            stats[2, pl.ds(slot, 1), cols] = jnp.sum(p * gp, axis=0, keepdims=True)
        return carry

    lax.fori_loop(0, SLOTS, scores, 0)

    tops = stats[0, 0:SLOTS, :]
    factor = jnp.exp2((tops - jnp.max(tops, axis=0, keepdims=True)) * (SCALE * LOG2E))
    total = jnp.sum(stats[1, 0:SLOTS, :] * factor, axis=0, keepdims=True)
    delta = jnp.sum(stats[2, 0:SLOTS, :] * factor, axis=0, keepdims=True) / total
    stats[0, 0:SLOTS, :] = factor / total
    stats[1, 0:1, :] = delta

    up_low = remote(sib_out.at[0], sib_in.at[0], s_sib.at[0], r_sib.at[0], sib)
    up_high = remote(sib_out.at[1], sib_in.at[1], s_sib.at[1], r_sib.at[1], sib)

    def scatter_y(index, by):
        there = pl.multiple_of(lax.rem(y + by, 8) * 32, 32)
        return remote(
            ys_out.at[index, pl.ds(there, 32), :], ys_in.at[index, by - 1],
            s_ys.at[index, by - 1], r_ys.at[index, by - 1], at_y(by),
        )

    def grads(t, carry):
        slot = jnp.minimum(t + 1 - 2 * lax.rem(t, 2), 4)
        start = pl.multiple_of(slot * ROWS, ROWS)
        rope_sum = jnp.zeros((ROWS, 128), F32)
        for h in range(HEADS_HERE):
            cols = slice(h * 256, h * 256 + 256)
            p = probs[pl.ds(start, ROWS), cols] * stats[0, pl.ds(slot, 1), cols]
            ds = (SCALE * p * (gprobs[pl.ds(start, ROWS), cols] - stats[1, 0:1, cols])).astype(BF16)
            dv = mm(p.astype(BF16), go_ref[:, h * 128 : h * 128 + 128])
            dk = mm(ds, qx[:, cols])
            dkv[pl.ds(start, ROWS), h * 128 : h * 128 + 128] = dk[:, :128].astype(BF16)
            dkv[pl.ds(start, ROWS), 512 + h * 128 : 640 + h * 128] = dv.astype(BF16)
            rope_sum = rope_sum + dk[:, 128:]
            key_t = jnp.concatenate(
                [kxt[slot, h * 128 : h * 128 + 128, :], kxt[slot, 512:, :]], axis=0
            )
            dqt[h] += mm(key_t, ds)
        part[:, LAT:] = rope_sum
        both = dkv[pl.ds(start, ROWS), :]
        for n in range(2):
            part[:, n * 256 : n * 256 + 256] = mm(both, ups[n * 256 : n * 256 + 256, :], NT)

        def add(which):
            part[...] += sib_in[which].astype(F32)

        def leave(index):
            ys_out[index] = part[...].astype(BF16)
            ys_own[index] = part[pl.ds(pl.multiple_of(y * 32, 32), 32), :]
            for by in (4, 3, 5, 2, 6, 1, 7):
                scatter_y(index, by).start()

        @pl.when(t == 0)
        def _():
            sib_out[0] = part[...].astype(BF16)
            up_low.start()

        @pl.when(t == 1)
        def _():
            @pl.when(core == 1)
            def _():
                up_low.wait_recv()
                add(0)

            leave(0)

        @pl.when(t == 2)
        def _():
            sib_out[1] = part[...].astype(BF16)
            up_high.start()

        @pl.when(t == 3)
        def _():
            @pl.when(core == 0)
            def _():
                up_low.wait_recv()
                add(0)

            @pl.when(core == 1)
            def _():
                up_high.wait_recv()
                add(1)

            leave(1)

        @pl.when(t == 4)
        def _():
            @pl.when(core == 0)
            def _():
                up_high.wait_recv()
                add(1)

            leave(2)

        return carry

    lax.fori_loop(0, SLOTS, grads, 0)

    theirs = pl.multiple_of((1 - core) * 256, 256)
    mine = pl.multiple_of(core * 256, 256)
    to_sib = remote(g_out, g_in, s_g.at[0], r_g.at[0], sib)
    for n in range(4):
        g_out[:, n * 256 : n * 256 + 256] = mm(
            latt[pl.ds(theirs, 256), :], dkv[:, n * 256 : n * 256 + 256]
        ).astype(BF16)
    to_sib.start()
    for n in range(4):
        g_own[:, n * 256 : n * 256 + 256] = mm(
            latt[pl.ds(mine, 256), :], dkv[:, n * 256 : n * 256 + 256]
        )
    to_sib.wait_recv()
    g_own[...] += g_in[...].astype(F32)
    gx_out[...] = g_own[...].astype(BF16)

    def scatter_x(by):
        there = pl.multiple_of(lax.rem(x + by, 4) * 64, 64)
        return remote(
            gx_out.at[pl.ds(there, 64), :], gx_in.at[by - 1], s_gx.at[by - 1], r_gx.at[by - 1], at_x(by)
        )

    for by in (2, 1, 3):
        scatter_x(by).start()

    def to_owner(index, other):
        slot = index * 2 + other
        part_of = lax.rem(zl + other, 2)
        return remote(
            own_out.at[index, pl.ds(pl.multiple_of(part_of * 16, 16), 16), :], own_in.at[slot],
            s_own.at[slot], r_own.at[slot], owner(-4 + 2 * index, other),
        )

    for index in range(3):
        here = ys_own[index]
        for by in range(1, 8):
            scatter_y(index, by).wait_recv()
        for by in range(1, 8):
            here = here + ys_in[index, by - 1].astype(F32)
        own_out[index] = here.astype(BF16)
        if index == 2:
            own_keep[...] = here
        for other in (0, 1):
            if index < 2 or other:
                to_owner(index, other).start()

    for h in range(HEADS_HERE):
        dq = dqt[h].T
        dq_ref[:, h * 192 : h * 192 + 192] = dq[:, :192].astype(BF16)

    for by in range(1, 4):
        scatter_x(by).wait_recv()
    g_sum = g_own[pl.ds(pl.multiple_of(x * 64, 64), 64), :]
    for by in range(1, 4):
        g_sum = g_sum + gx_in[by - 1].astype(F32)
    g_own[0:64, :] = g_sum
    gz_out[...] = g_sum.astype(BF16)

    def scatter_zh(by):
        there = pl.multiple_of(lax.rem(zh + by, 4) * 16, 16)
        return remote(
            gz_out.at[pl.ds(there, 16), :], gz_in.at[by - 1], s_gz.at[by - 1], r_gz.at[by - 1], at_zh(by)
        )

    for by in (2, 1, 3):
        scatter_zh(by).start()

    for index in range(3):
        for other in (0, 1):
            if index < 2 or other:
                to_owner(index, other).wait_recv()
    final = own_keep[pl.ds(pl.multiple_of(zl * 16, 16), 16), :]
    for slot in range(5):
        final = final + own_in[slot if slot < 4 else 5].astype(F32)
    my_rows = pl.ds(pl.multiple_of(dp * 16, 16), 16)
    gather[my_rows, :] = final.astype(BF16)

    def to_all(by):
        return remote(
            gather.at[my_rows, :], gather.at[my_rows, :], s_ag.at[by - 1], r_ag.at[by - 1], at_dp(by)
        )

    for by in (8, 7, 9, 6, 10, 5, 11, 4, 12, 3, 13, 2, 14, 1, 15):
        to_all(by).start()

    for by in range(1, 4):
        scatter_zh(by).wait_recv()
    g_last = g_own[pl.ds(pl.multiple_of(zh * 16, 16), 16), :]
    for by in range(1, 4):
        g_last = g_last + gz_in[by - 1].astype(F32)
    dupk_ref[...] = g_last[:, :512]
    dupv_ref[...] = g_last[:, 512:]

    for by in range(1, 16):
        to_all(by).wait_recv()
    dlat_ref[...] = gather[:, : LAT + ROPE].astype(F32)

    to_near.wait_send()
    to_far.wait_send()
    fw_own.wait_send()
    fw_mid_low.wait_send()
    for by in range(1, 8):
        along_y(2, 0, by).wait_send()
        along_y(0, 1, by).wait_send()
        for index in range(3):
            scatter_y(index, by).wait_send()
    up_low.wait_send()
    up_high.wait_send()
    to_sib.wait_send()
    for by in range(1, 4):
        scatter_x(by).wait_send()
        scatter_zh(by).wait_send()
    for index in range(3):
        for other in (0, 1):
            if index < 2 or other:
                to_owner(index, other).wait_send()
    for by in range(1, 16):
        to_all(by).wait_send()


def shards(queries, latent, grad_out, doc_ids, up_key, up_value):
    vmem = pl.BlockSpec(memory_space=pltpu.VMEM)
    dma = pltpu.SemaphoreType.DMA
    return tuple(pl.pallas_call(
        kernel,
        out_shape=(
            jax.ShapeDtypeStruct((ROWS, 768), BF16),
            jax.ShapeDtypeStruct((ROWS, LAT + ROPE), F32),
            jax.ShapeDtypeStruct((16, 512), F32),
            jax.ShapeDtypeStruct((16, 512), F32),
        ),
        in_specs=[vmem] * 6,
        out_specs=(vmem,) * 4,
        scratch_shapes=[
            pltpu.VMEM((SLOTS, ROWS, WIDE), BF16),
            pltpu.VMEM((ROWS, 1024), BF16),
            pltpu.VMEM((LAT, 1024), BF16),
            pltpu.VMEM((SLOTS * ROWS, 1024), BF16),
            pltpu.VMEM((SLOTS, WIDE, ROWS), BF16),
            pltpu.VMEM((LAT, SLOTS * ROWS), BF16),
            pltpu.VMEM((SLOTS * ROWS, 1024), F32),
            pltpu.VMEM((SLOTS * ROWS, 1024), F32),
            pltpu.VMEM((3, 8, 1024), F32),
            pltpu.VMEM((ROWS, ROWS), F32),
            pltpu.VMEM((HEADS_HERE, 256, ROWS), F32),
            pltpu.VMEM((SLOTS * ROWS, 1024), BF16),
            pltpu.VMEM((ROWS, WIDE), F32),
            pltpu.VMEM((2, ROWS, WIDE), BF16),
            pltpu.VMEM((2, ROWS, WIDE), BF16),
            pltpu.VMEM((3, ROWS, WIDE), BF16),
            pltpu.VMEM((3, 32, WIDE), F32),
            pltpu.VMEM((3, 7, 32, WIDE), BF16),
            pltpu.VMEM((3, 32, WIDE), BF16),
            pltpu.VMEM((6, 16, WIDE), BF16),
            pltpu.VMEM((32, WIDE), F32),
            pltpu.VMEM((ROWS, WIDE), BF16),
            pltpu.VMEM((256, 1024), BF16),
            pltpu.VMEM((256, 1024), BF16),
            pltpu.VMEM((256, 1024), F32),
            pltpu.VMEM((256, 1024), BF16),
            pltpu.VMEM((3, 64, 1024), BF16),
            pltpu.VMEM((64, 1024), BF16),
            pltpu.VMEM((3, 16, 1024), BF16),
            dma((2,)), dma((2,)),
            dma((2, 7)), dma((2, 7)),
            dma((2,)), dma((2,)),
            dma((2,)), dma((2,)),
            dma((3, 7)), dma((3, 7)),
            dma((6,)), dma((6,)),
            dma((15,)), dma((15,)),
            dma((1,)), dma((1,)),
            dma((3,)), dma((3,)),
            dma((3,)), dma((3,)),
        ],
        compiler_params=pltpu.CompilerParams(
            collective_id=0, has_side_effects=True, vmem_limit_bytes=56 * 1024 * 1024
        ),
        name="mla_backward",
    )(queries, latent, grad_out, doc_ids.reshape(1, ROWS), up_key, up_value))


def solution(mesh):
    return jax.shard_map(
        shards,
        mesh=mesh,
        in_specs=(P("ctx", "dp"), P("ctx", None), P("ctx", "dp"), P("ctx"), P(None, "dp"), P(None, "dp")),
        out_specs=(P("ctx", "dp"), P("ctx", None), P("ctx", "dp"), P("ctx", "dp")),
        check_vma=False,
    )
```

```python
import functools
import jax
import jax.numpy as jnp
from jax import lax
from jax.experimental import pallas as pl
from jax.experimental.pallas import tpu as pltpu
from jax.sharding import PartitionSpec as P

LAT = 512
ROPE = 64
NOPE = 128
ROWS = 256
HEADS_HERE = 4
WIDE = 640
SLOTS = 5
SCALE = (NOPE + ROPE) ** -0.5
LOG2E = 1.4426950408889634
LOW = -1e30
MESH = pl.DeviceIdType.MESH
F32 = jnp.float32
BF16 = jnp.bfloat16
NT = (((1,), (1,)), ((), ()))
NN = (((1,), (0,)), ((), ()))


def mm(a, b, dims=NN):
    return lax.dot_general(a, b, dims, preferred_element_type=F32)


def kernel(
    q_any, lat_any, go_any, doc_any, upk_any, upv_any,
    dq_ref, dlat_ref, dup_ref,
    q_ref, lat_ref, go_ref, doc_ref, win, qx, ups, kv, kxt, latt, probs, gprobs, stats, bias, dqt, dkv,
    part, sib_out, sib_in, ys_out, ys_own, ys_in, own_out, own_in, own_keep,
    g_out, g_in, g_own, gx_out, gx_in, gz_out, gz_in,
    s_in, s_z, r_z, s_y, r_y, s_fw, r_fw, s_sib, r_sib, s_ys, r_ys,
    s_own, r_own, s_ag, r_ag, s_g, r_g, s_gx, r_gx, s_gz, r_gz,
):
    dp = lax.axis_index("dp")
    ctx = lax.axis_index("ctx")
    y, zl = lax.div(dp, 2), lax.rem(dp, 2)
    x, zh, core = lax.div(ctx, 8), lax.rem(lax.div(ctx, 2), 4), lax.rem(ctx, 2)
    sib = (dp, ctx + 1 - 2 * core)

    def at_ctx(by):
        return lax.rem(ctx + by + 32, 32)

    def at_y(by):
        return (lax.rem(y + by + 8, 8) * 2 + zl, ctx)

    def at_dp(by):
        return (lax.rem(dp + by + 16, 16), ctx)

    def at_x(by):
        return (dp, lax.rem(x + by + 4, 4) * 8 + zh * 2 + core)

    def at_zh(by):
        return (dp, x * 8 + lax.rem(zh + by + 4, 4) * 2 + core)

    def owner(by, other):
        mate = dp + 1 - 2 * zl if other else dp
        return (mate, at_ctx(by))

    barrier = pltpu.get_barrier_semaphore()
    senders = [sib, (dp, at_ctx(-2)), (dp, at_ctx(-4))]
    senders += [owner(by, other) for by in (0, 2, 4) for other in (0, 1) if by or other]
    senders += [at_dp(-i) for i in range(1, 16)]
    senders += [at_x(-i) for i in range(1, 4)]
    senders += [at_zh(-i) for i in range(1, 4)]
    for sender in senders:
        pl.semaphore_signal(barrier, inc=1, device_id=sender, device_id_type=MESH)

    loads = [
        pltpu.make_async_copy(src, dst, s_in.at[i])
        for i, (src, dst) in enumerate((
            (lat_any, lat_ref), (doc_any, doc_ref), (upk_any, ups.at[:, :512]),
            (upv_any, ups.at[:, 512:]), (q_any, q_ref), (go_any, go_ref),
        ))
    ]
    for load in loads:
        load.start()

    def remote(src, dst, send, recv, to):
        return pltpu.make_async_remote_copy(
            src_ref=src, dst_ref=dst, send_sem=send, recv_sem=recv,
            device_id=to, device_id_type=MESH,
        )

    loads[0].wait()
    loads[1].wait()
    doc_row = doc_ref[...].astype(F32)
    line = lax.broadcasted_iota(jnp.int32, (ROWS, ROWS), 0)
    lane = lax.broadcasted_iota(jnp.int32, (ROWS, ROWS), 1)
    doc_col = jnp.sum(jnp.where(line == lane, doc_row, 0.0), axis=1, keepdims=True)
    win[4, :, :LAT] = lat_ref[:LAT, :].T
    tail = jnp.concatenate([lat_ref[LAT:, :].astype(F32), jnp.zeros((64, ROWS), F32)], axis=0).T
    tail_lane = lax.broadcasted_iota(jnp.int32, (ROWS, 128), 1)
    win[4, :, LAT:] = jnp.where(tail_lane == 64, doc_col, tail).astype(BF16)

    pl.semaphore_wait(barrier, len(senders))

    def shares(slot, who):
        return win.at[slot, pl.ds(pl.multiple_of(who * 32, 32), 32), :]

    def along_z(index, half):
        who = lax.rem(y + 4 * half, 8)
        return remote(
            shares(4, who), shares(2 - 2 * index, who), s_z.at[index, half], r_z.at[index, half],
            (dp, at_ctx(2 + 2 * index)),
        )

    for index in (0, 1):
        for half in (0, 1):
            along_z(index, half).start()

    fw_own = remote(win.at[4], win.at[3], s_fw.at[0], r_fw.at[0], sib)
    fw_mid = remote(win.at[2], win.at[3], s_fw.at[0], r_fw.at[0], sib)
    fw_mid_low = remote(win.at[2], win.at[1], s_fw.at[1], r_fw.at[1], sib)
    fw_far_low = remote(win.at[0], win.at[1], s_fw.at[1], r_fw.at[1], sib)

    @pl.when(core == 0)
    def _():
        fw_own.start()

    passes = ((2, 0), (-2, 0), (1, 0), (-1, 0), (1, 4), (-1, 4))

    def along_y(index, j):
        by, more = passes[j]
        rows = shares(2 - 2 * index, lax.rem(y + more, 8))
        return remote(rows, rows, s_y.at[index, j], r_y.at[index, j], at_y(by))

    for load in loads[2:]:
        load.wait()

    for h in range(HEADS_HERE):
        qx[:, h * 256 : h * 256 + 128] = q_ref[:, h * 192 : h * 192 + 128]
        qx[:, h * 256 + 128 : h * 256 + 256] = jnp.concatenate(
            [q_ref[:, h * 192 + 128 : h * 192 + 192], jnp.zeros((ROWS, 64), BF16)], axis=1
        )
    dqt[...] = jnp.zeros_like(dqt)

    for index in (0, 1):
        for half in (0, 1):
            along_z(index, half).wait_recv()
        for j in range(6):
            along_y(index, j).start()

    def scores(t, carry):
        slot = lax.rem(4 + 3 * t, 5)

        @pl.when(t == 1)
        def _():
            for j in range(6):
                along_y(0, j).wait_recv()

            @pl.when(core == 0)
            def _():
                fw_mid_low.start()

            @pl.when(core == 1)
            def _():
                fw_mid.start()

        @pl.when(t == 2)
        def _():
            for j in range(6):
                along_y(1, j).wait_recv()

            @pl.when(core == 1)
            def _():
                fw_far_low.start()

        @pl.when(t == 3)
        def _():
            fw_own.wait_recv()

        @pl.when(t == 4)
        def _():
            fw_mid_low.wait_recv()

        start = pl.multiple_of(slot * ROWS, ROWS)
        block = win[slot]
        latent = block[:, :LAT]
        rope = block[:, LAT:]
        for n in range(4):
            kv[pl.ds(start, ROWS), n * 256 : n * 256 + 256] = mm(
                latent, ups[:, n * 256 : n * 256 + 256]
            ).astype(BF16)
        keys = kv[pl.ds(start, ROWS), :512]
        kxt[slot, :512, :] = keys.T
        kxt[slot, 512:, :] = rope.T
        flipped = latent.T
        for g in range(32):
            row = (g % 2) * 256 + (g // 2) * 16
            latt[row : row + 16, pl.ds(start, ROWS)] = flipped[g * 16 : g * 16 + 16, :]
        docs = rope[:, 64:65].astype(F32)
        past = jnp.logical_or(slot < 4, line <= lane)
        bias[...] = jnp.where(jnp.logical_and(docs == doc_row, past), 0.0, LOW)
        for h in range(HEADS_HERE):
            cols = slice(h * 256, h * 256 + 256)
            key = kv[pl.ds(start, ROWS), h * 128 : h * 128 + 128]
            value = kv[pl.ds(start, ROWS), 512 + h * 128 : 640 + h * 128]
            s = mm(jnp.concatenate([key, rope], axis=1), qx[:, cols], NT) + bias[...]
            top = jnp.max(s, axis=0, keepdims=True)
            p = jnp.exp2((s - top) * (SCALE * LOG2E))
            gp = mm(value, go_ref[:, h * 128 : h * 128 + 128], NT)
            probs[pl.ds(start, ROWS), cols] = p
            gprobs[pl.ds(start, ROWS), cols] = gp
            stats[0, pl.ds(slot, 1), cols] = top
            stats[1, pl.ds(slot, 1), cols] = jnp.sum(p, axis=0, keepdims=True)
            stats[2, pl.ds(slot, 1), cols] = jnp.sum(p * gp, axis=0, keepdims=True)
        return carry

    lax.fori_loop(0, SLOTS, scores, 0)

    tops = stats[0, 0:SLOTS, :]
    factor = jnp.exp2((tops - jnp.max(tops, axis=0, keepdims=True)) * (SCALE * LOG2E))
    total = jnp.sum(stats[1, 0:SLOTS, :] * factor, axis=0, keepdims=True)
    delta = jnp.sum(stats[2, 0:SLOTS, :] * factor, axis=0, keepdims=True) / total
    stats[0, 0:SLOTS, :] = factor / total
    stats[1, 0:1, :] = delta

    up_low = remote(sib_out.at[0], sib_in.at[0], s_sib.at[0], r_sib.at[0], sib)
    up_high = remote(sib_out.at[1], sib_in.at[1], s_sib.at[1], r_sib.at[1], sib)

    def share_of(by):
        return pl.multiple_of(lax.rem(y + by + 8, 8) * 32, 32)

    def hop(index, step, way):
        lane_of = 0 if way > 0 else 1
        rows = pl.ds(share_of(way * (5 - step)), 32)
        into = pl.ds(0, 32)
        if step == 1:
            rows = pl.ds(pl.multiple_of(share_of(4) + 16 * lane_of, 16), 16)
            into = pl.ds(0, 16)
        return remote(
            ys_out.at[index, rows, :], ys_in.at[index, lane_of, step - 1, into, :],
            s_ys.at[index, lane_of, step - 1], r_ys.at[index, lane_of, step - 1], at_y(way),
        )

    def relay(index, step):
        for way in (1, -1):
            lane_of = 0 if way > 0 else 1
            hop(index, step - 1, way).wait_recv()
            first, count = share_of(way * (5 - step)), 32
            if step == 2:
                first, count = pl.multiple_of(first + 16 * lane_of, 16), 16
            rows = pl.ds(first, count)
            came = ys_in[index, lane_of, step - 2, 0:count, :].astype(F32)
            ys_out[index, rows, :] = (ys_out[index, rows, :].astype(F32) + came).astype(BF16)
            hop(index, step, way).start()

    def grads(t, carry):
        slot = jnp.minimum(t + 1 - 2 * lax.rem(t, 2), 4)
        start = pl.multiple_of(slot * ROWS, ROWS)
        rope_sum = jnp.zeros((ROWS, 128), F32)
        for h in range(HEADS_HERE):
            cols = slice(h * 256, h * 256 + 256)
            p = probs[pl.ds(start, ROWS), cols] * stats[0, pl.ds(slot, 1), cols]
            ds = (SCALE * p * (gprobs[pl.ds(start, ROWS), cols] - stats[1, 0:1, cols])).astype(BF16)
            dv = mm(p.astype(BF16), go_ref[:, h * 128 : h * 128 + 128])
            dk = mm(ds, qx[:, cols])
            dkv[pl.ds(start, ROWS), h * 128 : h * 128 + 128] = dk[:, :128].astype(BF16)
            dkv[pl.ds(start, ROWS), 512 + h * 128 : 640 + h * 128] = dv.astype(BF16)
            rope_sum = rope_sum + dk[:, 128:]
            key_t = jnp.concatenate(
                [kxt[slot, h * 128 : h * 128 + 128, :], kxt[slot, 512:, :]], axis=0
            )
            dqt[h] += mm(key_t, ds)
        part[:, LAT:] = rope_sum
        both = dkv[pl.ds(start, ROWS), :]
        for n in range(2):
            part[:, n * 256 : n * 256 + 256] = mm(both, ups[n * 256 : n * 256 + 256, :], NT)

        def add(which):
            part[...] += sib_in[which].astype(F32)

        def leave(index):
            ys_out[index] = part[...].astype(BF16)
            ys_own[index] = part[pl.ds(pl.multiple_of(y * 32, 32), 32), :]
            hop(index, 1, 1).start()
            hop(index, 1, -1).start()

        @pl.when(t == 0)
        def _():
            sib_out[0] = part[...].astype(BF16)
            up_low.start()

        @pl.when(t == 1)
        def _():
            @pl.when(core == 1)
            def _():
                up_low.wait_recv()
                add(0)

            leave(0)

        @pl.when(t == 2)
        def _():
            sib_out[1] = part[...].astype(BF16)
            up_high.start()

        @pl.when(t == 3)
        def _():
            @pl.when(core == 0)
            def _():
                up_low.wait_recv()
                add(0)

            @pl.when(core == 1)
            def _():
                up_high.wait_recv()
                add(1)

            relay(0, 2)
            leave(1)

        @pl.when(t == 4)
        def _():
            @pl.when(core == 0)
            def _():
                up_high.wait_recv()
                add(1)

            leave(2)

        return carry

    lax.fori_loop(0, SLOTS, grads, 0)

    theirs = pl.multiple_of((1 - core) * 256, 256)
    mine = pl.multiple_of(core * 256, 256)
    to_sib = remote(g_out, g_in, s_g.at[0], r_g.at[0], sib)
    for n in range(4):
        g_out[:, n * 256 : n * 256 + 256] = mm(
            latt[pl.ds(theirs, 256), :], dkv[:, n * 256 : n * 256 + 256]
        ).astype(BF16)
    to_sib.start()
    relay(0, 3)
    relay(1, 2)
    for n in range(4):
        g_own[:, n * 256 : n * 256 + 256] = mm(
            latt[pl.ds(mine, 256), :], dkv[:, n * 256 : n * 256 + 256]
        )
    relay(2, 2)
    relay(0, 4)
    relay(1, 3)
    to_sib.wait_recv()
    g_own[...] += g_in[...].astype(F32)
    gx_out[...] = g_own[...].astype(BF16)

    def scatter_x(by):
        there = pl.multiple_of(lax.rem(x + by, 4) * 64, 64)
        return remote(
            gx_out.at[pl.ds(there, 64), :], gx_in.at[by - 1], s_gx.at[by - 1], r_gx.at[by - 1], at_x(by)
        )

    for by in (2, 1, 3):
        scatter_x(by).start()

    def to_owner(index, other):
        slot = index * 2 + other
        part_of = lax.rem(zl + other, 2)
        return remote(
            own_out.at[index, pl.ds(pl.multiple_of(part_of * 16, 16), 16), :], own_in.at[slot],
            s_own.at[slot], r_own.at[slot], owner(-4 + 2 * index, other),
        )

    def settle(index):
        here = ys_own[index]
        for way in (1, -1):
            hop(index, 4, way).wait_recv()
            here = here + ys_in[index, 0 if way > 0 else 1, 3].astype(F32)
        own_out[index] = here.astype(BF16)
        if index == 2:
            own_keep[...] = here
        for other in (0, 1):
            if index < 2 or other:
                to_owner(index, other).start()

    relay(2, 3)
    settle(0)
    relay(1, 4)

    for h in range(HEADS_HERE):
        dq = dqt[h].T
        dq_ref[:, h * 192 : h * 192 + 192] = dq[:, :192].astype(BF16)

    relay(2, 4)
    settle(1)
    settle(2)

    for by in range(1, 4):
        scatter_x(by).wait_recv()
    g_sum = g_own[pl.ds(pl.multiple_of(x * 64, 64), 64), :]
    for by in range(1, 4):
        g_sum = g_sum + gx_in[by - 1].astype(F32)
    g_own[0:64, :] = g_sum
    gz_out[...] = g_sum.astype(BF16)

    def scatter_zh(by):
        there = pl.multiple_of(lax.rem(zh + by, 4) * 16, 16)
        return remote(
            gz_out.at[pl.ds(there, 16), :], gz_in.at[by - 1], s_gz.at[by - 1], r_gz.at[by - 1], at_zh(by)
        )

    for by in (2, 1, 3):
        scatter_zh(by).start()

    for index in range(3):
        for other in (0, 1):
            if index < 2 or other:
                to_owner(index, other).wait_recv()
    final = own_keep[pl.ds(pl.multiple_of(zl * 16, 16), 16), :]
    for slot in range(5):
        final = final + own_in[slot if slot < 4 else 5].astype(F32)
    my_rows = pl.ds(pl.multiple_of(dp * 16, 16), 16)
    dlat_ref[my_rows, :] = final.astype(BF16)

    def to_all(by):
        return remote(
            dlat_ref.at[my_rows, :], dlat_ref.at[my_rows, :], s_ag.at[by - 1], r_ag.at[by - 1], at_dp(by)
        )

    for by in (8, 7, 9, 6, 10, 5, 11, 4, 12, 3, 13, 2, 14, 1, 15):
        to_all(by).start()

    for by in range(1, 4):
        scatter_zh(by).wait_recv()
    g_last = g_own[pl.ds(pl.multiple_of(zh * 16, 16), 16), :]
    for by in range(1, 4):
        g_last = g_last + gz_in[by - 1].astype(F32)
    dup_ref[...] = g_last

    for by in range(1, 16):
        to_all(by).wait_recv()

    for index in (0, 1):
        for half in (0, 1):
            along_z(index, half).wait_send()
        for j in range(6):
            along_y(index, j).wait_send()
    fw_own.wait_send()
    fw_mid_low.wait_send()
    for index in range(3):
        for step in range(1, 5):
            for way in (1, -1):
                hop(index, step, way).wait_send()
    up_low.wait_send()
    up_high.wait_send()
    to_sib.wait_send()
    for by in range(1, 4):
        scatter_x(by).wait_send()
        scatter_zh(by).wait_send()
    for index in range(3):
        for other in (0, 1):
            if index < 2 or other:
                to_owner(index, other).wait_send()
    for by in range(1, 16):
        to_all(by).wait_send()


def write_out(dq_in, dlat_in, dup_in, dq_ref, dlat_ref, dupk_ref, dupv_ref):
    dq_ref[...] = dq_in[...]
    dlat_ref[...] = dlat_in[...].astype(F32).T[: LAT + ROPE, :]
    dupk_ref[...] = dup_in[:, :512]
    dupv_ref[...] = dup_in[:, 512:]


def shards(queries, latent, grad_out, doc_ids, up_key, up_value):
    vmem = pl.BlockSpec(memory_space=pltpu.VMEM)
    dma = pltpu.SemaphoreType.DMA
    shape = jax.ShapeDtypeStruct
    made = pl.pallas_call(
        kernel,
        out_shape=(shape((ROWS, 768), BF16), shape((ROWS, WIDE), BF16), shape((16, 1024), F32)),
        in_specs=[pl.BlockSpec(memory_space=pl.ANY)] * 6,
        out_specs=(vmem,) * 3,
        scratch_shapes=[
            pltpu.VMEM((ROWS, 768), BF16),
            pltpu.VMEM((LAT + ROPE, ROWS), BF16),
            pltpu.VMEM((ROWS, 512), BF16),
            pltpu.VMEM((1, ROWS), jnp.int32),
            pltpu.VMEM((SLOTS, ROWS, WIDE), BF16),
            pltpu.VMEM((ROWS, 1024), BF16),
            pltpu.VMEM((LAT, 1024), BF16),
            pltpu.VMEM((SLOTS * ROWS, 1024), BF16),
            pltpu.VMEM((SLOTS, WIDE, ROWS), BF16),
            pltpu.VMEM((LAT, SLOTS * ROWS), BF16),
            pltpu.VMEM((SLOTS * ROWS, 1024), F32),
            pltpu.VMEM((SLOTS * ROWS, 1024), F32),
            pltpu.VMEM((3, 8, 1024), F32),
            pltpu.VMEM((ROWS, ROWS), F32),
            pltpu.VMEM((HEADS_HERE, 256, ROWS), F32),
            pltpu.VMEM((SLOTS * ROWS, 1024), BF16),
            pltpu.VMEM((ROWS, WIDE), F32),
            pltpu.VMEM((2, ROWS, WIDE), BF16),
            pltpu.VMEM((2, ROWS, WIDE), BF16),
            pltpu.VMEM((3, ROWS, WIDE), BF16),
            pltpu.VMEM((3, 32, WIDE), F32),
            pltpu.VMEM((3, 2, 4, 32, WIDE), BF16),
            pltpu.VMEM((3, 32, WIDE), BF16),
            pltpu.VMEM((6, 16, WIDE), BF16),
            pltpu.VMEM((32, WIDE), F32),
            pltpu.VMEM((256, 1024), BF16),
            pltpu.VMEM((256, 1024), BF16),
            pltpu.VMEM((256, 1024), F32),
            pltpu.VMEM((256, 1024), BF16),
            pltpu.VMEM((3, 64, 1024), BF16),
            pltpu.VMEM((64, 1024), BF16),
            pltpu.VMEM((3, 16, 1024), BF16),
            dma((6,)),
            dma((2, 2)), dma((2, 2)),
            dma((2, 6)), dma((2, 6)),
            dma((2,)), dma((2,)),
            dma((2,)), dma((2,)),
            dma((3, 2, 4)), dma((3, 2, 4)),
            dma((6,)), dma((6,)),
            dma((15,)), dma((15,)),
            dma((1,)), dma((1,)),
            dma((3,)), dma((3,)),
            dma((3,)), dma((3,)),
        ],
        compiler_params=pltpu.CompilerParams(
            collective_id=0, has_side_effects=True, vmem_limit_bytes=56 * 1024 * 1024
        ),
        name="mla_backward",
    )(queries, latent.T, grad_out, doc_ids.reshape(1, ROWS), up_key, up_value)
    grad_queries, grad_latent, grad_up_key, grad_up_value = pl.pallas_call(
        write_out,
        out_shape=(
            shape((ROWS, 768), BF16), shape((LAT + ROPE, ROWS), F32),
            shape((16, 512), F32), shape((16, 512), F32),
        ),
        in_specs=[vmem] * 3,
        out_specs=(vmem,) * 4,
        compiler_params=pltpu.CompilerParams(vmem_limit_bytes=16 * 1024 * 1024),
        name="write_out",
    )(*made)
    return grad_queries, grad_latent.T, grad_up_key, grad_up_value


def solution(mesh):
    return jax.shard_map(
        shards,
        mesh=mesh,
        in_specs=(P("ctx", "dp"), P("ctx", None), P("ctx", "dp"), P("ctx"), P(None, "dp"), P(None, "dp")),
        out_specs=(P("ctx", "dp"), P("ctx", None), P("ctx", "dp"), P("ctx", "dp")),
        check_vma=False,
    )
```

```python
import functools
import jax
import jax.numpy as jnp
from jax import lax
from jax.experimental import pallas as pl
from jax.experimental.pallas import tpu as pltpu
from jax.sharding import PartitionSpec as P

LAT = 512
ROPE = 64
NOPE = 128
ROWS = 256
HEADS_HERE = 4
WIDE = 640
SLOTS = 5
SCALE = (NOPE + ROPE) ** -0.5
LOG2E = 1.4426950408889634
LOW = -1e30
MESH = pl.DeviceIdType.MESH
F32 = jnp.float32
BF16 = jnp.bfloat16
NT = (((1,), (1,)), ((), ()))
NN = (((1,), (0,)), ((), ()))


def mm(a, b, dims=NN):
    return lax.dot_general(a, b, dims, preferred_element_type=F32)


def kernel(
    q_any, lat_any, go_any, doc_any, upk_any, upv_any,
    dq_any, dlat_any, dup_any,
    dq_ref, dlat_ref, dup_ref, q_ref, lat_ref, go_ref, doc_ref, win, qx, ups, kv, kxt, latt, probs, gprobs, stats, bias, dqt, dkv,
    part, sib_out, sib_in, ys_out, ys_own, ys_in, own_out, own_in, own_keep,
    g_out, g_in, g_own, gx_out, gx_in, gz_out, gz_in,
    s_in, s_out, s_z, r_z, s_y, r_y, s_fw, r_fw, s_sib, r_sib, s_ys, r_ys,
    s_own, r_own, s_ag, r_ag, s_g, r_g, s_gx, r_gx, s_gz, r_gz,
):
    dp = lax.axis_index("dp")
    ctx = lax.axis_index("ctx")
    y, zl = lax.div(dp, 2), lax.rem(dp, 2)
    x, zh, core = lax.div(ctx, 8), lax.rem(lax.div(ctx, 2), 4), lax.rem(ctx, 2)
    sib = (dp, ctx + 1 - 2 * core)

    def at_ctx(by):
        return lax.rem(ctx + by + 32, 32)

    def at_y(by):
        return (lax.rem(y + by + 8, 8) * 2 + zl, ctx)

    def at_dp(by):
        return (lax.rem(dp + by + 16, 16), ctx)

    def at_x(by):
        return (dp, lax.rem(x + by + 4, 4) * 8 + zh * 2 + core)

    def at_zh(by):
        return (dp, x * 8 + lax.rem(zh + by + 4, 4) * 2 + core)

    def owner(by, other):
        mate = dp + 1 - 2 * zl if other else dp
        return (mate, at_ctx(by))

    barrier = pltpu.get_barrier_semaphore()
    senders = [sib, (dp, at_ctx(-2)), (dp, at_ctx(-4))]
    senders += [owner(by, other) for by in (0, 2, 4) for other in (0, 1) if by or other]
    senders += [at_dp(-i) for i in range(1, 16)]
    senders += [at_x(-i) for i in range(1, 4)]
    senders += [at_zh(-i) for i in range(1, 4)]
    for sender in senders:
        pl.semaphore_signal(barrier, inc=1, device_id=sender, device_id_type=MESH)

    loads = [
        pltpu.make_async_copy(src, dst, s_in.at[i])
        for i, (src, dst) in enumerate((
            (lat_any, lat_ref), (doc_any, doc_ref), (upk_any, ups.at[:, :512]),
            (upv_any, ups.at[:, 512:]), (q_any, q_ref), (go_any, go_ref),
        ))
    ]
    for load in loads:
        load.start()

    def remote(src, dst, send, recv, to):
        return pltpu.make_async_remote_copy(
            src_ref=src, dst_ref=dst, send_sem=send, recv_sem=recv,
            device_id=to, device_id_type=MESH,
        )

    loads[0].wait()
    loads[1].wait()
    doc_row = doc_ref[...].astype(F32)
    line = lax.broadcasted_iota(jnp.int32, (ROWS, ROWS), 0)
    lane = lax.broadcasted_iota(jnp.int32, (ROWS, ROWS), 1)
    doc_col = jnp.sum(jnp.where(line == lane, doc_row, 0.0), axis=1, keepdims=True)
    win[4, :, :LAT] = lat_ref[:LAT, :].T
    tail = jnp.concatenate([lat_ref[LAT:, :].astype(F32), jnp.zeros((64, ROWS), F32)], axis=0).T
    tail_lane = lax.broadcasted_iota(jnp.int32, (ROWS, 128), 1)
    win[4, :, LAT:] = jnp.where(tail_lane == 64, doc_col, tail).astype(BF16)

    pl.semaphore_wait(barrier, len(senders))

    def shares(slot, who):
        return win.at[slot, pl.ds(pl.multiple_of(who * 32, 32), 32), :]

    def along_z(index, half):
        who = lax.rem(y + 4 * half, 8)
        return remote(
            shares(4, who), shares(2 - 2 * index, who), s_z.at[index, half], r_z.at[index, half],
            (dp, at_ctx(2 + 2 * index)),
        )

    for index in (0, 1):
        for half in (0, 1):
            along_z(index, half).start()

    fw_own = remote(win.at[4], win.at[3], s_fw.at[0], r_fw.at[0], sib)
    fw_mid = remote(win.at[2], win.at[3], s_fw.at[0], r_fw.at[0], sib)
    fw_mid_low = remote(win.at[2], win.at[1], s_fw.at[1], r_fw.at[1], sib)
    fw_far_low = remote(win.at[0], win.at[1], s_fw.at[1], r_fw.at[1], sib)

    @pl.when(core == 0)
    def _():
        fw_own.start()

    passes = ((2, 0), (-2, 0), (1, 0), (-1, 0), (1, 4), (-1, 4))

    def along_y(index, j):
        by, more = passes[j]
        rows = shares(2 - 2 * index, lax.rem(y + more, 8))
        return remote(rows, rows, s_y.at[index, j], r_y.at[index, j], at_y(by))

    for load in loads[2:]:
        load.wait()

    for h in range(HEADS_HERE):
        qx[:, h * 256 : h * 256 + 128] = q_ref[:, h * 192 : h * 192 + 128]
        qx[:, h * 256 + 128 : h * 256 + 256] = jnp.concatenate(
            [q_ref[:, h * 192 + 128 : h * 192 + 192], jnp.zeros((ROWS, 64), BF16)], axis=1
        )
    dqt[...] = jnp.zeros_like(dqt)

    for index in (0, 1):
        for half in (0, 1):
            along_z(index, half).wait_recv()
        for j in range(6):
            along_y(index, j).start()

    def scores(t, carry):
        slot = lax.rem(4 + 3 * t, 5)

        @pl.when(t == 1)
        def _():
            for j in range(6):
                along_y(0, j).wait_recv()

            @pl.when(core == 0)
            def _():
                fw_mid_low.start()

            @pl.when(core == 1)
            def _():
                fw_mid.start()

        @pl.when(t == 2)
        def _():
            for j in range(6):
                along_y(1, j).wait_recv()

            @pl.when(core == 1)
            def _():
                fw_far_low.start()

        @pl.when(t == 3)
        def _():
            fw_own.wait_recv()

        @pl.when(t == 4)
        def _():
            fw_mid_low.wait_recv()

        start = pl.multiple_of(slot * ROWS, ROWS)
        block = win[slot]
        latent = block[:, :LAT]
        rope = block[:, LAT:]
        for n in range(4):
            kv[pl.ds(start, ROWS), n * 256 : n * 256 + 256] = mm(
                latent, ups[:, n * 256 : n * 256 + 256]
            ).astype(BF16)
        keys = kv[pl.ds(start, ROWS), :512]
        kxt[slot, :512, :] = keys.T
        kxt[slot, 512:, :] = rope.T
        flipped = latent.T
        for g in range(32):
            row = (g % 2) * 256 + (g // 2) * 16
            latt[row : row + 16, pl.ds(start, ROWS)] = flipped[g * 16 : g * 16 + 16, :]
        docs = rope[:, 64:65].astype(F32)
        past = jnp.logical_or(slot < 4, line <= lane)
        bias[...] = jnp.where(jnp.logical_and(docs == doc_row, past), 0.0, LOW)
        for h in range(HEADS_HERE):
            cols = slice(h * 256, h * 256 + 256)
            key = kv[pl.ds(start, ROWS), h * 128 : h * 128 + 128]
            value = kv[pl.ds(start, ROWS), 512 + h * 128 : 640 + h * 128]
            s = mm(jnp.concatenate([key, rope], axis=1), qx[:, cols], NT) + bias[...]
            top = jnp.max(s, axis=0, keepdims=True)
            p = jnp.exp2((s - top) * (SCALE * LOG2E))
            gp = mm(value, go_ref[:, h * 128 : h * 128 + 128], NT)
            probs[pl.ds(start, ROWS), cols] = p
            gprobs[pl.ds(start, ROWS), cols] = gp
            stats[0, pl.ds(slot, 1), cols] = top
            stats[1, pl.ds(slot, 1), cols] = jnp.sum(p, axis=0, keepdims=True)
            stats[2, pl.ds(slot, 1), cols] = jnp.sum(p * gp, axis=0, keepdims=True)
        return carry

    lax.fori_loop(0, SLOTS, scores, 0)

    tops = stats[0, 0:SLOTS, :]
    factor = jnp.exp2((tops - jnp.max(tops, axis=0, keepdims=True)) * (SCALE * LOG2E))
    total = jnp.sum(stats[1, 0:SLOTS, :] * factor, axis=0, keepdims=True)
    delta = jnp.sum(stats[2, 0:SLOTS, :] * factor, axis=0, keepdims=True) / total
    stats[0, 0:SLOTS, :] = factor / total
    stats[1, 0:1, :] = delta

    up_low = remote(sib_out.at[0], sib_in.at[0], s_sib.at[0], r_sib.at[0], sib)
    up_high = remote(sib_out.at[1], sib_in.at[1], s_sib.at[1], r_sib.at[1], sib)

    def share_of(by):
        return pl.multiple_of(lax.rem(y + by + 8, 8) * 32, 32)

    def hop(index, kind, way):
        side = 0 if way > 0 else 1
        by, dest = ((1, 1), (1, 3), (2, 4), (2, 2))[kind]
        rows, into = pl.ds(share_of(way * dest), 32), pl.ds(0, 32)
        if kind == 2:
            rows = pl.ds(pl.multiple_of(share_of(4) + 16 * side, 16), 16)
            into = pl.ds(0, 16)
        return remote(
            ys_out.at[index, rows, :], ys_in.at[index, side, kind, into, :],
            s_ys.at[index, side, kind], r_ys.at[index, side, kind], at_y(way * by),
        )

    def relay(index):
        for way in (1, -1):
            side = 0 if way > 0 else 1
            hop(index, 1, way).wait_recv()
            hop(index, 2, way).wait_recv()
            rows = pl.ds(share_of(2 * way), 32)
            more = ys_in[index, side, 1].astype(F32)
            half = ys_in[index, side, 2, 0:16, :].astype(F32)
            empty = jnp.zeros_like(half)
            more = more + jnp.concatenate([empty, half] if side else [half, empty], axis=0)
            ys_out[index, rows, :] = (ys_out[index, rows, :].astype(F32) + more).astype(BF16)
            hop(index, 3, way).start()

    def grads(t, carry):
        slot = jnp.where(
            t == 0, 4 * core, jnp.where(t < 3, 2 * t - 1, jnp.where(t == 3, 2 - 2 * core, 4 - 2 * core))
        )
        start = pl.multiple_of(slot * ROWS, ROWS)
        rope_sum = jnp.zeros((ROWS, 128), F32)
        for h in range(HEADS_HERE):
            cols = slice(h * 256, h * 256 + 256)
            p = probs[pl.ds(start, ROWS), cols] * stats[0, pl.ds(slot, 1), cols]
            ds = (SCALE * p * (gprobs[pl.ds(start, ROWS), cols] - stats[1, 0:1, cols])).astype(BF16)
            dv = mm(p.astype(BF16), go_ref[:, h * 128 : h * 128 + 128])
            dk = mm(ds, qx[:, cols])
            dkv[pl.ds(start, ROWS), h * 128 : h * 128 + 128] = dk[:, :128].astype(BF16)
            dkv[pl.ds(start, ROWS), 512 + h * 128 : 640 + h * 128] = dv.astype(BF16)
            rope_sum = rope_sum + dk[:, 128:]
            key_t = jnp.concatenate(
                [kxt[slot, h * 128 : h * 128 + 128, :], kxt[slot, 512:, :]], axis=0
            )
            dqt[h] += mm(key_t, ds)
        part[:, LAT:] = rope_sum
        both = dkv[pl.ds(start, ROWS), :]
        for n in range(2):
            part[:, n * 256 : n * 256 + 256] = mm(both, ups[n * 256 : n * 256 + 256, :], NT)

        def add(which):
            part[...] += sib_in[which].astype(F32)

        def leave(index):
            ys_out[index] = part[...].astype(BF16)
            ys_own[index] = part[pl.ds(pl.multiple_of(y * 32, 32), 32), :]
            for kind in (2, 1, 0):
                for way in (1, -1):
                    hop(index, kind, way).start()

        @pl.when(t == 0)
        def _():
            leave(0)

        @pl.when(t == 1)
        def _():
            sib_out[0] = part[...].astype(BF16)
            up_low.start()

        @pl.when(t == 2)
        def _():
            sib_out[1] = part[...].astype(BF16)
            up_high.start()

        @pl.when(t == 3)
        def _():
            up_low.wait_recv()
            add(0)
            leave(1)
            relay(0)

        @pl.when(t == 4)
        def _():
            up_high.wait_recv()
            add(1)
            leave(2)

        return carry

    lax.fori_loop(0, SLOTS, grads, 0)

    theirs = pl.multiple_of((1 - core) * 256, 256)
    mine = pl.multiple_of(core * 256, 256)
    to_sib = remote(g_out, g_in, s_g.at[0], r_g.at[0], sib)
    for n in range(4):
        g_out[:, n * 256 : n * 256 + 256] = mm(
            latt[pl.ds(theirs, 256), :], dkv[:, n * 256 : n * 256 + 256]
        ).astype(BF16)
    to_sib.start()
    for n in range(4):
        g_own[:, n * 256 : n * 256 + 256] = mm(
            latt[pl.ds(mine, 256), :], dkv[:, n * 256 : n * 256 + 256]
        )
    relay(1)

    for h in range(HEADS_HERE):
        dq = dqt[h].T
        dq_ref[:, h * 192 : h * 192 + 192] = dq[:, :192].astype(BF16)
    dq_out = pltpu.make_async_copy(dq_ref, dq_any, s_out.at[0])
    dq_out.start()

    to_sib.wait_recv()
    g_own[...] += g_in[...].astype(F32)
    gx_out[...] = g_own[...].astype(BF16)

    def scatter_x(by):
        there = pl.multiple_of(lax.rem(x + by, 4) * 64, 64)
        return remote(
            gx_out.at[pl.ds(there, 64), :], gx_in.at[by - 1], s_gx.at[by - 1], r_gx.at[by - 1], at_x(by)
        )

    for by in (2, 1, 3):
        scatter_x(by).start()
    relay(2)

    def to_owner(index, other):
        slot = index * 2 + other
        part_of = lax.rem(zl + other, 2)
        return remote(
            own_out.at[index, pl.ds(pl.multiple_of(part_of * 16, 16), 16), :], own_in.at[slot],
            s_own.at[slot], r_own.at[slot], owner(-4 + 2 * index, other),
        )

    def settle(index):
        which = lax.rem(index + 2 * core, 3)
        here = ys_own[index]
        for way in (1, -1):
            for kind in (0, 3):
                hop(index, kind, way).wait_recv()
                here = here + ys_in[index, 0 if way > 0 else 1, kind].astype(F32)
        own_out[which] = here.astype(BF16)

        @pl.when(which == 2)
        def _():
            own_keep[...] = here

        @pl.when(which < 2)
        def _():
            to_owner(which, 0).start()

        to_owner(which, 1).start()

    for index in range(3):
        settle(index)

    for by in range(1, 4):
        scatter_x(by).wait_recv()
    g_sum = g_own[pl.ds(pl.multiple_of(x * 64, 64), 64), :]
    for by in range(1, 4):
        g_sum = g_sum + gx_in[by - 1].astype(F32)
    g_own[0:64, :] = g_sum
    gz_out[...] = g_sum.astype(BF16)

    def scatter_zh(by):
        there = pl.multiple_of(lax.rem(zh + by, 4) * 16, 16)
        return remote(
            gz_out.at[pl.ds(there, 16), :], gz_in.at[by - 1], s_gz.at[by - 1], r_gz.at[by - 1], at_zh(by)
        )

    for by in (2, 1, 3):
        scatter_zh(by).start()

    for index in range(3):
        for other in (0, 1):
            if index < 2 or other:
                to_owner(index, other).wait_recv()
    final = own_keep[pl.ds(pl.multiple_of(zl * 16, 16), 16), :]
    for slot in range(5):
        final = final + own_in[slot if slot < 4 else 5].astype(F32)
    my_rows = pl.ds(pl.multiple_of(dp * 16, 16), 16)
    dlat_ref[my_rows, :] = final.astype(BF16)

    def to_all(by):
        return remote(
            dlat_ref.at[my_rows, :], dlat_ref.at[my_rows, :], s_ag.at[by - 1], r_ag.at[by - 1], at_dp(by)
        )

    for by in (8, 7, 9, 6, 10, 5, 11, 4, 12, 3, 13, 2, 14, 1, 15):
        to_all(by).start()

    for by in range(1, 4):
        scatter_zh(by).wait_recv()
    g_last = g_own[pl.ds(pl.multiple_of(zh * 16, 16), 16), :]
    for by in range(1, 4):
        g_last = g_last + gz_in[by - 1].astype(F32)
    dup_ref[...] = g_last
    dup_out = pltpu.make_async_copy(dup_ref, dup_any, s_out.at[1])
    dup_out.start()

    for by in range(1, 16):
        to_all(by).wait_recv()
    dlat_out = pltpu.make_async_copy(dlat_ref, dlat_any, s_out.at[2])
    dlat_out.start()

    for index in (0, 1):
        for half in (0, 1):
            along_z(index, half).wait_send()
        for j in range(6):
            along_y(index, j).wait_send()
    fw_own.wait_send()
    fw_mid_low.wait_send()
    for index in range(3):
        for kind in range(4):
            for way in (1, -1):
                hop(index, kind, way).wait_send()
    up_low.wait_send()
    up_high.wait_send()
    to_sib.wait_send()
    for by in range(1, 4):
        scatter_x(by).wait_send()
        scatter_zh(by).wait_send()
    for index in range(3):
        for other in (0, 1):
            if index < 2 or other:
                to_owner(index, other).wait_send()
    for by in range(1, 16):
        to_all(by).wait_send()
    dq_out.wait()
    dup_out.wait()
    dlat_out.wait()


def write_out(dq_in, dlat_in, dup_in, dq_any, dlat_ref, dupk_ref, dupv_ref, dlat, dup, sem):
    copies = [
        pltpu.make_async_copy(src, dst, sem.at[i])
        for i, (src, dst) in enumerate(((dlat_in, dlat), (dup_in, dup), (dq_in, dq_any)))
    ]
    for copy in copies:
        copy.start()
    copies[0].wait()
    dlat_ref[...] = dlat[...].astype(F32).T[: LAT + ROPE, :]
    copies[1].wait()
    dupk_ref[...] = dup[:, :512]
    dupv_ref[...] = dup[:, 512:]
    copies[2].wait()


def shards(queries, latent, grad_out, doc_ids, up_key, up_value):
    vmem = pl.BlockSpec(memory_space=pltpu.VMEM)
    anywhere = pl.BlockSpec(memory_space=pl.ANY)
    dma = pltpu.SemaphoreType.DMA
    shape = jax.ShapeDtypeStruct
    made = pl.pallas_call(
        kernel,
        out_shape=(shape((ROWS, 768), BF16), shape((ROWS, WIDE), BF16), shape((16, 1024), F32)),
        in_specs=[anywhere] * 6,
        out_specs=(anywhere,) * 3,
        scratch_shapes=[
            pltpu.VMEM((ROWS, 768), BF16),
            pltpu.VMEM((ROWS, WIDE), BF16),
            pltpu.VMEM((16, 1024), F32),
            pltpu.VMEM((ROWS, 768), BF16),
            pltpu.VMEM((LAT + ROPE, ROWS), BF16),
            pltpu.VMEM((ROWS, 512), BF16),
            pltpu.VMEM((1, ROWS), jnp.int32),
            pltpu.VMEM((SLOTS, ROWS, WIDE), BF16),
            pltpu.VMEM((ROWS, 1024), BF16),
            pltpu.VMEM((LAT, 1024), BF16),
            pltpu.VMEM((SLOTS * ROWS, 1024), BF16),
            pltpu.VMEM((SLOTS, WIDE, ROWS), BF16),
            pltpu.VMEM((LAT, SLOTS * ROWS), BF16),
            pltpu.VMEM((SLOTS * ROWS, 1024), F32),
            pltpu.VMEM((SLOTS * ROWS, 1024), F32),
            pltpu.VMEM((3, 8, 1024), F32),
            pltpu.VMEM((ROWS, ROWS), F32),
            pltpu.VMEM((HEADS_HERE, 256, ROWS), F32),
            pltpu.VMEM((SLOTS * ROWS, 1024), BF16),
            pltpu.VMEM((ROWS, WIDE), F32),
            pltpu.VMEM((2, ROWS, WIDE), BF16),
            pltpu.VMEM((2, ROWS, WIDE), BF16),
            pltpu.VMEM((3, ROWS, WIDE), BF16),
            pltpu.VMEM((3, 32, WIDE), F32),
            pltpu.VMEM((3, 2, 4, 32, WIDE), BF16),
            pltpu.VMEM((3, 32, WIDE), BF16),
            pltpu.VMEM((6, 16, WIDE), BF16),
            pltpu.VMEM((32, WIDE), F32),
            pltpu.VMEM((256, 1024), BF16),
            pltpu.VMEM((256, 1024), BF16),
            pltpu.VMEM((256, 1024), F32),
            pltpu.VMEM((256, 1024), BF16),
            pltpu.VMEM((3, 64, 1024), BF16),
            pltpu.VMEM((64, 1024), BF16),
            pltpu.VMEM((3, 16, 1024), BF16),
            dma((6,)),
            dma((3,)),
            dma((2, 2)), dma((2, 2)),
            dma((2, 6)), dma((2, 6)),
            dma((2,)), dma((2,)),
            dma((2,)), dma((2,)),
            dma((3, 2, 4)), dma((3, 2, 4)),
            dma((6,)), dma((6,)),
            dma((15,)), dma((15,)),
            dma((1,)), dma((1,)),
            dma((3,)), dma((3,)),
            dma((3,)), dma((3,)),
        ],
        compiler_params=pltpu.CompilerParams(
            collective_id=0, has_side_effects=True, vmem_limit_bytes=56 * 1024 * 1024
        ),
        name="mla_backward",
    )(queries, latent.T, grad_out, doc_ids.reshape(1, ROWS), up_key, up_value)
    grad_queries, grad_latent, grad_up_key, grad_up_value = pl.pallas_call(
        write_out,
        out_shape=(
            shape((ROWS, 768), BF16), shape((LAT + ROPE, ROWS), F32),
            shape((16, 512), F32), shape((16, 512), F32),
        ),
        in_specs=[anywhere] * 3,
        out_specs=(anywhere, vmem, vmem, vmem),
        scratch_shapes=[pltpu.VMEM((ROWS, WIDE), BF16), pltpu.VMEM((16, 1024), F32), dma((3,))],
        compiler_params=pltpu.CompilerParams(vmem_limit_bytes=63 * 1024 * 1024),
        name="write_out",
    )(*made)
    return grad_queries, grad_latent.T, grad_up_key, grad_up_value


def solution(mesh):
    return jax.shard_map(
        shards,
        mesh=mesh,
        in_specs=(P("ctx", "dp"), P("ctx", None), P("ctx", "dp"), P("ctx"), P(None, "dp"), P(None, "dp")),
        out_specs=(P("ctx", "dp"), P("ctx", None), P("ctx", "dp"), P("ctx", "dp")),
        check_vma=False,
    )
```

```python
import functools
import jax
import jax.numpy as jnp
from jax import lax
from jax.experimental import pallas as pl
from jax.experimental.pallas import tpu as pltpu
from jax.sharding import PartitionSpec as P

LAT = 512
ROPE = 64
NOPE = 128
ROWS = 256
HEADS_HERE = 4
WIDE = 640
SLOTS = 5
SCALE = (NOPE + ROPE) ** -0.5
LOG2E = 1.4426950408889634
LOW = -1e30
MESH = pl.DeviceIdType.MESH
F32 = jnp.float32
BF16 = jnp.bfloat16
NT = (((1,), (1,)), ((), ()))
NN = (((1,), (0,)), ((), ()))


def mm(a, b, dims=NN):
    return lax.dot_general(a, b, dims, preferred_element_type=F32)


def kernel(
    q_any, lat_any, go_any, doc_any, upk_any, upv_any,
    dq_any, dlat_any, dup_any,
    dq_ref, dlat_ref, dup_ref, q_ref, lat_ref, go_ref, doc_ref, win, qx, ups, kv, kxt, latt, probs, gprobs, stats, bias, dqt, dkv,
    part, sib_out, sib_in, ys_out, ys_own, ys_in, own_out, own_in, own_keep,
    g_out, g_in, g_own, gx_out, gx_in, gz_out, gz_in,
    s_in, s_out, s_z, r_z, s_y, r_y, s_fw, r_fw, s_sib, r_sib, s_ys, r_ys,
    s_own, r_own, s_ag, r_ag, s_g, r_g, s_gx, r_gx, s_gz, r_gz,
):
    dp = lax.axis_index("dp")
    ctx = lax.axis_index("ctx")
    y, zl = lax.div(dp, 2), lax.rem(dp, 2)
    x, zh, core = lax.div(ctx, 8), lax.rem(lax.div(ctx, 2), 4), lax.rem(ctx, 2)
    sib = (dp, ctx + 1 - 2 * core)

    def at_ctx(by):
        return lax.rem(ctx + by + 32, 32)

    def at_y(by):
        return (lax.rem(y + by + 8, 8) * 2 + zl, ctx)

    def at_dp(by):
        return (lax.rem(dp + by + 16, 16), ctx)

    def at_x(by):
        return (dp, lax.rem(x + by + 4, 4) * 8 + zh * 2 + core)

    def at_zh(by):
        return (dp, x * 8 + lax.rem(zh + by + 4, 4) * 2 + core)

    def owner(by, other):
        mate = dp + 1 - 2 * zl if other else dp
        return (mate, at_ctx(by))

    barrier = pltpu.get_barrier_semaphore()
    senders = [sib, (dp, at_ctx(-2)), (dp, at_ctx(-4))]
    senders += [owner(by, other) for by in (0, 2, 4) for other in (0, 1) if by or other]
    senders += [at_dp(-i) for i in range(1, 16)]
    senders += [at_x(-i) for i in range(1, 4)]
    senders += [at_zh(-i) for i in range(1, 4)]
    for sender in senders:
        pl.semaphore_signal(barrier, inc=1, device_id=sender, device_id_type=MESH)

    loads = [
        pltpu.make_async_copy(src, dst, s_in.at[i])
        for i, (src, dst) in enumerate((
            (lat_any, lat_ref), (doc_any, doc_ref), (upk_any, ups.at[:, :512]),
            (upv_any, ups.at[:, 512:]), (q_any, q_ref), (go_any, go_ref),
        ))
    ]
    for load in loads:
        load.start()

    def remote(src, dst, send, recv, to):
        return pltpu.make_async_remote_copy(
            src_ref=src, dst_ref=dst, send_sem=send, recv_sem=recv,
            device_id=to, device_id_type=MESH,
        )

    loads[0].wait()
    loads[1].wait()
    doc_row = doc_ref[...].astype(F32)
    line = lax.broadcasted_iota(jnp.int32, (ROWS, ROWS), 0)
    lane = lax.broadcasted_iota(jnp.int32, (ROWS, ROWS), 1)
    doc_col = jnp.sum(jnp.where(line == lane, doc_row, 0.0), axis=1, keepdims=True)
    win[4, :, :LAT] = lat_ref[:LAT, :].T
    tail = jnp.concatenate([lat_ref[LAT:, :].astype(F32), jnp.zeros((64, ROWS), F32)], axis=0).T
    tail_lane = lax.broadcasted_iota(jnp.int32, (ROWS, 128), 1)
    win[4, :, LAT:] = jnp.where(tail_lane == 64, doc_col, tail).astype(BF16)

    pl.semaphore_wait(barrier, len(senders))

    def shares(slot, who):
        return win.at[slot, pl.ds(pl.multiple_of(who * 32, 32), 32), :]

    def along_z(index, half):
        who = lax.rem(y + 4 * half, 8)
        return remote(
            shares(4, who), shares(2 - 2 * index, who), s_z.at[index, half], r_z.at[index, half],
            (dp, at_ctx(2 + 2 * index)),
        )

    for index in (0, 1):
        for half in (0, 1):
            along_z(index, half).start()

    fw_own = remote(win.at[4], win.at[3], s_fw.at[0], r_fw.at[0], sib)
    fw_mid = remote(win.at[2], win.at[3], s_fw.at[0], r_fw.at[0], sib)
    fw_mid_low = remote(win.at[2], win.at[1], s_fw.at[1], r_fw.at[1], sib)
    fw_far_low = remote(win.at[0], win.at[1], s_fw.at[1], r_fw.at[1], sib)

    @pl.when(core == 0)
    def _():
        fw_own.start()

    passes = ((2, 0), (-2, 0), (1, 0), (-1, 0), (1, 4), (-1, 4))

    def along_y(index, j):
        by, more = passes[j]
        rows = shares(2 - 2 * index, lax.rem(y + more, 8))
        return remote(rows, rows, s_y.at[index, j], r_y.at[index, j], at_y(by))

    for load in loads[2:]:
        load.wait()

    for h in range(HEADS_HERE):
        qx[:, h * 256 : h * 256 + 128] = q_ref[:, h * 192 : h * 192 + 128]
        qx[:, h * 256 + 128 : h * 256 + 256] = jnp.concatenate(
            [q_ref[:, h * 192 + 128 : h * 192 + 192], jnp.zeros((ROWS, 64), BF16)], axis=1
        )
    dqt[...] = jnp.zeros_like(dqt)

    for index in (0, 1):
        for half in (0, 1):
            along_z(index, half).wait_recv()
        for j in range(6):
            along_y(index, j).start()

    def scores(t, carry):
        slot = jnp.where(
            t == 0, 4,
            jnp.where(t == 1, 2 + core, jnp.where(t == 2, 3 - core, jnp.where(t == 3, 0, 1))),
        )

        @pl.when(t == 1 + core)
        def _():
            for j in range(6):
                along_y(0, j).wait_recv()

            @pl.when(core == 0)
            def _():
                fw_mid_low.start()

            @pl.when(core == 1)
            def _():
                fw_mid.start()

        @pl.when(t == 3)
        def _():
            for j in range(6):
                along_y(1, j).wait_recv()

            @pl.when(core == 1)
            def _():
                fw_far_low.start()

        @pl.when(t == 2 - core)
        def _():
            fw_own.wait_recv()

        @pl.when(t == 4)
        def _():
            fw_mid_low.wait_recv()

        start = pl.multiple_of(slot * ROWS, ROWS)
        block = win[slot]
        latent = block[:, :LAT]
        rope = block[:, LAT:]
        for n in range(4):
            kv[pl.ds(start, ROWS), n * 256 : n * 256 + 256] = mm(
                latent, ups[:, n * 256 : n * 256 + 256]
            ).astype(BF16)
        keys = kv[pl.ds(start, ROWS), :512]
        kxt[slot, :512, :] = keys.T
        kxt[slot, 512:, :] = rope.T
        flipped = latent.T
        for g in range(32):
            row = (g % 2) * 256 + (g // 2) * 16
            latt[row : row + 16, pl.ds(start, ROWS)] = flipped[g * 16 : g * 16 + 16, :]
        docs = rope[:, 64:65].astype(F32)
        past = jnp.logical_or(slot < 4, line <= lane)
        bias[...] = jnp.where(jnp.logical_and(docs == doc_row, past), 0.0, LOW)
        for h in range(HEADS_HERE):
            cols = slice(h * 256, h * 256 + 256)
            key = kv[pl.ds(start, ROWS), h * 128 : h * 128 + 128]
            value = kv[pl.ds(start, ROWS), 512 + h * 128 : 640 + h * 128]
            s = mm(jnp.concatenate([key, rope], axis=1), qx[:, cols], NT) + bias[...]
            top = jnp.max(s, axis=0, keepdims=True)
            p = jnp.exp2((s - top) * (SCALE * LOG2E))
            gp = mm(value, go_ref[:, h * 128 : h * 128 + 128], NT)
            probs[pl.ds(start, ROWS), cols] = p
            gprobs[pl.ds(start, ROWS), cols] = gp
            stats[0, pl.ds(slot, 1), cols] = top
            stats[1, pl.ds(slot, 1), cols] = jnp.sum(p, axis=0, keepdims=True)
            stats[2, pl.ds(slot, 1), cols] = jnp.sum(p * gp, axis=0, keepdims=True)
        return carry

    lax.fori_loop(0, SLOTS, scores, 0)

    tops = stats[0, 0:SLOTS, :]
    factor = jnp.exp2((tops - jnp.max(tops, axis=0, keepdims=True)) * (SCALE * LOG2E))
    total = jnp.sum(stats[1, 0:SLOTS, :] * factor, axis=0, keepdims=True)
    delta = jnp.sum(stats[2, 0:SLOTS, :] * factor, axis=0, keepdims=True) / total
    stats[0, 0:SLOTS, :] = factor / total
    stats[1, 0:1, :] = delta

    up_low = remote(sib_out.at[0], sib_in.at[0], s_sib.at[0], r_sib.at[0], sib)
    up_high = remote(sib_out.at[1], sib_in.at[1], s_sib.at[1], r_sib.at[1], sib)

    def share_of(by):
        return pl.multiple_of(lax.rem(y + by + 8, 8) * 32, 32)

    def hop(index, kind, way):
        side = 0 if way > 0 else 1
        by, dest = ((1, 1), (1, 3), (2, 4), (2, 2))[kind]
        rows, into = pl.ds(share_of(way * dest), 32), pl.ds(0, 32)
        if kind == 2:
            rows = pl.ds(pl.multiple_of(share_of(4) + 16 * side, 16), 16)
            into = pl.ds(0, 16)
        return remote(
            ys_out.at[index, rows, :], ys_in.at[index, side, kind, into, :],
            s_ys.at[index, side, kind], r_ys.at[index, side, kind], at_y(way * by),
        )

    def relay(index):
        for way in (1, -1):
            side = 0 if way > 0 else 1
            hop(index, 1, way).wait_recv()
            hop(index, 2, way).wait_recv()
            rows = pl.ds(share_of(2 * way), 32)
            more = ys_in[index, side, 1].astype(F32)
            half = ys_in[index, side, 2, 0:16, :].astype(F32)
            empty = jnp.zeros_like(half)
            more = more + jnp.concatenate([empty, half] if side else [half, empty], axis=0)
            ys_out[index, rows, :] = (ys_out[index, rows, :].astype(F32) + more).astype(BF16)
            hop(index, 3, way).start()

    def grads(t, carry):
        slot = jnp.where(
            t == 0, 4 * core, jnp.where(t < 3, 2 * t - 1, jnp.where(t == 3, 2 - 2 * core, 4 - 2 * core))
        )
        start = pl.multiple_of(slot * ROWS, ROWS)
        rope_sum = jnp.zeros((ROWS, 128), F32)
        for h in range(HEADS_HERE):
            cols = slice(h * 256, h * 256 + 256)
            p = probs[pl.ds(start, ROWS), cols] * stats[0, pl.ds(slot, 1), cols]
            ds = (SCALE * p * (gprobs[pl.ds(start, ROWS), cols] - stats[1, 0:1, cols])).astype(BF16)
            dv = mm(p.astype(BF16), go_ref[:, h * 128 : h * 128 + 128])
            dk = mm(ds, qx[:, cols])
            dkv[pl.ds(start, ROWS), h * 128 : h * 128 + 128] = dk[:, :128].astype(BF16)
            dkv[pl.ds(start, ROWS), 512 + h * 128 : 640 + h * 128] = dv.astype(BF16)
            rope_sum = rope_sum + dk[:, 128:]
            key_t = jnp.concatenate(
                [kxt[slot, h * 128 : h * 128 + 128, :], kxt[slot, 512:, :]], axis=0
            )
            dqt[h] += mm(key_t, ds)
        part[:, LAT:] = rope_sum
        both = dkv[pl.ds(start, ROWS), :]
        for n in range(2):
            part[:, n * 256 : n * 256 + 256] = mm(both, ups[n * 256 : n * 256 + 256, :], NT)

        def add(which):
            part[...] += sib_in[which].astype(F32)

        def leave(index):
            ys_out[index] = part[...].astype(BF16)
            ys_own[index] = part[pl.ds(pl.multiple_of(y * 32, 32), 32), :]
            for kind in (2, 1, 0):
                for way in (1, -1):
                    hop(index, kind, way).start()

        @pl.when(t == 0)
        def _():
            leave(0)

        @pl.when(t == 1)
        def _():
            sib_out[0] = part[...].astype(BF16)
            up_low.start()

        @pl.when(t == 2)
        def _():
            sib_out[1] = part[...].astype(BF16)
            up_high.start()

        @pl.when(t == 3)
        def _():
            up_low.wait_recv()
            add(0)
            leave(1)
            relay(0)

        @pl.when(t == 4)
        def _():
            up_high.wait_recv()
            add(1)
            leave(2)

        return carry

    lax.fori_loop(0, SLOTS, grads, 0)

    theirs = pl.multiple_of((1 - core) * 256, 256)
    mine = pl.multiple_of(core * 256, 256)
    to_sib = remote(g_out, g_in, s_g.at[0], r_g.at[0], sib)
    for n in range(4):
        g_out[:, n * 256 : n * 256 + 256] = mm(
            latt[pl.ds(theirs, 256), :], dkv[:, n * 256 : n * 256 + 256]
        ).astype(BF16)
    to_sib.start()
    for n in range(4):
        g_own[:, n * 256 : n * 256 + 256] = mm(
            latt[pl.ds(mine, 256), :], dkv[:, n * 256 : n * 256 + 256]
        )
    relay(1)
    relay(2)

    for h in range(HEADS_HERE):
        dq = dqt[h].T
        dq_ref[:, h * 192 : h * 192 + 192] = dq[:, :192].astype(BF16)
    dq_out = pltpu.make_async_copy(dq_ref, dq_any, s_out.at[0])
    dq_out.start()

    to_sib.wait_recv()
    g_own[...] += g_in[...].astype(F32)
    gx_out[...] = g_own[...].astype(BF16)

    def scatter_x(by):
        there = pl.multiple_of(lax.rem(x + by, 4) * 64, 64)
        return remote(
            gx_out.at[pl.ds(there, 64), :], gx_in.at[by - 1], s_gx.at[by - 1], r_gx.at[by - 1], at_x(by)
        )

    for by in (2, 1, 3):
        scatter_x(by).start()

    def to_owner(index, other):
        slot = index * 2 + other
        part_of = lax.rem(zl + other, 2)
        return remote(
            own_out.at[index, pl.ds(pl.multiple_of(part_of * 16, 16), 16), :], own_in.at[slot],
            s_own.at[slot], r_own.at[slot], owner(-4 + 2 * index, other),
        )

    def settle(index):
        which = lax.rem(index + 2 * core, 3)
        here = ys_own[index]
        for way in (1, -1):
            for kind in (0, 3):
                hop(index, kind, way).wait_recv()
                here = here + ys_in[index, 0 if way > 0 else 1, kind].astype(F32)
        own_out[which] = here.astype(BF16)

        @pl.when(which == 2)
        def _():
            own_keep[...] = here

        @pl.when(which < 2)
        def _():
            to_owner(which, 0).start()

        to_owner(which, 1).start()

    for index in range(3):
        settle(index)

    for index in range(3):
        for other in (0, 1):
            if index < 2 or other:
                to_owner(index, other).wait_recv()
    final = own_keep[pl.ds(pl.multiple_of(zl * 16, 16), 16), :]
    for slot in range(5):
        final = final + own_in[slot if slot < 4 else 5].astype(F32)
    my_rows = pl.ds(pl.multiple_of(dp * 16, 16), 16)
    dlat_ref[my_rows, :] = final.astype(BF16)

    def to_all(by):
        return remote(
            dlat_ref.at[my_rows, :], dlat_ref.at[my_rows, :], s_ag.at[by - 1], r_ag.at[by - 1], at_dp(by)
        )

    for by in (8, 7, 9, 6, 10, 5, 11, 4, 12, 3, 13, 2, 14, 1, 15):
        to_all(by).start()

    for by in range(1, 4):
        scatter_x(by).wait_recv()
    g_sum = g_own[pl.ds(pl.multiple_of(x * 64, 64), 64), :]
    for by in range(1, 4):
        g_sum = g_sum + gx_in[by - 1].astype(F32)
    g_own[0:64, :] = g_sum
    gz_out[...] = g_sum.astype(BF16)

    def scatter_zh(by):
        there = pl.multiple_of(lax.rem(zh + by, 4) * 16, 16)
        return remote(
            gz_out.at[pl.ds(there, 16), :], gz_in.at[by - 1], s_gz.at[by - 1], r_gz.at[by - 1], at_zh(by)
        )

    for by in (2, 1, 3):
        scatter_zh(by).start()

    for by in range(1, 4):
        scatter_zh(by).wait_recv()
    g_last = g_own[pl.ds(pl.multiple_of(zh * 16, 16), 16), :]
    for by in range(1, 4):
        g_last = g_last + gz_in[by - 1].astype(F32)
    dup_ref[...] = g_last
    dup_out = pltpu.make_async_copy(dup_ref, dup_any, s_out.at[1])
    dup_out.start()

    for by in range(1, 16):
        to_all(by).wait_recv()
    dlat_out = pltpu.make_async_copy(dlat_ref, dlat_any, s_out.at[2])
    dlat_out.start()

    for index in (0, 1):
        for half in (0, 1):
            along_z(index, half).wait_send()
        for j in range(6):
            along_y(index, j).wait_send()
    fw_own.wait_send()
    fw_mid_low.wait_send()
    for index in range(3):
        for kind in range(4):
            for way in (1, -1):
                hop(index, kind, way).wait_send()
    up_low.wait_send()
    up_high.wait_send()
    to_sib.wait_send()
    for by in range(1, 4):
        scatter_x(by).wait_send()
        scatter_zh(by).wait_send()
    for index in range(3):
        for other in (0, 1):
            if index < 2 or other:
                to_owner(index, other).wait_send()
    for by in range(1, 16):
        to_all(by).wait_send()
    dq_out.wait()
    dup_out.wait()
    dlat_out.wait()


def write_out(dq_in, dlat_in, dup_in, dq_ref, dlat_ref, dupk_ref, dupv_ref, dlat, dup, sem):
    copies = [
        pltpu.make_async_copy(src, dst, sem.at[i])
        for i, (src, dst) in enumerate(((dlat_in, dlat), (dup_in, dup), (dq_in, dq_ref)))
    ]
    for copy in copies:
        copy.start()
    copies[0].wait()
    dlat_ref[...] = dlat[...].astype(F32).T[: LAT + ROPE, :]
    copies[1].wait()
    dupk_ref[...] = dup[:, :512]
    dupv_ref[...] = dup[:, 512:]
    copies[2].wait()


def shards(queries, latent, grad_out, doc_ids, up_key, up_value):
    vmem = pl.BlockSpec(memory_space=pltpu.VMEM)
    anywhere = pl.BlockSpec(memory_space=pl.ANY)
    dma = pltpu.SemaphoreType.DMA
    shape = jax.ShapeDtypeStruct
    made = pl.pallas_call(
        kernel,
        out_shape=(shape((ROWS, 768), BF16), shape((ROWS, WIDE), BF16), shape((16, 1024), F32)),
        in_specs=[anywhere] * 6,
        out_specs=(anywhere,) * 3,
        scratch_shapes=[
            pltpu.VMEM((ROWS, 768), BF16),
            pltpu.VMEM((ROWS, WIDE), BF16),
            pltpu.VMEM((16, 1024), F32),
            pltpu.VMEM((ROWS, 768), BF16),
            pltpu.VMEM((LAT + ROPE, ROWS), BF16),
            pltpu.VMEM((ROWS, 512), BF16),
            pltpu.VMEM((1, ROWS), jnp.int32),
            pltpu.VMEM((SLOTS, ROWS, WIDE), BF16),
            pltpu.VMEM((ROWS, 1024), BF16),
            pltpu.VMEM((LAT, 1024), BF16),
            pltpu.VMEM((SLOTS * ROWS, 1024), BF16),
            pltpu.VMEM((SLOTS, WIDE, ROWS), BF16),
            pltpu.VMEM((LAT, SLOTS * ROWS), BF16),
            pltpu.VMEM((SLOTS * ROWS, 1024), F32),
            pltpu.VMEM((SLOTS * ROWS, 1024), F32),
            pltpu.VMEM((3, 8, 1024), F32),
            pltpu.VMEM((ROWS, ROWS), F32),
            pltpu.VMEM((HEADS_HERE, 256, ROWS), F32),
            pltpu.VMEM((SLOTS * ROWS, 1024), BF16),
            pltpu.VMEM((ROWS, WIDE), F32),
            pltpu.VMEM((2, ROWS, WIDE), BF16),
            pltpu.VMEM((2, ROWS, WIDE), BF16),
            pltpu.VMEM((3, ROWS, WIDE), BF16),
            pltpu.VMEM((3, 32, WIDE), F32),
            pltpu.VMEM((3, 2, 4, 32, WIDE), BF16),
            pltpu.VMEM((3, 32, WIDE), BF16),
            pltpu.VMEM((6, 16, WIDE), BF16),
            pltpu.VMEM((32, WIDE), F32),
            pltpu.VMEM((256, 1024), BF16),
            pltpu.VMEM((256, 1024), BF16),
            pltpu.VMEM((256, 1024), F32),
            pltpu.VMEM((256, 1024), BF16),
            pltpu.VMEM((3, 64, 1024), BF16),
            pltpu.VMEM((64, 1024), BF16),
            pltpu.VMEM((3, 16, 1024), BF16),
            dma((6,)),
            dma((3,)),
            dma((2, 2)), dma((2, 2)),
            dma((2, 6)), dma((2, 6)),
            dma((2,)), dma((2,)),
            dma((2,)), dma((2,)),
            dma((3, 2, 4)), dma((3, 2, 4)),
            dma((6,)), dma((6,)),
            dma((15,)), dma((15,)),
            dma((1,)), dma((1,)),
            dma((3,)), dma((3,)),
            dma((3,)), dma((3,)),
        ],
        compiler_params=pltpu.CompilerParams(
            collective_id=0, has_side_effects=True, vmem_limit_bytes=56 * 1024 * 1024
        ),
        name="mla_backward",
    )(queries, latent.T, grad_out, doc_ids.reshape(1, ROWS), up_key, up_value)
    grad_queries, grad_latent, grad_up_key, grad_up_value = pl.pallas_call(
        write_out,
        out_shape=(
            shape((ROWS, 768), BF16), shape((LAT + ROPE, ROWS), F32),
            shape((16, 512), F32), shape((16, 512), F32),
        ),
        in_specs=[anywhere] * 3,
        out_specs=(vmem,) * 4,
        scratch_shapes=[pltpu.VMEM((ROWS, WIDE), BF16), pltpu.VMEM((16, 1024), F32), dma((3,))],
        compiler_params=pltpu.CompilerParams(vmem_limit_bytes=63 * 1024 * 1024),
        name="write_out",
    )(*made)
    return grad_queries, grad_latent.T, grad_up_key, grad_up_value


def solution(mesh):
    return jax.shard_map(
        shards,
        mesh=mesh,
        in_specs=(P("ctx", "dp"), P("ctx", None), P("ctx", "dp"), P("ctx"), P(None, "dp"), P(None, "dp")),
        out_specs=(P("ctx", "dp"), P("ctx", None), P("ctx", "dp"), P("ctx", "dp")),
        check_vma=False,
    )
```

```python
import functools
import jax
import jax.numpy as jnp
from jax import lax
from jax.experimental import pallas as pl
from jax.experimental.pallas import tpu as pltpu
from jax.sharding import PartitionSpec as P

LAT = 512
ROPE = 64
NOPE = 128
ROWS = 256
HEADS_HERE = 4
WIDE = 640
PACK = 144
SLOTS = 5
SCALE = (NOPE + ROPE) ** -0.5
LOG2E = 1.4426950408889634
LOW = -1e30
MESH = pl.DeviceIdType.MESH
F32 = jnp.float32
BF16 = jnp.bfloat16
NT = (((1,), (1,)), ((), ()))
NN = (((1,), (0,)), ((), ()))


def mm(a, b, dims=NN):
    return lax.dot_general(a, b, dims, preferred_element_type=F32)


def side_by_side(first, second):
    return first + pltpu.roll(second, 64, 1)


def packed(block):
    tiles = [block[:, n * 128 : n * 128 + 128] for n in range(4)]
    return jnp.concatenate(tiles + [side_by_side(block[:16, LAT:], block[16:, LAT:])], axis=0)


def kernel(
    q_any, lat_any, go_any, doc_any, upk_any, upv_any,
    dq_any, dlat_any, dup_any,
    dq_ref, dlat_ref, dup_ref, q_ref, lat_ref, go_ref, docs, win, latent_ref, rope_ref, qx, ups, kv, kxt, latt, probs, gprobs, stats, bias, dqt, dkv,
    part, sib_out, sib_in, ys_out, ys_own, ys_in, own_out, own_in, own_keep,
    g_out, g_in, g_own, gx_out, gx_in, gz_out, gz_in,
    s_in, s_out, s_doc, r_doc, s_z, r_z, s_y, r_y, s_fw, r_fw, s_sib, r_sib, s_ys, r_ys,
    s_own, r_own, s_ag, r_ag, s_g, r_g, s_gx, r_gx, s_gz, r_gz,
):
    dp = lax.axis_index("dp")
    ctx = lax.axis_index("ctx")
    y, zl = lax.div(dp, 2), lax.rem(dp, 2)
    x, zh, core = lax.div(ctx, 8), lax.rem(lax.div(ctx, 2), 4), lax.rem(ctx, 2)
    sib = (dp, ctx + 1 - 2 * core)

    def at_ctx(by):
        return lax.rem(ctx + by + 32, 32)

    def at_y(by):
        return (lax.rem(y + by + 8, 8) * 2 + zl, ctx)

    def at_dp(by):
        return (lax.rem(dp + by + 16, 16), ctx)

    def at_x(by):
        return (dp, lax.rem(x + by + 4, 4) * 8 + zh * 2 + core)

    def at_zh(by):
        return (dp, x * 8 + lax.rem(zh + by + 4, 4) * 2 + core)

    def owner(by, other):
        mate = dp + 1 - 2 * zl if other else dp
        return (mate, at_ctx(by))

    barrier = pltpu.get_barrier_semaphore()
    senders = [sib] + [(dp, at_ctx(-i)) for i in range(1, 5)]
    senders += [owner(by, other) for by in (0, 2, 4) for other in (0, 1) if by or other]
    senders += [at_dp(-i) for i in range(1, 16)]
    senders += [at_x(-i) for i in range(1, 4)]
    senders += [at_zh(-i) for i in range(1, 4)]
    for sender in senders:
        pl.semaphore_signal(barrier, inc=1, device_id=sender, device_id_type=MESH)

    loads = [
        pltpu.make_async_copy(src, dst, s_in.at[i])
        for i, (src, dst) in enumerate((
            (lat_any, lat_ref), (doc_any, docs.at[4, 0:1, :]), (upk_any, ups.at[:, :512]),
            (upv_any, ups.at[:, 512:]), (q_any, q_ref), (go_any, go_ref),
        ))
    ]
    for load in loads:
        load.start()

    def remote(src, dst, send, recv, to):
        return pltpu.make_async_remote_copy(
            src_ref=src, dst_ref=dst, send_sem=send, recv_sem=recv,
            device_id=to, device_id_type=MESH,
        )

    loads[0].wait()
    loads[1].wait()
    doc_row = docs[4, 0:1, :]
    line = lax.broadcasted_iota(jnp.int32, (ROWS, ROWS), 0)
    lane = lax.broadcasted_iota(jnp.int32, (ROWS, ROWS), 1)
    rows_of = lat_ref[:LAT, :].T
    tail = jnp.concatenate([lat_ref[LAT:, :].astype(F32), jnp.zeros((64, ROWS), F32)], axis=0).T
    for who in range(8):
        for n in range(4):
            win[4, who, n * 32 : n * 32 + 32, :] = rows_of[who * 32 : who * 32 + 32, n * 128 : n * 128 + 128]
        win[4, who, 128:, :] = side_by_side(
            tail[who * 32 : who * 32 + 16, :], tail[who * 32 + 16 : who * 32 + 32, :]
        ).astype(BF16)

    pl.semaphore_wait(barrier, len(senders))

    def shares(slot, who):
        return win.at[slot, who]

    def tell(by):
        return remote(
            docs.at[4], docs.at[4 - by], s_doc.at[by - 1], r_doc.at[by - 1], (dp, at_ctx(by))
        )

    def along_z(index, half):
        who = lax.rem(y + 4 * half, 8)
        return remote(
            shares(4, who), shares(2 - 2 * index, who), s_z.at[index, half], r_z.at[index, half],
            (dp, at_ctx(2 + 2 * index)),
        )

    for index in (0, 1):
        for half in (0, 1):
            along_z(index, half).start()
    for by in range(1, 5):
        tell(by).start()

    fw_own = remote(win.at[4], win.at[3], s_fw.at[0], r_fw.at[0], sib)
    fw_mid = remote(win.at[2], win.at[3], s_fw.at[0], r_fw.at[0], sib)
    fw_mid_low = remote(win.at[2], win.at[1], s_fw.at[1], r_fw.at[1], sib)
    fw_far_low = remote(win.at[0], win.at[1], s_fw.at[1], r_fw.at[1], sib)

    @pl.when(core == 0)
    def _():
        fw_own.start()

    passes = ((2, 0, 0), (-2, 0, 0), (1, 0, 0), (-1, 0, 0), (1, 4, 1), (-1, 4, 1))

    def along_y(index, j):
        by, more, _ = passes[j]
        rows = shares(2 - 2 * index, lax.rem(y + more, 8))
        return remote(rows, rows, s_y.at[index, j], r_y.at[index, j], at_y(by))

    for load in loads[2:]:
        load.wait()

    for h in range(HEADS_HERE):
        qx[:, h * 256 : h * 256 + 128] = q_ref[:, h * 192 : h * 192 + 128]
        qx[:, h * 256 + 128 : h * 256 + 256] = jnp.concatenate(
            [q_ref[:, h * 192 + 128 : h * 192 + 192], jnp.zeros((ROWS, 64), BF16)], axis=1
        )
    dqt[...] = jnp.zeros_like(dqt)

    for index in (0, 1):
        for half in (0, 1):
            along_z(index, half).wait_recv()
            for j in range(6):
                if passes[j][2] == half:
                    along_y(index, j).start()
    for by in range(1, 5):
        tell(by).wait_recv()

    def scores(t, carry):
        slot = jnp.where(
            t == 0, 4,
            jnp.where(t == 1, 2 + core, jnp.where(t == 2, 3 - core, jnp.where(t == 3, 0, 1))),
        )

        @pl.when(t == 1 + core)
        def _():
            for j in range(6):
                along_y(0, j).wait_recv()

            @pl.when(core == 0)
            def _():
                fw_mid_low.start()

            @pl.when(core == 1)
            def _():
                fw_mid.start()

        @pl.when(t == 3)
        def _():
            for j in range(6):
                along_y(1, j).wait_recv()

            @pl.when(core == 1)
            def _():
                fw_far_low.start()

        @pl.when(t == 2 - core)
        def _():
            fw_own.wait_recv()

        @pl.when(t == 4)
        def _():
            fw_mid_low.wait_recv()

        start = pl.multiple_of(slot * ROWS, ROWS)
        for who in range(8):
            for n in range(4):
                latent_ref[who * 32 : who * 32 + 32, n * 128 : n * 128 + 128] = win[
                    slot, who, n * 32 : n * 32 + 32, :
                ]
            both_ropes = win[slot, who, 128:, :]
            rope_ref[who * 32 : who * 32 + 16, :] = both_ropes
            rope_ref[who * 32 + 16 : who * 32 + 32, :] = pltpu.roll(
                both_ropes.astype(F32), 64, 1
            ).astype(BF16)
        latent = latent_ref[...]
        rope = rope_ref[...]
        for n in range(4):
            kv[pl.ds(start, ROWS), n * 256 : n * 256 + 256] = mm(
                latent, ups[:, n * 256 : n * 256 + 256]
            ).astype(BF16)
        keys = kv[pl.ds(start, ROWS), :512]
        kxt[slot, :512, :] = keys.T
        kxt[slot, 512:, :] = rope.T
        flipped = latent.T
        for g in range(32):
            row = (g % 2) * 256 + (g // 2) * 16
            latt[row : row + 16, pl.ds(start, ROWS)] = flipped[g * 16 : g * 16 + 16, :]
        key_docs = jnp.sum(jnp.where(line == lane, docs[slot, 0:1, :], 0), axis=1, keepdims=True)
        past = jnp.logical_or(slot < 4, line <= lane)
        bias[...] = jnp.where(jnp.logical_and(key_docs == doc_row, past), 0.0, LOW)
        for h in range(HEADS_HERE):
            cols = slice(h * 256, h * 256 + 256)
            key = kv[pl.ds(start, ROWS), h * 128 : h * 128 + 128]
            value = kv[pl.ds(start, ROWS), 512 + h * 128 : 640 + h * 128]
            s = mm(jnp.concatenate([key, rope], axis=1), qx[:, cols], NT) + bias[...]
            top = jnp.max(s, axis=0, keepdims=True)
            p = jnp.exp2((s - top) * (SCALE * LOG2E))
            gp = mm(value, go_ref[:, h * 128 : h * 128 + 128], NT)
            probs[pl.ds(start, ROWS), cols] = p
            gprobs[pl.ds(start, ROWS), cols] = gp
            stats[0, pl.ds(slot, 1), cols] = top
            stats[1, pl.ds(slot, 1), cols] = jnp.sum(p, axis=0, keepdims=True)
            stats[2, pl.ds(slot, 1), cols] = jnp.sum(p * gp, axis=0, keepdims=True)
        return carry

    lax.fori_loop(0, SLOTS, scores, 0)

    tops = stats[0, 0:SLOTS, :]
    factor = jnp.exp2((tops - jnp.max(tops, axis=0, keepdims=True)) * (SCALE * LOG2E))
    total = jnp.sum(stats[1, 0:SLOTS, :] * factor, axis=0, keepdims=True)
    delta = jnp.sum(stats[2, 0:SLOTS, :] * factor, axis=0, keepdims=True) / total
    stats[0, 0:SLOTS, :] = factor / total
    stats[1, 0:1, :] = delta

    up_low = remote(sib_out.at[0], sib_in.at[0], s_sib.at[0], r_sib.at[0], sib)
    up_high = remote(sib_out.at[1], sib_in.at[1], s_sib.at[1], r_sib.at[1], sib)

    def share_of(by):
        return lax.rem(y + by + 8, 8)

    def hop(index, kind, way):
        side = 0 if way > 0 else 1
        by, dest = ((1, 1), (1, 3), (2, 4), (2, 2))[kind]
        rows = pl.ds(0, PACK)
        if kind == 2:
            rows = pl.ds(80, 64) if side else pl.ds(0, 80)
        return remote(
            ys_out.at[index, share_of(way * dest), rows, :], ys_in.at[index, side, kind, rows, :],
            s_ys.at[index, side, kind], r_ys.at[index, side, kind], at_y(way * by),
        )

    def relay(index):
        for way in (1, -1):
            side = 0 if way > 0 else 1
            hop(index, 1, way).wait_recv()
            hop(index, 2, way).wait_recv()
            dest = share_of(2 * way)
            more = ys_out[index, dest].astype(F32) + ys_in[index, side, 1].astype(F32)
            rows = slice(80, 144) if side else slice(0, 80)
            half = more[rows] + ys_in[index, side, 2, rows, :].astype(F32)
            ys_out[index, dest] = more.astype(BF16)
            ys_out[index, dest, rows, :] = half.astype(BF16)
            hop(index, 3, way).start()

    def grads(t, carry):
        slot = jnp.where(
            t == 0, 4 * core, jnp.where(t < 3, 2 * t - 1, jnp.where(t == 3, 2 - 2 * core, 4 - 2 * core))
        )
        start = pl.multiple_of(slot * ROWS, ROWS)
        rope_sum = jnp.zeros((ROWS, 128), F32)
        for h in range(HEADS_HERE):
            cols = slice(h * 256, h * 256 + 256)
            p = probs[pl.ds(start, ROWS), cols] * stats[0, pl.ds(slot, 1), cols]
            ds = (SCALE * p * (gprobs[pl.ds(start, ROWS), cols] - stats[1, 0:1, cols])).astype(BF16)
            dv = mm(p.astype(BF16), go_ref[:, h * 128 : h * 128 + 128])
            dk = mm(ds, qx[:, cols])
            dkv[pl.ds(start, ROWS), h * 128 : h * 128 + 128] = dk[:, :128].astype(BF16)
            dkv[pl.ds(start, ROWS), 512 + h * 128 : 640 + h * 128] = dv.astype(BF16)
            rope_sum = rope_sum + dk[:, 128:]
            key_t = jnp.concatenate(
                [kxt[slot, h * 128 : h * 128 + 128, :], kxt[slot, 512:, :]], axis=0
            )
            dqt[h] += mm(key_t, ds)
        part[:, LAT:] = rope_sum
        both = dkv[pl.ds(start, ROWS), :]
        for n in range(2):
            part[:, n * 256 : n * 256 + 256] = mm(both, ups[n * 256 : n * 256 + 256, :], NT)

        def add(which):
            part[...] += sib_in[which].astype(F32)

        def leave(index):
            for who in range(8):
                ys_out[index, who] = packed(part[who * 32 : who * 32 + 32, :]).astype(BF16)
            ys_own[index] = packed(part[pl.ds(pl.multiple_of(y * 32, 32), 32), :])
            for kind in (2, 1, 0):
                for way in (1, -1):
                    hop(index, kind, way).start()

        @pl.when(t == 0)
        def _():
            leave(0)

        @pl.when(t == 1)
        def _():
            sib_out[0] = part[...].astype(BF16)
            up_low.start()

        @pl.when(t == 2)
        def _():
            sib_out[1] = part[...].astype(BF16)
            up_high.start()

        @pl.when(t == 3)
        def _():
            up_low.wait_recv()
            add(0)
            leave(1)

        @pl.when(t == 4)
        def _():
            up_high.wait_recv()
            add(1)
            leave(2)
            relay(0)

        return carry

    lax.fori_loop(0, SLOTS, grads, 0)

    theirs = pl.multiple_of((1 - core) * 256, 256)
    mine = pl.multiple_of(core * 256, 256)
    to_sib = remote(g_out, g_in, s_g.at[0], r_g.at[0], sib)
    for n in range(4):
        g_out[:, n * 256 : n * 256 + 256] = mm(
            latt[pl.ds(theirs, 256), :], dkv[:, n * 256 : n * 256 + 256]
        ).astype(BF16)
    to_sib.start()
    for n in range(4):
        g_own[:, n * 256 : n * 256 + 256] = mm(
            latt[pl.ds(mine, 256), :], dkv[:, n * 256 : n * 256 + 256]
        )
    relay(1)
    relay(2)

    for h in range(HEADS_HERE):
        dq = dqt[h].T
        dq_ref[:, h * 192 : h * 192 + 192] = dq[:, :192].astype(BF16)
    dq_out = pltpu.make_async_copy(dq_ref, dq_any, s_out.at[0])
    dq_out.start()

    to_sib.wait_recv()
    g_own[...] += g_in[...].astype(F32)
    gx_out[...] = g_own[...].astype(BF16)

    def scatter_x(by):
        there = pl.multiple_of(lax.rem(x + by, 4) * 64, 64)
        return remote(
            gx_out.at[pl.ds(there, 64), :], gx_in.at[by - 1], s_gx.at[by - 1], r_gx.at[by - 1], at_x(by)
        )

    for by in (2, 1, 3):
        scatter_x(by).start()

    def to_owner(index, other):
        slot = index * 2 + other
        part_of = lax.rem(zl + other, 2)
        return remote(
            own_out.at[index, part_of], own_in.at[slot],
            s_own.at[slot], r_own.at[slot], owner(-4 + 2 * index, other),
        )

    def settle(index):
        which = lax.rem(index + 2 * core, 3)
        here = ys_own[index]
        for way in (1, -1):
            for kind in (0, 3):
                hop(index, kind, way).wait_recv()
                here = here + ys_in[index, 0 if way > 0 else 1, kind].astype(F32)
        for half in (0, 1):
            rope = pltpu.roll(here[128:], 64, 1) if half else here[128:]
            tiles = [here[n * 32 + half * 16 : n * 32 + half * 16 + 16] for n in range(4)]
            mine_of = jnp.concatenate(tiles + [rope], axis=0)
            own_out[which, half] = mine_of.astype(BF16)

            @pl.when(which == 2)
            def _():
                own_keep[half] = mine_of

        @pl.when(which < 2)
        def _():
            to_owner(which, 0).start()

        to_owner(which, 1).start()

    for index in range(3):
        settle(index)

    for index in range(3):
        for other in (0, 1):
            if index < 2 or other:
                to_owner(index, other).wait_recv()
    final = own_keep[zl]
    for slot in range(5):
        final = final + own_in[slot if slot < 4 else 5].astype(F32)
    my_rows = pl.ds(pl.multiple_of(dp * 16, 16), 16)
    for n in range(5):
        dlat_ref[my_rows, n * 128 : n * 128 + 128] = final[n * 16 : n * 16 + 16].astype(BF16)

    def to_all(by):
        return remote(
            dlat_ref.at[my_rows, :], dlat_ref.at[my_rows, :], s_ag.at[by - 1], r_ag.at[by - 1], at_dp(by)
        )

    for by in (8, 7, 9, 6, 10, 5, 11, 4, 12, 3, 13, 2, 14, 1, 15):
        to_all(by).start()

    for by in range(1, 4):
        scatter_x(by).wait_recv()
    g_sum = g_own[pl.ds(pl.multiple_of(x * 64, 64), 64), :]
    for by in range(1, 4):
        g_sum = g_sum + gx_in[by - 1].astype(F32)
    g_own[0:64, :] = g_sum
    gz_out[...] = g_sum.astype(BF16)

    def scatter_zh(by):
        there = pl.multiple_of(lax.rem(zh + by, 4) * 16, 16)
        return remote(
            gz_out.at[pl.ds(there, 16), :], gz_in.at[by - 1], s_gz.at[by - 1], r_gz.at[by - 1], at_zh(by)
        )

    for by in (2, 1, 3):
        scatter_zh(by).start()

    for by in range(1, 4):
        scatter_zh(by).wait_recv()
    g_last = g_own[pl.ds(pl.multiple_of(zh * 16, 16), 16), :]
    for by in range(1, 4):
        g_last = g_last + gz_in[by - 1].astype(F32)
    dup_ref[...] = g_last
    dup_out = pltpu.make_async_copy(dup_ref, dup_any, s_out.at[1])
    dup_out.start()

    for by in range(1, 16):
        to_all(by).wait_recv()
    dlat_out = pltpu.make_async_copy(dlat_ref, dlat_any, s_out.at[2])
    dlat_out.start()

    for index in (0, 1):
        for half in (0, 1):
            along_z(index, half).wait_send()
        for j in range(6):
            along_y(index, j).wait_send()
    for by in range(1, 5):
        tell(by).wait_send()
    fw_own.wait_send()
    fw_mid_low.wait_send()
    for index in range(3):
        for kind in range(4):
            for way in (1, -1):
                hop(index, kind, way).wait_send()
    up_low.wait_send()
    up_high.wait_send()
    to_sib.wait_send()
    for by in range(1, 4):
        scatter_x(by).wait_send()
        scatter_zh(by).wait_send()
    for index in range(3):
        for other in (0, 1):
            if index < 2 or other:
                to_owner(index, other).wait_send()
    for by in range(1, 16):
        to_all(by).wait_send()
    dq_out.wait()
    dup_out.wait()
    dlat_out.wait()


def write_out(dq_in, dlat_in, dup_in, dq_ref, dlat_ref, dupk_ref, dupv_ref, dlat, dup, sem):
    copies = [
        pltpu.make_async_copy(src, dst, sem.at[i])
        for i, (src, dst) in enumerate(((dlat_in, dlat), (dup_in, dup), (dq_in, dq_ref)))
    ]
    for copy in copies:
        copy.start()
    copies[0].wait()
    dlat_ref[...] = dlat[...].astype(F32).T[: LAT + ROPE, :]
    copies[1].wait()
    dupk_ref[...] = dup[:, :512]
    dupv_ref[...] = dup[:, 512:]
    copies[2].wait()


def shards(queries, latent, grad_out, doc_ids, up_key, up_value):
    vmem = pl.BlockSpec(memory_space=pltpu.VMEM)
    anywhere = pl.BlockSpec(memory_space=pl.ANY)
    dma = pltpu.SemaphoreType.DMA
    shape = jax.ShapeDtypeStruct
    made = pl.pallas_call(
        kernel,
        out_shape=(shape((ROWS, 768), BF16), shape((ROWS, WIDE), BF16), shape((16, 1024), F32)),
        in_specs=[anywhere] * 6,
        out_specs=(anywhere,) * 3,
        scratch_shapes=[
            pltpu.VMEM((ROWS, 768), BF16),
            pltpu.VMEM((ROWS, WIDE), BF16),
            pltpu.VMEM((16, 1024), F32),
            pltpu.VMEM((ROWS, 768), BF16),
            pltpu.VMEM((LAT + ROPE, ROWS), BF16),
            pltpu.VMEM((ROWS, 512), BF16),
            pltpu.VMEM((SLOTS, 8, ROWS), jnp.int32),
            pltpu.VMEM((SLOTS, 8, PACK, 128), BF16),
            pltpu.VMEM((ROWS, LAT), BF16),
            pltpu.VMEM((ROWS, 128), BF16),
            pltpu.VMEM((ROWS, 1024), BF16),
            pltpu.VMEM((LAT, 1024), BF16),
            pltpu.VMEM((SLOTS * ROWS, 1024), BF16),
            pltpu.VMEM((SLOTS, WIDE, ROWS), BF16),
            pltpu.VMEM((LAT, SLOTS * ROWS), BF16),
            pltpu.VMEM((SLOTS * ROWS, 1024), F32),
            pltpu.VMEM((SLOTS * ROWS, 1024), F32),
            pltpu.VMEM((3, 8, 1024), F32),
            pltpu.VMEM((ROWS, ROWS), F32),
            pltpu.VMEM((HEADS_HERE, 256, ROWS), F32),
            pltpu.VMEM((SLOTS * ROWS, 1024), BF16),
            pltpu.VMEM((ROWS, WIDE), F32),
            pltpu.VMEM((2, ROWS, WIDE), BF16),
            pltpu.VMEM((2, ROWS, WIDE), BF16),
            pltpu.VMEM((3, 8, PACK, 128), BF16),
            pltpu.VMEM((3, PACK, 128), F32),
            pltpu.VMEM((3, 2, 4, PACK, 128), BF16),
            pltpu.VMEM((3, 2, 80, 128), BF16),
            pltpu.VMEM((6, 80, 128), BF16),
            pltpu.VMEM((2, 80, 128), F32),
            pltpu.VMEM((256, 1024), BF16),
            pltpu.VMEM((256, 1024), BF16),
            pltpu.VMEM((256, 1024), F32),
            pltpu.VMEM((256, 1024), BF16),
            pltpu.VMEM((3, 64, 1024), BF16),
            pltpu.VMEM((64, 1024), BF16),
            pltpu.VMEM((3, 16, 1024), BF16),
            dma((6,)),
            dma((3,)),
            dma((4,)), dma((4,)),
            dma((2, 2)), dma((2, 2)),
            dma((2, 6)), dma((2, 6)),
            dma((2,)), dma((2,)),
            dma((2,)), dma((2,)),
            dma((3, 2, 4)), dma((3, 2, 4)),
            dma((6,)), dma((6,)),
            dma((15,)), dma((15,)),
            dma((1,)), dma((1,)),
            dma((3,)), dma((3,)),
            dma((3,)), dma((3,)),
        ],
        compiler_params=pltpu.CompilerParams(
            collective_id=0, has_side_effects=True, vmem_limit_bytes=56 * 1024 * 1024
        ),
        name="mla_backward",
    )(queries, latent.T, grad_out, doc_ids.reshape(1, ROWS), up_key, up_value)
    grad_queries, grad_latent, grad_up_key, grad_up_value = pl.pallas_call(
        write_out,
        out_shape=(
            shape((ROWS, 768), BF16), shape((LAT + ROPE, ROWS), F32),
            shape((16, 512), F32), shape((16, 512), F32),
        ),
        in_specs=[anywhere] * 3,
        out_specs=(vmem,) * 4,
        scratch_shapes=[pltpu.VMEM((ROWS, WIDE), BF16), pltpu.VMEM((16, 1024), F32), dma((3,))],
        compiler_params=pltpu.CompilerParams(vmem_limit_bytes=63 * 1024 * 1024),
        name="write_out",
    )(*made)
    return grad_queries, grad_latent.T, grad_up_key, grad_up_value


def solution(mesh):
    return jax.shard_map(
        shards,
        mesh=mesh,
        in_specs=(P("ctx", "dp"), P("ctx", None), P("ctx", "dp"), P("ctx"), P(None, "dp"), P(None, "dp")),
        out_specs=(P("ctx", "dp"), P("ctx", None), P("ctx", "dp"), P("ctx", "dp")),
        check_vma=False,
    )
```

```python
import functools
import jax
import jax.numpy as jnp
from jax import lax
from jax.experimental import pallas as pl
from jax.experimental.pallas import tpu as pltpu
from jax.sharding import PartitionSpec as P

LAT = 512
ROPE = 64
NOPE = 128
ROWS = 256
HEADS_HERE = 4
WIDE = 640
PACK = 144
HALVES = ((0, 80), (80, 64))
SLOTS = 5
SCALE = (NOPE + ROPE) ** -0.5
LOG2E = 1.4426950408889634
LOW = -1e30
MESH = pl.DeviceIdType.MESH
F32 = jnp.float32
BF16 = jnp.bfloat16
NT = (((1,), (1,)), ((), ()))
NN = (((1,), (0,)), ((), ()))


def mm(a, b, dims=NN):
    return lax.dot_general(a, b, dims, preferred_element_type=F32)


def side_by_side(first, second):
    return first + pltpu.roll(second, 64, 1)


def packed(block):
    tiles = [block[:, n * 128 : n * 128 + 128] for n in range(4)]
    return jnp.concatenate(tiles + [side_by_side(block[:16, LAT:], block[16:, LAT:])], axis=0)


def kernel(
    q_any, lat_any, go_any, doc_any, upk_any, upv_any,
    dq_any, dlat_any, dup_any,
    dq_ref, all_rows, dup_ref, q_ref, lat_ref, go_ref, docs, win, latent_ref, rope_ref, qx, ups, kv, kxt, latt, probs, gprobs, stats, bias, dqt, dkv,
    part, sib_out, sib_in, ys_out, ys_own, ys_in, own_out, own_in, own_keep,
    g_out, g_in, g_own, gx_out, gx_in, gz_out, gz_in,
    s_in, s_out, s_doc, r_doc, s_z, r_z, s_y, r_y, s_fw, r_fw, s_sib, r_sib, s_ys, r_ys,
    s_own, r_own, s_ag, r_ag, s_g, r_g, s_gx, r_gx, s_gz, r_gz,
):
    dp = lax.axis_index("dp")
    ctx = lax.axis_index("ctx")
    y, zl = lax.div(dp, 2), lax.rem(dp, 2)
    x, zh, core = lax.div(ctx, 8), lax.rem(lax.div(ctx, 2), 4), lax.rem(ctx, 2)
    sib = (dp, ctx + 1 - 2 * core)
    mate = dp + 1 - 2 * zl

    def at_ctx(by):
        return lax.rem(ctx + by + 32, 32)

    def at_y(by):
        return (lax.rem(y + by + 8, 8) * 2 + zl, ctx)

    def at_dp(by):
        return (lax.rem(dp + by + 16, 16), ctx)

    def at_x(by):
        return (dp, lax.rem(x + by + 4, 4) * 8 + zh * 2 + core)

    def at_zh(by):
        return (dp, x * 8 + lax.rem(zh + by + 4, 4) * 2 + core)

    def owner(by, other):
        return (mate if other else dp, at_ctx(by))

    barrier = pltpu.get_barrier_semaphore()
    senders = [(mate, at_ctx(-4)), (dp, at_ctx(-2)), sib, (mate, ctx)]
    senders += [at_y(by) for by in (-2, 2, -1, 1)]
    senders += [at_x(-i) for i in range(1, 4)]
    senders += [at_zh(-1), at_zh(1)]
    for sender in senders:
        pl.semaphore_signal(barrier, inc=1, device_id=sender, device_id_type=MESH)

    loads = [
        pltpu.make_async_copy(src, dst, s_in.at[i])
        for i, (src, dst) in enumerate((
            (lat_any, lat_ref), (doc_any, docs.at[4, 0:1, :]), (upk_any, ups.at[:, :512]),
            (upv_any, ups.at[:, 512:]), (q_any, q_ref), (go_any, go_ref),
        ))
    ]
    for load in loads:
        load.start()

    def remote(src, dst, send, recv, to):
        return pltpu.make_async_remote_copy(
            src_ref=src, dst_ref=dst, send_sem=send, recv_sem=recv,
            device_id=to, device_id_type=MESH,
        )

    loads[0].wait()
    loads[1].wait()
    doc_row = docs[4, 0:1, :]
    line = lax.broadcasted_iota(jnp.int32, (ROWS, ROWS), 0)
    lane = lax.broadcasted_iota(jnp.int32, (ROWS, ROWS), 1)
    rows_of = lat_ref[:LAT, :].T
    tail = jnp.concatenate([lat_ref[LAT:, :].astype(F32), jnp.zeros((64, ROWS), F32)], axis=0).T
    for who in range(8):
        for n in range(4):
            win[4, who, n * 32 : n * 32 + 32, :] = rows_of[who * 32 : who * 32 + 32, n * 128 : n * 128 + 128]
        win[4, who, 128:, :] = side_by_side(
            tail[who * 32 : who * 32 + 16, :], tail[who * 32 + 16 : who * 32 + 32, :]
        ).astype(BF16)

    pl.semaphore_wait(barrier, len(senders))

    def shares(slot, who):
        return win.at[slot, who]

    def along_ctx(index):
        return (mate, at_ctx(4)) if index else (dp, at_ctx(2))

    def tell(index):
        return remote(
            docs.at[4], docs.at[2 - 2 * index], s_doc.at[index], r_doc.at[index], along_ctx(index)
        )

    def along_z(index, half):
        who = lax.rem(y + 4 * half, 8)
        return remote(
            shares(4, who), shares(2 - 2 * index, who), s_z.at[index, half], r_z.at[index, half],
            along_ctx(index),
        )

    for index in (0, 1):
        for half in (0, 1):
            along_z(index, half).start()
        tell(index).start()

    class Forward:
        def __init__(self, slot, to, at):
            self.copies = [
                remote(win.at[slot], win.at[to], s_fw.at[at], r_fw.at[at], sib),
                remote(docs.at[slot], docs.at[to], s_fw.at[2 + at], r_fw.at[2 + at], sib),
            ]

        def start(self):
            for copy in self.copies:
                copy.start()

        def wait_recv(self):
            for copy in self.copies:
                copy.wait_recv()

        def wait_send(self):
            for copy in self.copies:
                copy.wait_send()

    fw_own, fw_mid = Forward(4, 3, 0), Forward(2, 3, 0)
    fw_mid_low, fw_far_low = Forward(2, 1, 1), Forward(0, 1, 1)

    @pl.when(core == 0)
    def _():
        fw_own.start()

    passes = ((2, 0, 0), (-2, 0, 0), (1, 0, 0), (-1, 0, 0), (1, 4, 1), (-1, 4, 1))

    def along_y(index, j):
        by, more, _ = passes[j]
        rows = shares(2 - 2 * index, lax.rem(y + more, 8))
        return remote(rows, rows, s_y.at[index, j], r_y.at[index, j], at_y(by))

    for load in loads[2:]:
        load.wait()

    for h in range(HEADS_HERE):
        qx[:, h * 256 : h * 256 + 128] = q_ref[:, h * 192 : h * 192 + 128]
        qx[:, h * 256 + 128 : h * 256 + 256] = jnp.concatenate(
            [q_ref[:, h * 192 + 128 : h * 192 + 192], jnp.zeros((ROWS, 64), BF16)], axis=1
        )
    dqt[...] = jnp.zeros_like(dqt)

    for index in (0, 1):
        for half in (0, 1):
            along_z(index, half).wait_recv()
            for j in range(6):
                if passes[j][2] == half:
                    along_y(index, j).start()
        tell(index).wait_recv()

    def scores(t, carry):
        slot = jnp.where(
            t == 0, 4,
            jnp.where(t == 1, 2 + core, jnp.where(t == 2, 3 - core, jnp.where(t == 3, 0, 1))),
        )

        @pl.when(t == 1 + core)
        def _():
            for j in range(6):
                along_y(0, j).wait_recv()

            @pl.when(core == 0)
            def _():
                fw_mid_low.start()

            @pl.when(core == 1)
            def _():
                fw_mid.start()

        @pl.when(t == 3)
        def _():
            for j in range(6):
                along_y(1, j).wait_recv()

            @pl.when(core == 1)
            def _():
                fw_far_low.start()

        @pl.when(t == 2 - core)
        def _():
            fw_own.wait_recv()

        @pl.when(t == 4)
        def _():
            fw_mid_low.wait_recv()

        start = pl.multiple_of(slot * ROWS, ROWS)
        for who in range(8):
            for n in range(4):
                latent_ref[who * 32 : who * 32 + 32, n * 128 : n * 128 + 128] = win[
                    slot, who, n * 32 : n * 32 + 32, :
                ]
            both_ropes = win[slot, who, 128:, :]
            rope_ref[who * 32 : who * 32 + 16, :] = both_ropes
            rope_ref[who * 32 + 16 : who * 32 + 32, :] = pltpu.roll(
                both_ropes.astype(F32), 64, 1
            ).astype(BF16)
        latent = latent_ref[...]
        rope = rope_ref[...]
        for n in range(4):
            kv[pl.ds(start, ROWS), n * 256 : n * 256 + 256] = mm(
                latent, ups[:, n * 256 : n * 256 + 256]
            ).astype(BF16)
        keys = kv[pl.ds(start, ROWS), :512]
        kxt[slot, :512, :] = keys.T
        kxt[slot, 512:, :] = rope.T
        flipped = latent.T
        for g in range(32):
            row = (g % 2) * 256 + (g // 2) * 16
            latt[row : row + 16, pl.ds(start, ROWS)] = flipped[g * 16 : g * 16 + 16, :]
        key_docs = jnp.sum(jnp.where(line == lane, docs[slot, 0:1, :], 0), axis=1, keepdims=True)
        past = jnp.logical_or(slot < 4, line <= lane)
        bias[...] = jnp.where(jnp.logical_and(key_docs == doc_row, past), 0.0, LOW)
        for h in range(HEADS_HERE):
            cols = slice(h * 256, h * 256 + 256)
            key = kv[pl.ds(start, ROWS), h * 128 : h * 128 + 128]
            value = kv[pl.ds(start, ROWS), 512 + h * 128 : 640 + h * 128]
            s = mm(jnp.concatenate([key, rope], axis=1), qx[:, cols], NT) + bias[...]
            top = jnp.max(s, axis=0, keepdims=True)
            p = jnp.exp2((s - top) * (SCALE * LOG2E))
            gp = mm(value, go_ref[:, h * 128 : h * 128 + 128], NT)
            probs[pl.ds(start, ROWS), cols] = p
            gprobs[pl.ds(start, ROWS), cols] = gp
            stats[0, pl.ds(slot, 1), cols] = top
            stats[1, pl.ds(slot, 1), cols] = jnp.sum(p, axis=0, keepdims=True)
            stats[2, pl.ds(slot, 1), cols] = jnp.sum(p * gp, axis=0, keepdims=True)
        return carry

    lax.fori_loop(0, SLOTS, scores, 0)

    tops = stats[0, 0:SLOTS, :]
    factor = jnp.exp2((tops - jnp.max(tops, axis=0, keepdims=True)) * (SCALE * LOG2E))
    total = jnp.sum(stats[1, 0:SLOTS, :] * factor, axis=0, keepdims=True)
    delta = jnp.sum(stats[2, 0:SLOTS, :] * factor, axis=0, keepdims=True) / total
    stats[0, 0:SLOTS, :] = factor / total
    stats[1, 0:1, :] = delta

    up_low = remote(sib_out.at[0], sib_in.at[0], s_sib.at[0], r_sib.at[0], sib)
    up_high = remote(sib_out.at[1], sib_in.at[1], s_sib.at[1], r_sib.at[1], sib)

    def share_of(by):
        return lax.rem(y + by + 8, 8)

    def hop(index, kind, way):
        side = 0 if way > 0 else 1
        by, dest = ((1, 1), (1, 3), (2, 4), (2, 2))[kind]
        rows = pl.ds(0, PACK)
        if kind == 2:
            rows = pl.ds(80, 64) if side else pl.ds(0, 80)
        return remote(
            ys_out.at[index, share_of(way * dest), rows, :], ys_in.at[index, side, kind, rows, :],
            s_ys.at[index, side, kind], r_ys.at[index, side, kind], at_y(way * by),
        )

    def relay(index):
        for way in (1, -1):
            side = 0 if way > 0 else 1
            hop(index, 1, way).wait_recv()
            hop(index, 2, way).wait_recv()
            dest = share_of(2 * way)
            more = ys_out[index, dest].astype(F32) + ys_in[index, side, 1].astype(F32)
            rows = slice(80, 144) if side else slice(0, 80)
            half = more[rows] + ys_in[index, side, 2, rows, :].astype(F32)
            ys_out[index, dest] = more.astype(BF16)
            ys_out[index, dest, rows, :] = half.astype(BF16)
            hop(index, 3, way).start()

    def grads(t, carry):
        slot = jnp.where(
            t == 0, 4 * core, jnp.where(t < 3, 2 * t - 1, jnp.where(t == 3, 2 - 2 * core, 4 - 2 * core))
        )
        start = pl.multiple_of(slot * ROWS, ROWS)
        rope_sum = jnp.zeros((ROWS, 128), F32)
        for h in range(HEADS_HERE):
            cols = slice(h * 256, h * 256 + 256)
            p = probs[pl.ds(start, ROWS), cols] * stats[0, pl.ds(slot, 1), cols]
            ds = (SCALE * p * (gprobs[pl.ds(start, ROWS), cols] - stats[1, 0:1, cols])).astype(BF16)
            dv = mm(p.astype(BF16), go_ref[:, h * 128 : h * 128 + 128])
            dk = mm(ds, qx[:, cols])
            dkv[pl.ds(start, ROWS), h * 128 : h * 128 + 128] = dk[:, :128].astype(BF16)
            dkv[pl.ds(start, ROWS), 512 + h * 128 : 640 + h * 128] = dv.astype(BF16)
            rope_sum = rope_sum + dk[:, 128:]
            key_t = jnp.concatenate(
                [kxt[slot, h * 128 : h * 128 + 128, :], kxt[slot, 512:, :]], axis=0
            )
            dqt[h] += mm(key_t, ds)
        part[:, LAT:] = rope_sum
        both = dkv[pl.ds(start, ROWS), :]
        for n in range(2):
            part[:, n * 256 : n * 256 + 256] = mm(both, ups[n * 256 : n * 256 + 256, :], NT)

        def add(which):
            part[...] += sib_in[which].astype(F32)

        def leave(index):
            for who in range(8):
                ys_out[index, who] = packed(part[who * 32 : who * 32 + 32, :]).astype(BF16)
            ys_own[index] = packed(part[pl.ds(pl.multiple_of(y * 32, 32), 32), :])
            for kind in (2, 1, 0):
                for way in (1, -1):
                    hop(index, kind, way).start()

        @pl.when(t == 0)
        def _():
            leave(0)

        @pl.when(t == 1)
        def _():
            sib_out[0] = part[...].astype(BF16)
            up_low.start()

        @pl.when(t == 2)
        def _():
            sib_out[1] = part[...].astype(BF16)
            up_high.start()

        @pl.when(t == 3)
        def _():
            up_low.wait_recv()
            add(0)
            leave(1)

        @pl.when(t == 4)
        def _():
            up_high.wait_recv()
            add(1)
            leave(2)
            relay(0)

        return carry

    lax.fori_loop(0, SLOTS, grads, 0)

    theirs = pl.multiple_of((1 - core) * 256, 256)
    mine = pl.multiple_of(core * 256, 256)
    to_sib = remote(g_out, g_in, s_g.at[0], r_g.at[0], sib)
    for n in range(4):
        g_out[:, n * 256 : n * 256 + 256] = mm(
            latt[pl.ds(theirs, 256), :], dkv[:, n * 256 : n * 256 + 256]
        ).astype(BF16)
    to_sib.start()
    for n in range(4):
        g_own[:, n * 256 : n * 256 + 256] = mm(
            latt[pl.ds(mine, 256), :], dkv[:, n * 256 : n * 256 + 256]
        )
    relay(1)
    relay(2)

    for h in range(HEADS_HERE):
        dq = dqt[h].T
        dq_ref[:, h * 192 : h * 192 + 192] = dq[:, :192].astype(BF16)
    dq_out = pltpu.make_async_copy(dq_ref, dq_any, s_out.at[0])
    dq_out.start()

    to_sib.wait_recv()
    g_own[...] += g_in[...].astype(F32)
    gx_out[...] = g_own[...].astype(BF16)

    def scatter_x(by):
        there = pl.multiple_of(lax.rem(x + by, 4) * 64, 64)
        return remote(
            gx_out.at[pl.ds(there, 64), :], gx_in.at[by - 1], s_gx.at[by - 1], r_gx.at[by - 1], at_x(by)
        )

    for by in (2, 1, 3):
        scatter_x(by).start()

    def to_owner(index, other, half):
        slot, rows = index * 2 + other, pl.ds(*HALVES[half])
        return remote(
            own_out.at[index, rows, :], own_in.at[slot, rows, :],
            s_own.at[slot], r_own.at[slot], owner(-4 + 2 * index, other),
        )

    def by_side(act):
        for mine_is in (0, 1):
            pl.when(zl == mine_is)(functools.partial(act, mine_is))

    def settle(index):
        which = lax.rem(index + 2 * core, 3)
        here = ys_own[index]
        for way in (1, -1):
            for kind in (0, 3):
                hop(index, kind, way).wait_recv()
                here = here + ys_in[index, 0 if way > 0 else 1, kind].astype(F32)
        own_out[which] = here.astype(BF16)

        @pl.when(which == 2)
        def _():
            own_keep[...] = here

        @pl.when(which < 2)
        def _():
            by_side(lambda side: to_owner(which, 0, side).start())

        by_side(lambda side: to_owner(which, 1, 1 - side).start())

    for index in range(3):
        settle(index)

    pairs = [(index, other) for index in range(3) for other in (0, 1) if index < 2 or other]

    def to_all(by, half):
        mine_rows = all_rows.at[y, pl.ds(*HALVES[half]), :]
        return remote(mine_rows, mine_rows, s_ag.at[by - 1], r_ag.at[by - 1], at_dp(by))

    def gather(side):
        first, count = HALVES[side]
        rows = slice(first, first + count)
        for index, other in pairs:
            to_owner(index, other, side).wait_recv()
        final = own_keep[rows]
        for index, other in pairs:
            final = final + own_in[index * 2 + other, rows, :].astype(F32)
        all_rows[y, rows, :] = final.astype(BF16)
        for by in (8, 7, 9, 6, 10, 5, 11, 4, 12, 3, 13, 2, 14, 1, 15):
            to_all(by, side).start()

    by_side(gather)

    for by in range(1, 4):
        scatter_x(by).wait_recv()
    g_sum = g_own[pl.ds(pl.multiple_of(x * 64, 64), 64), :]
    for by in range(1, 4):
        g_sum = g_sum + gx_in[by - 1].astype(F32)
    g_own[0:64, :] = g_sum
    gz_out[...] = g_sum.astype(BF16)

    def scatter_zh(by):
        there = pl.multiple_of(lax.rem(zh + by, 4) * 16, 16)
        return remote(
            gz_out.at[pl.ds(there, 16), :], gz_in.at[by - 1], s_gz.at[by - 1], r_gz.at[by - 1], at_zh(by)
        )

    for by in (2, 1, 3):
        scatter_zh(by).start()

    for by in range(1, 4):
        scatter_zh(by).wait_recv()
    g_last = g_own[pl.ds(pl.multiple_of(zh * 16, 16), 16), :]
    for by in range(1, 4):
        g_last = g_last + gz_in[by - 1].astype(F32)
    dup_ref[...] = g_last
    dup_out = pltpu.make_async_copy(dup_ref, dup_any, s_out.at[1])
    dup_out.start()

    def gathered(side):
        for by in range(1, 16):
            to_all(by, (side + by) % 2).wait_recv()

    by_side(gathered)
    dlat_out = pltpu.make_async_copy(all_rows, dlat_any, s_out.at[2])
    dlat_out.start()

    for index in (0, 1):
        for half in (0, 1):
            along_z(index, half).wait_send()
        for j in range(6):
            along_y(index, j).wait_send()
    for index in (0, 1):
        tell(index).wait_send()
    fw_own.wait_send()
    fw_mid_low.wait_send()
    for index in range(3):
        for kind in range(4):
            for way in (1, -1):
                hop(index, kind, way).wait_send()
    up_low.wait_send()
    up_high.wait_send()
    to_sib.wait_send()
    for by in range(1, 4):
        scatter_x(by).wait_send()
        scatter_zh(by).wait_send()

    def left(side):
        for index, other in pairs:
            to_owner(index, other, (side + other) % 2).wait_send()
        for by in range(1, 16):
            to_all(by, side).wait_send()

    by_side(left)
    dq_out.wait()
    dup_out.wait()
    dlat_out.wait()


def write_out(dq_in, dlat_in, dup_in, dq_ref, dlat_ref, dupk_ref, dupv_ref, dlat, dup, wide, sem):
    copies = [
        pltpu.make_async_copy(src, dst, sem.at[i])
        for i, (src, dst) in enumerate(((dlat_in, dlat), (dup_in, dup), (dq_in, dq_ref)))
    ]
    for copy in copies:
        copy.start()
    copies[0].wait()
    for who in range(8):
        block = dlat[who].astype(F32)
        for n in range(4):
            wide[who * 32 : who * 32 + 32, n * 128 : n * 128 + 128] = block[n * 32 : n * 32 + 32]
        wide[who * 32 : who * 32 + 16, LAT:] = block[128:]
        wide[who * 32 + 16 : who * 32 + 32, LAT:] = pltpu.roll(block[128:], 64, 1)
    dlat_ref[...] = wide[...].T[: LAT + ROPE, :]
    copies[1].wait()
    dupk_ref[...] = dup[:, :512]
    dupv_ref[...] = dup[:, 512:]
    copies[2].wait()


def shards(queries, latent, grad_out, doc_ids, up_key, up_value):
    vmem = pl.BlockSpec(memory_space=pltpu.VMEM)
    anywhere = pl.BlockSpec(memory_space=pl.ANY)
    dma = pltpu.SemaphoreType.DMA
    shape = jax.ShapeDtypeStruct
    made = pl.pallas_call(
        kernel,
        out_shape=(shape((ROWS, 768), BF16), shape((8, PACK, 128), BF16), shape((16, 1024), F32)),
        in_specs=[anywhere] * 6,
        out_specs=(anywhere,) * 3,
        scratch_shapes=[
            pltpu.VMEM((ROWS, 768), BF16),
            pltpu.VMEM((8, PACK, 128), BF16),
            pltpu.VMEM((16, 1024), F32),
            pltpu.VMEM((ROWS, 768), BF16),
            pltpu.VMEM((LAT + ROPE, ROWS), BF16),
            pltpu.VMEM((ROWS, 512), BF16),
            pltpu.VMEM((SLOTS, 8, ROWS), jnp.int32),
            pltpu.VMEM((SLOTS, 8, PACK, 128), BF16),
            pltpu.VMEM((ROWS, LAT), BF16),
            pltpu.VMEM((ROWS, 128), BF16),
            pltpu.VMEM((ROWS, 1024), BF16),
            pltpu.VMEM((LAT, 1024), BF16),
            pltpu.VMEM((SLOTS * ROWS, 1024), BF16),
            pltpu.VMEM((SLOTS, WIDE, ROWS), BF16),
            pltpu.VMEM((LAT, SLOTS * ROWS), BF16),
            pltpu.VMEM((SLOTS * ROWS, 1024), F32),
            pltpu.VMEM((SLOTS * ROWS, 1024), F32),
            pltpu.VMEM((3, 8, 1024), F32),
            pltpu.VMEM((ROWS, ROWS), F32),
            pltpu.VMEM((HEADS_HERE, 256, ROWS), F32),
            pltpu.VMEM((SLOTS * ROWS, 1024), BF16),
            pltpu.VMEM((ROWS, WIDE), F32),
            pltpu.VMEM((2, ROWS, WIDE), BF16),
            pltpu.VMEM((2, ROWS, WIDE), BF16),
            pltpu.VMEM((3, 8, PACK, 128), BF16),
            pltpu.VMEM((3, PACK, 128), F32),
            pltpu.VMEM((3, 2, 4, PACK, 128), BF16),
            pltpu.VMEM((3, PACK, 128), BF16),
            pltpu.VMEM((6, PACK, 128), BF16),
            pltpu.VMEM((PACK, 128), F32),
            pltpu.VMEM((256, 1024), BF16),
            pltpu.VMEM((256, 1024), BF16),
            pltpu.VMEM((256, 1024), F32),
            pltpu.VMEM((256, 1024), BF16),
            pltpu.VMEM((3, 64, 1024), BF16),
            pltpu.VMEM((64, 1024), BF16),
            pltpu.VMEM((3, 16, 1024), BF16),
            dma((6,)),
            dma((3,)),
            dma((2,)), dma((2,)),
            dma((2, 2)), dma((2, 2)),
            dma((2, 6)), dma((2, 6)),
            dma((4,)), dma((4,)),
            dma((2,)), dma((2,)),
            dma((3, 2, 4)), dma((3, 2, 4)),
            dma((6,)), dma((6,)),
            dma((15,)), dma((15,)),
            dma((1,)), dma((1,)),
            dma((3,)), dma((3,)),
            dma((3,)), dma((3,)),
        ],
        compiler_params=pltpu.CompilerParams(
            collective_id=0, has_side_effects=True, vmem_limit_bytes=56 * 1024 * 1024
        ),
        name="mla_backward",
    )(queries, latent.T, grad_out, doc_ids.reshape(1, ROWS), up_key, up_value)
    grad_queries, grad_latent, grad_up_key, grad_up_value = pl.pallas_call(
        write_out,
        out_shape=(
            shape((ROWS, 768), BF16), shape((LAT + ROPE, ROWS), F32),
            shape((16, 512), F32), shape((16, 512), F32),
        ),
        in_specs=[anywhere] * 3,
        out_specs=(vmem,) * 4,
        scratch_shapes=[
            pltpu.VMEM((8, PACK, 128), BF16), pltpu.VMEM((16, 1024), F32),
            pltpu.VMEM((ROWS, WIDE), F32), dma((3,)),
        ],
        compiler_params=pltpu.CompilerParams(vmem_limit_bytes=63 * 1024 * 1024),
        name="write_out",
    )(*made)
    return grad_queries, grad_latent.T, grad_up_key, grad_up_value


def solution(mesh):
    return jax.shard_map(
        shards,
        mesh=mesh,
        in_specs=(P("ctx", "dp"), P("ctx", None), P("ctx", "dp"), P("ctx"), P(None, "dp"), P(None, "dp")),
        out_specs=(P("ctx", "dp"), P("ctx", None), P("ctx", "dp"), P("ctx", "dp")),
        check_vma=False,
    )
```

```python
import functools
import jax
import jax.numpy as jnp
from jax import lax
from jax.experimental import pallas as pl
from jax.experimental.pallas import tpu as pltpu
from jax.sharding import PartitionSpec as P

LAT = 512
ROPE = 64
NOPE = 128
ROWS = 256
HEADS_HERE = 4
WIDE = 640
PACK = 144
HALVES = ((0, 80), (80, 64))
SLOTS = 5
SCALE = (NOPE + ROPE) ** -0.5
LOG2E = 1.4426950408889634
LOW = -1e30
MESH = pl.DeviceIdType.MESH
F32 = jnp.float32
BF16 = jnp.bfloat16
NT = (((1,), (1,)), ((), ()))
NN = (((1,), (0,)), ((), ()))


def mm(a, b, dims=NN):
    return lax.dot_general(a, b, dims, preferred_element_type=F32)


def side_by_side(first, second):
    return first + pltpu.roll(second, 64, 1)


def packed(block):
    tiles = [block[:, n * 128 : n * 128 + 128] for n in range(4)]
    return jnp.concatenate(tiles + [side_by_side(block[:16, LAT:], block[16:, LAT:])], axis=0)


def kernel(
    q_any, lat_any, go_any, doc_any, upk_any, upv_any,
    dq_any, dlat_any, dup_any,
    dq_ref, all_rows, dup_ref, q_ref, lat_ref, go_ref, docs, win, latent_ref, rope_ref, qx, ups, kv, kxt, latt, probs, gprobs, stats, bias, dqt, dkv,
    part, sib_out, sib_in, ys_out, ys_own, ys_in, own_out, own_in, own_keep,
    g_out, g_in, g_own, gx_out, gx_in, gz_out, gz_in,
    s_in, s_out, s_doc, r_doc, s_z, r_z, s_y, r_y, s_fw, r_fw, s_sib, r_sib, s_ys, r_ys,
    s_own, r_own, s_ag, r_ag, s_g, r_g, s_gx, r_gx, s_gz, r_gz,
):
    dp = lax.axis_index("dp")
    ctx = lax.axis_index("ctx")
    y, zl = lax.div(dp, 2), lax.rem(dp, 2)
    x, zh, core = lax.div(ctx, 8), lax.rem(lax.div(ctx, 2), 4), lax.rem(ctx, 2)
    sib = (dp, ctx + 1 - 2 * core)
    mate = dp + 1 - 2 * zl

    def at_ctx(by):
        return lax.rem(ctx + by + 32, 32)

    def at_y(by):
        return (lax.rem(y + by + 8, 8) * 2 + zl, ctx)

    def at_dp(by):
        return (lax.rem(dp + by + 16, 16), ctx)

    def at_x(by):
        return (dp, lax.rem(x + by + 4, 4) * 8 + zh * 2 + core)

    def at_zh(by):
        return (dp, x * 8 + lax.rem(zh + by + 4, 4) * 2 + core)

    def owner(by, other):
        return (mate if other else dp, at_ctx(by))

    barrier = pltpu.get_barrier_semaphore()
    senders = [(mate, at_ctx(-4)), (dp, at_ctx(-2)), sib, (mate, ctx)]
    senders += [at_y(by) for by in (-2, 2, -1, 1)]
    senders += [at_x(-i) for i in range(1, 4)]
    senders += [at_zh(-1), at_zh(1)]
    for sender in senders:
        pl.semaphore_signal(barrier, inc=1, device_id=sender, device_id_type=MESH)

    loads = [
        pltpu.make_async_copy(src, dst, s_in.at[i])
        for i, (src, dst) in enumerate((
            (lat_any, lat_ref), (doc_any, docs.at[4, 0:1, :]), (upk_any, ups.at[:, :512]),
            (upv_any, ups.at[:, 512:]), (q_any, q_ref), (go_any, go_ref),
        ))
    ]
    for load in loads:
        load.start()

    def remote(src, dst, send, recv, to):
        return pltpu.make_async_remote_copy(
            src_ref=src, dst_ref=dst, send_sem=send, recv_sem=recv,
            device_id=to, device_id_type=MESH,
        )

    loads[0].wait()
    loads[1].wait()
    doc_row = docs[4, 0:1, :]
    line = lax.broadcasted_iota(jnp.int32, (ROWS, ROWS), 0)
    lane = lax.broadcasted_iota(jnp.int32, (ROWS, ROWS), 1)
    rows_of = lat_ref[:LAT, :].T
    tail = jnp.concatenate([lat_ref[LAT:, :].astype(F32), jnp.zeros((64, ROWS), F32)], axis=0).T
    for who in range(8):
        for n in range(4):
            win[4, who, n * 32 : n * 32 + 32, :] = rows_of[who * 32 : who * 32 + 32, n * 128 : n * 128 + 128]
        win[4, who, 128:, :] = side_by_side(
            tail[who * 32 : who * 32 + 16, :], tail[who * 32 + 16 : who * 32 + 32, :]
        ).astype(BF16)

    pl.semaphore_wait(barrier, len(senders))

    def shares(slot, who):
        return win.at[slot, who]

    def along_ctx(index):
        return (mate, at_ctx(4)) if index else (dp, at_ctx(2))

    def tell(index):
        return remote(
            docs.at[4], docs.at[2 - 2 * index], s_doc.at[index], r_doc.at[index], along_ctx(index)
        )

    def along_z(index, half):
        who = lax.rem(y + 4 * half, 8)
        return remote(
            shares(4, who), shares(2 - 2 * index, who), s_z.at[index, half], r_z.at[index, half],
            along_ctx(index),
        )

    for index in (0, 1):
        for half in (0, 1):
            along_z(index, half).start()
        tell(index).start()

    class Forward:
        def __init__(self, slot, to, at):
            self.copies = [
                remote(win.at[slot], win.at[to], s_fw.at[at], r_fw.at[at], sib),
                remote(docs.at[slot], docs.at[to], s_fw.at[2 + at], r_fw.at[2 + at], sib),
            ]

        def start(self):
            for copy in self.copies:
                copy.start()

        def wait_recv(self):
            for copy in self.copies:
                copy.wait_recv()

        def wait_send(self):
            for copy in self.copies:
                copy.wait_send()

    fw_own, fw_mid = Forward(4, 3, 0), Forward(2, 3, 0)
    fw_mid_low = Forward(2, 1, 1)

    def fw_far(who):
        remote(win.at[0, who], win.at[1, who], s_fw.at[1], r_fw.at[1], sib).start()


    @pl.when(core == 0)
    def _():
        fw_own.start()

    passes = ((2, 0, 0), (-2, 0, 0), (1, 0, 0), (-1, 0, 0), (1, 4, 1), (-1, 4, 1))

    def along_y(index, j):
        by, more, _ = passes[j]
        rows = shares(2 - 2 * index, lax.rem(y + more, 8))
        return remote(rows, rows, s_y.at[index, j], r_y.at[index, j], at_y(by))

    for load in loads[2:]:
        load.wait()

    for h in range(HEADS_HERE):
        qx[:, h * 256 : h * 256 + 128] = q_ref[:, h * 192 : h * 192 + 128]
        qx[:, h * 256 + 128 : h * 256 + 256] = jnp.concatenate(
            [q_ref[:, h * 192 + 128 : h * 192 + 192], jnp.zeros((ROWS, 64), BF16)], axis=1
        )
    dqt[...] = jnp.zeros_like(dqt)

    for index in (0, 1):
        for half in (0, 1):
            along_z(index, half).wait_recv()
            for j in range(6):
                if passes[j][2] == half:
                    along_y(index, j).start()
        tell(index).wait_recv()

    @pl.when(core == 1)
    def _():
        for half in (0, 1):
            fw_far(lax.rem(y + 4 * half, 8))
        remote(docs.at[0], docs.at[1], s_fw.at[3], r_fw.at[3], sib).start()

    def scores(t, carry):
        slot = jnp.where(
            t == 0, 4,
            jnp.where(t == 1, 2 + core, jnp.where(t == 2, 3 - core, jnp.where(t == 3, 0, 1))),
        )

        @pl.when(t == 1 + core)
        def _():
            for j in range(6):
                along_y(0, j).wait_recv()

            @pl.when(core == 0)
            def _():
                fw_mid_low.start()

            @pl.when(core == 1)
            def _():
                fw_mid.start()

        @pl.when(t == 3)
        def _():
            for j in (4, 5, 2, 3, 0, 1):
                along_y(1, j).wait_recv()
                by, more, _ = passes[j]

                @pl.when(core == 1)
                def _():
                    fw_far(lax.rem(y - by + more + 8, 8))

        @pl.when(t == 2 - core)
        def _():
            fw_own.wait_recv()

        @pl.when(t == 4)
        def _():
            fw_mid_low.wait_recv()

        start = pl.multiple_of(slot * ROWS, ROWS)
        for who in range(8):
            for n in range(4):
                latent_ref[who * 32 : who * 32 + 32, n * 128 : n * 128 + 128] = win[
                    slot, who, n * 32 : n * 32 + 32, :
                ]
            both_ropes = win[slot, who, 128:, :]
            rope_ref[who * 32 : who * 32 + 16, :] = both_ropes
            rope_ref[who * 32 + 16 : who * 32 + 32, :] = pltpu.roll(
                both_ropes.astype(F32), 64, 1
            ).astype(BF16)
        latent = latent_ref[...]
        rope = rope_ref[...]
        for n in range(4):
            kv[pl.ds(start, ROWS), n * 256 : n * 256 + 256] = mm(
                latent, ups[:, n * 256 : n * 256 + 256]
            ).astype(BF16)
        keys = kv[pl.ds(start, ROWS), :512]
        kxt[slot, :512, :] = keys.T
        kxt[slot, 512:, :] = rope.T
        flipped = latent.T
        for g in range(32):
            row = (g % 2) * 256 + (g // 2) * 16
            latt[row : row + 16, pl.ds(start, ROWS)] = flipped[g * 16 : g * 16 + 16, :]
        key_docs = jnp.sum(jnp.where(line == lane, docs[slot, 0:1, :], 0), axis=1, keepdims=True)
        past = jnp.logical_or(slot < 4, line <= lane)
        bias[...] = jnp.where(jnp.logical_and(key_docs == doc_row, past), 0.0, LOW)
        for h in range(HEADS_HERE):
            cols = slice(h * 256, h * 256 + 256)
            key = kv[pl.ds(start, ROWS), h * 128 : h * 128 + 128]
            value = kv[pl.ds(start, ROWS), 512 + h * 128 : 640 + h * 128]
            s = mm(jnp.concatenate([key, rope], axis=1), qx[:, cols], NT) + bias[...]
            top = jnp.max(s, axis=0, keepdims=True)
            p = jnp.exp2((s - top) * (SCALE * LOG2E))
            gp = mm(value, go_ref[:, h * 128 : h * 128 + 128], NT)
            probs[pl.ds(start, ROWS), cols] = p
            gprobs[pl.ds(start, ROWS), cols] = gp
            stats[0, pl.ds(slot, 1), cols] = top
            stats[1, pl.ds(slot, 1), cols] = jnp.sum(p, axis=0, keepdims=True)
            stats[2, pl.ds(slot, 1), cols] = jnp.sum(p * gp, axis=0, keepdims=True)
        return carry

    lax.fori_loop(0, SLOTS, scores, 0)

    tops = stats[0, 0:SLOTS, :]
    factor = jnp.exp2((tops - jnp.max(tops, axis=0, keepdims=True)) * (SCALE * LOG2E))
    total = jnp.sum(stats[1, 0:SLOTS, :] * factor, axis=0, keepdims=True)
    delta = jnp.sum(stats[2, 0:SLOTS, :] * factor, axis=0, keepdims=True) / total
    stats[0, 0:SLOTS, :] = factor / total
    stats[1, 0:1, :] = delta

    up_low = remote(sib_out.at[0], sib_in.at[0], s_sib.at[0], r_sib.at[0], sib)
    up_high = remote(sib_out.at[1], sib_in.at[1], s_sib.at[1], r_sib.at[1], sib)

    def share_of(by):
        return lax.rem(y + by + 8, 8)

    def hop(index, kind, way):
        side = 0 if way > 0 else 1
        by, dest = ((1, 1), (1, 3), (2, 4), (2, 2))[kind]
        rows = pl.ds(0, PACK)
        if kind == 2:
            rows = pl.ds(80, 64) if side else pl.ds(0, 80)
        return remote(
            ys_out.at[index, share_of(way * dest), rows, :], ys_in.at[index, side, kind, rows, :],
            s_ys.at[index, side, kind], r_ys.at[index, side, kind], at_y(way * by),
        )

    def relay(index):
        for way in (1, -1):
            side = 0 if way > 0 else 1
            hop(index, 1, way).wait_recv()
            hop(index, 2, way).wait_recv()
            dest = share_of(2 * way)
            more = ys_out[index, dest].astype(F32) + ys_in[index, side, 1].astype(F32)
            rows = slice(80, 144) if side else slice(0, 80)
            half = more[rows] + ys_in[index, side, 2, rows, :].astype(F32)
            ys_out[index, dest] = more.astype(BF16)
            ys_out[index, dest, rows, :] = half.astype(BF16)
            hop(index, 3, way).start()

    def grads(t, carry):
        slot = jnp.where(
            t == 0, 4 * core, jnp.where(t < 3, 2 * t - 1, jnp.where(t == 3, 2 - 2 * core, 4 - 2 * core))
        )
        start = pl.multiple_of(slot * ROWS, ROWS)
        rope_sum = jnp.zeros((ROWS, 128), F32)
        for h in range(HEADS_HERE):
            cols = slice(h * 256, h * 256 + 256)
            p = probs[pl.ds(start, ROWS), cols] * stats[0, pl.ds(slot, 1), cols]
            ds = (SCALE * p * (gprobs[pl.ds(start, ROWS), cols] - stats[1, 0:1, cols])).astype(BF16)
            dv = mm(p.astype(BF16), go_ref[:, h * 128 : h * 128 + 128])
            dk = mm(ds, qx[:, cols])
            dkv[pl.ds(start, ROWS), h * 128 : h * 128 + 128] = dk[:, :128].astype(BF16)
            dkv[pl.ds(start, ROWS), 512 + h * 128 : 640 + h * 128] = dv.astype(BF16)
            rope_sum = rope_sum + dk[:, 128:]
            key_t = jnp.concatenate(
                [kxt[slot, h * 128 : h * 128 + 128, :], kxt[slot, 512:, :]], axis=0
            )
            dqt[h] += mm(key_t, ds)
        part[:, LAT:] = rope_sum
        both = dkv[pl.ds(start, ROWS), :]
        for n in range(2):
            part[:, n * 256 : n * 256 + 256] = mm(both, ups[n * 256 : n * 256 + 256, :], NT)

        def add(which):
            part[...] += sib_in[which].astype(F32)

        def leave(index):
            for who in range(8):
                ys_out[index, who] = packed(part[who * 32 : who * 32 + 32, :]).astype(BF16)
            ys_own[index] = packed(part[pl.ds(pl.multiple_of(y * 32, 32), 32), :])
            for kind in (2, 1, 0):
                for way in (1, -1):
                    hop(index, kind, way).start()

        @pl.when(t == 0)
        def _():
            leave(0)

        @pl.when(t == 1)
        def _():
            sib_out[0] = part[...].astype(BF16)
            up_low.start()

        @pl.when(t == 2)
        def _():
            sib_out[1] = part[...].astype(BF16)
            up_high.start()

        @pl.when(t == 3)
        def _():
            up_low.wait_recv()
            add(0)
            leave(1)

        @pl.when(t == 4)
        def _():
            up_high.wait_recv()
            add(1)
            leave(2)
            relay(0)

        return carry

    lax.fori_loop(0, SLOTS, grads, 0)

    theirs = pl.multiple_of((1 - core) * 256, 256)
    mine = pl.multiple_of(core * 256, 256)
    to_sib = remote(g_out, g_in, s_g.at[0], r_g.at[0], sib)
    for n in range(4):
        g_out[:, n * 256 : n * 256 + 256] = mm(
            latt[pl.ds(theirs, 256), :], dkv[:, n * 256 : n * 256 + 256]
        ).astype(BF16)
    to_sib.start()
    for n in range(4):
        g_own[:, n * 256 : n * 256 + 256] = mm(
            latt[pl.ds(mine, 256), :], dkv[:, n * 256 : n * 256 + 256]
        )
    def to_owner(index, other, half):
        slot, rows = index * 2 + other, pl.ds(*HALVES[half])
        return remote(
            own_out.at[index, rows, :], own_in.at[slot, rows, :],
            s_own.at[slot], r_own.at[slot], owner(-4 + 2 * index, other),
        )

    def by_side(act):
        for mine_is in (0, 1):
            pl.when(zl == mine_is)(functools.partial(act, mine_is))

    def settle(index):
        which = lax.rem(index + 2 * core, 3)
        here = ys_own[index]
        for way in (1, -1):
            for kind in (0, 3):
                hop(index, kind, way).wait_recv()
                here = here + ys_in[index, 0 if way > 0 else 1, kind].astype(F32)
        own_out[which] = here.astype(BF16)

        @pl.when(which == 2)
        def _():
            own_keep[...] = here

        @pl.when(which < 2)
        def _():
            by_side(lambda side: to_owner(which, 0, side).start())

        by_side(lambda side: to_owner(which, 1, 1 - side).start())

    relay(1)
    relay(2)
    settle(0)

    for h in range(HEADS_HERE):
        dq = dqt[h].T
        dq_ref[:, h * 192 : h * 192 + 192] = dq[:, :192].astype(BF16)
    dq_out = pltpu.make_async_copy(dq_ref, dq_any, s_out.at[0])
    dq_out.start()
    settle(1)

    to_sib.wait_recv()
    g_own[...] += g_in[...].astype(F32)
    gx_out[...] = g_own[...].astype(BF16)

    def scatter_x(by):
        there = pl.multiple_of(lax.rem(x + by, 4) * 64, 64)
        return remote(
            gx_out.at[pl.ds(there, 64), :], gx_in.at[by - 1], s_gx.at[by - 1], r_gx.at[by - 1], at_x(by)
        )

    for by in (2, 1, 3):
        scatter_x(by).start()

    settle(2)

    pairs = [(index, other) for index in range(3) for other in (0, 1) if index < 2 or other]

    def to_all(by, half):
        mine_rows = all_rows.at[y, pl.ds(*HALVES[half]), :]
        return remote(mine_rows, mine_rows, s_ag.at[by - 1], r_ag.at[by - 1], at_dp(by))

    def gather(side):
        first, count = HALVES[side]
        rows = slice(first, first + count)
        for index, other in pairs:
            to_owner(index, other, side).wait_recv()
        final = own_keep[rows]
        for index, other in pairs:
            final = final + own_in[index * 2 + other, rows, :].astype(F32)
        all_rows[y, rows, :] = final.astype(BF16)
        for by in (8, 7 + 2 * side, 6, 10, 5, 11, 4, 12, 3, 13, 2, 14, 1, 15):
            to_all(by, side).start()

    by_side(gather)

    def pass_on(side):
        to_all(8, side).wait_recv()
        piece = all_rows.at[lax.rem(y + 4, 8), pl.ds(*HALVES[side]), :]
        at = 8 - 2 * side
        remote(piece, piece, s_ag.at[at], r_ag.at[at], (mate, ctx)).start()


    for by in range(1, 4):
        scatter_x(by).wait_recv()
    g_sum = g_own[pl.ds(pl.multiple_of(x * 64, 64), 64), :]
    for by in range(1, 4):
        g_sum = g_sum + gx_in[by - 1].astype(F32)
    g_own[0:64, :] = g_sum
    gz_out[...] = g_sum.astype(BF16)

    def scatter_zh(by):
        there = pl.multiple_of(lax.rem(zh + by, 4) * 16, 16)
        return remote(
            gz_out.at[pl.ds(there, 16), :], gz_in.at[by - 1], s_gz.at[by - 1], r_gz.at[by - 1], at_zh(by)
        )

    for by in (2, 1, 3):
        scatter_zh(by).start()
    by_side(pass_on)

    for by in range(1, 4):
        scatter_zh(by).wait_recv()
    g_last = g_own[pl.ds(pl.multiple_of(zh * 16, 16), 16), :]
    for by in range(1, 4):
        g_last = g_last + gz_in[by - 1].astype(F32)
    dup_ref[...] = g_last
    dup_out = pltpu.make_async_copy(dup_ref, dup_any, s_out.at[1])
    dup_out.start()

    def gathered(side):
        for by in range(1, 16):
            if by != 8:
                to_all(by, (side + by) % 2).wait_recv()

    by_side(gathered)
    dlat_out = pltpu.make_async_copy(all_rows, dlat_any, s_out.at[2])
    dlat_out.start()

    for index in (0, 1):
        for half in (0, 1):
            along_z(index, half).wait_send()
        for j in range(6):
            along_y(index, j).wait_send()
    for index in (0, 1):
        tell(index).wait_send()
    fw_own.wait_send()
    fw_mid_low.wait_send()
    for index in range(3):
        for kind in range(4):
            for way in (1, -1):
                hop(index, kind, way).wait_send()
    up_low.wait_send()
    up_high.wait_send()
    to_sib.wait_send()
    for by in range(1, 4):
        scatter_x(by).wait_send()
        scatter_zh(by).wait_send()

    def left(side):
        for index, other in pairs:
            to_owner(index, other, (side + other) % 2).wait_send()
        for by in range(1, 16):
            to_all(by, side).wait_send()

    by_side(left)
    dq_out.wait()
    dup_out.wait()
    dlat_out.wait()


def write_out(dq_in, dlat_in, dup_in, dq_ref, dlat_ref, dupk_ref, dupv_ref, dlat, dup, wide, sem):
    copies = [
        pltpu.make_async_copy(src, dst, sem.at[i])
        for i, (src, dst) in enumerate(((dlat_in, dlat), (dup_in, dup), (dq_in, dq_ref)))
    ]
    for copy in copies:
        copy.start()
    copies[0].wait()
    for who in range(8):
        block = dlat[who].astype(F32)
        for n in range(4):
            wide[who * 32 : who * 32 + 32, n * 128 : n * 128 + 128] = block[n * 32 : n * 32 + 32]
        wide[who * 32 : who * 32 + 16, LAT:] = block[128:]
        wide[who * 32 + 16 : who * 32 + 32, LAT:] = pltpu.roll(block[128:], 64, 1)
    dlat_ref[...] = wide[...].T[: LAT + ROPE, :]
    copies[1].wait()
    dupk_ref[...] = dup[:, :512]
    dupv_ref[...] = dup[:, 512:]
    copies[2].wait()


def shards(queries, latent, grad_out, doc_ids, up_key, up_value):
    vmem = pl.BlockSpec(memory_space=pltpu.VMEM)
    anywhere = pl.BlockSpec(memory_space=pl.ANY)
    dma = pltpu.SemaphoreType.DMA
    shape = jax.ShapeDtypeStruct
    made = pl.pallas_call(
        kernel,
        out_shape=(shape((ROWS, 768), BF16), shape((8, PACK, 128), BF16), shape((16, 1024), F32)),
        in_specs=[anywhere] * 6,
        out_specs=(anywhere,) * 3,
        scratch_shapes=[
            pltpu.VMEM((ROWS, 768), BF16),
            pltpu.VMEM((8, PACK, 128), BF16),
            pltpu.VMEM((16, 1024), F32),
            pltpu.VMEM((ROWS, 768), BF16),
            pltpu.VMEM((LAT + ROPE, ROWS), BF16),
            pltpu.VMEM((ROWS, 512), BF16),
            pltpu.VMEM((SLOTS, 8, ROWS), jnp.int32),
            pltpu.VMEM((SLOTS, 8, PACK, 128), BF16),
            pltpu.VMEM((ROWS, LAT), BF16),
            pltpu.VMEM((ROWS, 128), BF16),
            pltpu.VMEM((ROWS, 1024), BF16),
            pltpu.VMEM((LAT, 1024), BF16),
            pltpu.VMEM((SLOTS * ROWS, 1024), BF16),
            pltpu.VMEM((SLOTS, WIDE, ROWS), BF16),
            pltpu.VMEM((LAT, SLOTS * ROWS), BF16),
            pltpu.VMEM((SLOTS * ROWS, 1024), F32),
            pltpu.VMEM((SLOTS * ROWS, 1024), F32),
            pltpu.VMEM((3, 8, 1024), F32),
            pltpu.VMEM((ROWS, ROWS), F32),
            pltpu.VMEM((HEADS_HERE, 256, ROWS), F32),
            pltpu.VMEM((SLOTS * ROWS, 1024), BF16),
            pltpu.VMEM((ROWS, WIDE), F32),
            pltpu.VMEM((2, ROWS, WIDE), BF16),
            pltpu.VMEM((2, ROWS, WIDE), BF16),
            pltpu.VMEM((3, 8, PACK, 128), BF16),
            pltpu.VMEM((3, PACK, 128), F32),
            pltpu.VMEM((3, 2, 4, PACK, 128), BF16),
            pltpu.VMEM((3, PACK, 128), BF16),
            pltpu.VMEM((6, PACK, 128), BF16),
            pltpu.VMEM((PACK, 128), F32),
            pltpu.VMEM((256, 1024), BF16),
            pltpu.VMEM((256, 1024), BF16),
            pltpu.VMEM((256, 1024), F32),
            pltpu.VMEM((256, 1024), BF16),
            pltpu.VMEM((3, 64, 1024), BF16),
            pltpu.VMEM((64, 1024), BF16),
            pltpu.VMEM((3, 16, 1024), BF16),
            dma((6,)),
            dma((3,)),
            dma((2,)), dma((2,)),
            dma((2, 2)), dma((2, 2)),
            dma((2, 6)), dma((2, 6)),
            dma((4,)), dma((4,)),
            dma((2,)), dma((2,)),
            dma((3, 2, 4)), dma((3, 2, 4)),
            dma((6,)), dma((6,)),
            dma((15,)), dma((15,)),
            dma((1,)), dma((1,)),
            dma((3,)), dma((3,)),
            dma((3,)), dma((3,)),
        ],
        compiler_params=pltpu.CompilerParams(
            collective_id=0, has_side_effects=True, vmem_limit_bytes=56 * 1024 * 1024
        ),
        name="mla_backward",
    )(queries, latent.T, grad_out, doc_ids.reshape(1, ROWS), up_key, up_value)
    grad_queries, grad_latent, grad_up_key, grad_up_value = pl.pallas_call(
        write_out,
        out_shape=(
            shape((ROWS, 768), BF16), shape((LAT + ROPE, ROWS), F32),
            shape((16, 512), F32), shape((16, 512), F32),
        ),
        in_specs=[anywhere] * 3,
        out_specs=(vmem,) * 4,
        scratch_shapes=[
            pltpu.VMEM((8, PACK, 128), BF16), pltpu.VMEM((16, 1024), F32),
            pltpu.VMEM((ROWS, WIDE), F32), dma((3,)),
        ],
        compiler_params=pltpu.CompilerParams(vmem_limit_bytes=63 * 1024 * 1024),
        name="write_out",
    )(*made)
    return grad_queries, grad_latent.T, grad_up_key, grad_up_value


def solution(mesh):
    return jax.shard_map(
        shards,
        mesh=mesh,
        in_specs=(P("ctx", "dp"), P("ctx", None), P("ctx", "dp"), P("ctx"), P(None, "dp"), P(None, "dp")),
        out_specs=(P("ctx", "dp"), P("ctx", None), P("ctx", "dp"), P("ctx", "dp")),
        check_vma=False,
    )
```

```python
import functools
import jax
import jax.numpy as jnp
from jax import lax
from jax.experimental import pallas as pl
from jax.experimental.pallas import tpu as pltpu
from jax.sharding import PartitionSpec as P

LAT = 512
ROPE = 64
NOPE = 128
ROWS = 256
HEADS_HERE = 4
WIDE = 640
PACK = 144
HALVES = ((0, 80), (80, 64))
PASSED_ON = (2, 6, 3, 5, 4)
SLOTS = 5
SCALE = (NOPE + ROPE) ** -0.5
LOG2E = 1.4426950408889634
LOW = -1e30
MESH = pl.DeviceIdType.MESH
F32 = jnp.float32
BF16 = jnp.bfloat16
NT = (((1,), (1,)), ((), ()))
NN = (((1,), (0,)), ((), ()))


def mm(a, b, dims=NN):
    return lax.dot_general(a, b, dims, preferred_element_type=F32)


def side_by_side(first, second):
    return first + pltpu.roll(second, 64, 1)


def packed(block):
    tiles = [block[:, n * 128 : n * 128 + 128] for n in range(4)]
    return jnp.concatenate(tiles + [side_by_side(block[:16, LAT:], block[16:, LAT:])], axis=0)


def kernel(
    q_any, lat_any, go_any, doc_any, upk_any, upv_any,
    dq_any, dlat_any, dup_any,
    dq_ref, all_rows, dup_ref, q_ref, lat_ref, go_ref, docs, win, latent_ref, rope_ref, qx, ups, kv, kxt, latt, probs, gprobs, stats, bias, dqt, dkv,
    part, sib_out, sib_in, ys_out, ys_own, ys_in, own_out, own_in, own_keep,
    g_out, g_in, g_own, gx_out, gx_in, gz_out, gz_in,
    s_in, s_out, s_doc, r_doc, s_z, r_z, s_y, r_y, s_fw, r_fw, s_sib, r_sib, s_ys, r_ys,
    s_own, r_own, s_ag, r_ag, s_g, r_g, s_gx, r_gx, s_gz, r_gz,
):
    dp = lax.axis_index("dp")
    ctx = lax.axis_index("ctx")
    y, zl = lax.div(dp, 2), lax.rem(dp, 2)
    x, zh, core = lax.div(ctx, 8), lax.rem(lax.div(ctx, 2), 4), lax.rem(ctx, 2)
    sib = (dp, ctx + 1 - 2 * core)
    mate = dp + 1 - 2 * zl

    def at_ctx(by):
        return lax.rem(ctx + by + 32, 32)

    def at_y(by):
        return (lax.rem(y + by + 8, 8) * 2 + zl, ctx)

    def at_dp(by):
        return (lax.rem(dp + by + 16, 16), ctx)

    def at_x(by):
        return (dp, lax.rem(x + by + 4, 4) * 8 + zh * 2 + core)

    def at_zh(by):
        return (dp, x * 8 + lax.rem(zh + by + 4, 4) * 2 + core)

    def owner(by, other):
        return (mate if other else dp, at_ctx(by))

    barrier = pltpu.get_barrier_semaphore()
    senders = [(mate, at_ctx(-4)), (dp, at_ctx(-2)), sib, (mate, ctx)]
    senders += [at_y(by) for by in (-2, 2, -1, 1)]
    senders += [at_x(-i) for i in range(1, 4)]
    senders += [at_zh(-1), at_zh(1)]
    for sender in senders:
        pl.semaphore_signal(barrier, inc=1, device_id=sender, device_id_type=MESH)

    loads = [
        pltpu.make_async_copy(src, dst, s_in.at[i])
        for i, (src, dst) in enumerate((
            (lat_any, lat_ref), (doc_any, docs.at[4, 0:1, :]), (upk_any, ups.at[:, :512]),
            (upv_any, ups.at[:, 512:]), (q_any, q_ref), (go_any, go_ref),
        ))
    ]
    for load in loads:
        load.start()

    def remote(src, dst, send, recv, to):
        return pltpu.make_async_remote_copy(
            src_ref=src, dst_ref=dst, send_sem=send, recv_sem=recv,
            device_id=to, device_id_type=MESH,
        )

    loads[0].wait()
    loads[1].wait()
    doc_row = docs[4, 0:1, :]
    line = lax.broadcasted_iota(jnp.int32, (ROWS, ROWS), 0)
    lane = lax.broadcasted_iota(jnp.int32, (ROWS, ROWS), 1)
    rows_of = lat_ref[:LAT, :].T
    tail = jnp.concatenate([lat_ref[LAT:, :].astype(F32), jnp.zeros((64, ROWS), F32)], axis=0).T
    for who in range(8):
        for n in range(4):
            win[4, who, n * 32 : n * 32 + 32, :] = rows_of[who * 32 : who * 32 + 32, n * 128 : n * 128 + 128]
        win[4, who, 128:, :] = side_by_side(
            tail[who * 32 : who * 32 + 16, :], tail[who * 32 + 16 : who * 32 + 32, :]
        ).astype(BF16)

    pl.semaphore_wait(barrier, len(senders))

    def shares(slot, who):
        return win.at[slot, who]

    def along_ctx(index):
        return (mate, at_ctx(4)) if index else (dp, at_ctx(2))

    def tell(index):
        return remote(
            docs.at[4], docs.at[2 - 2 * index], s_doc.at[index], r_doc.at[index], along_ctx(index)
        )

    def along_z(index, half):
        who = lax.rem(y + 4 * half, 8)
        return remote(
            shares(4, who), shares(2 - 2 * index, who), s_z.at[index, half], r_z.at[index, half],
            along_ctx(index),
        )

    for index in (0, 1):
        for half in (0, 1):
            along_z(index, half).start()
        tell(index).start()

    class Forward:
        def __init__(self, slot, to, at):
            self.copies = [
                remote(win.at[slot], win.at[to], s_fw.at[at], r_fw.at[at], sib),
                remote(docs.at[slot], docs.at[to], s_fw.at[2 + at], r_fw.at[2 + at], sib),
            ]

        def start(self):
            for copy in self.copies:
                copy.start()

        def wait_recv(self):
            for copy in self.copies:
                copy.wait_recv()

        def wait_send(self):
            for copy in self.copies:
                copy.wait_send()

    fw_own, fw_mid = Forward(4, 3, 0), Forward(2, 3, 0)
    fw_mid_low = Forward(2, 1, 1)

    def fw_far(who):
        remote(win.at[0, who], win.at[1, who], s_fw.at[1], r_fw.at[1], sib).start()


    @pl.when(core == 0)
    def _():
        fw_own.start()

    passes = ((2, 0, 0), (-2, 0, 0), (1, 0, 0), (-1, 0, 0), (1, 4, 1), (-1, 4, 1))

    def along_y(index, j):
        by, more, _ = passes[j]
        rows = shares(2 - 2 * index, lax.rem(y + more, 8))
        return remote(rows, rows, s_y.at[index, j], r_y.at[index, j], at_y(by))

    for load in loads[2:]:
        load.wait()

    for h in range(HEADS_HERE):
        qx[:, h * 256 : h * 256 + 128] = q_ref[:, h * 192 : h * 192 + 128]
        qx[:, h * 256 + 128 : h * 256 + 256] = jnp.concatenate(
            [q_ref[:, h * 192 + 128 : h * 192 + 192], jnp.zeros((ROWS, 64), BF16)], axis=1
        )
    dqt[...] = jnp.zeros_like(dqt)

    for index in (0, 1):
        for half in (0, 1):
            along_z(index, half).wait_recv()
            for j in range(6):
                if passes[j][2] == half:
                    along_y(index, j).start()
        tell(index).wait_recv()

    @pl.when(core == 1)
    def _():
        for half in (0, 1):
            fw_far(lax.rem(y + 4 * half, 8))
        remote(docs.at[0], docs.at[1], s_fw.at[3], r_fw.at[3], sib).start()

    def scores(t, carry):
        slot = jnp.where(
            t == 0, 4,
            jnp.where(t == 1, 2 + core, jnp.where(t == 2, 3 - core, jnp.where(t == 3, 0, 1))),
        )

        @pl.when(t == 1 + core)
        def _():
            for j in range(6):
                along_y(0, j).wait_recv()

            @pl.when(core == 0)
            def _():
                fw_mid_low.start()

            @pl.when(core == 1)
            def _():
                fw_mid.start()

        @pl.when(t == 3)
        def _():
            for j in (4, 5, 2, 3, 0, 1):
                along_y(1, j).wait_recv()
                by, more, _ = passes[j]

                @pl.when(core == 1)
                def _():
                    fw_far(lax.rem(y - by + more + 8, 8))

        @pl.when(t == 2 - core)
        def _():
            fw_own.wait_recv()

        @pl.when(t == 4)
        def _():
            fw_mid_low.wait_recv()

        start = pl.multiple_of(slot * ROWS, ROWS)
        for who in range(8):
            for n in range(4):
                latent_ref[who * 32 : who * 32 + 32, n * 128 : n * 128 + 128] = win[
                    slot, who, n * 32 : n * 32 + 32, :
                ]
            both_ropes = win[slot, who, 128:, :]
            rope_ref[who * 32 : who * 32 + 16, :] = both_ropes
            rope_ref[who * 32 + 16 : who * 32 + 32, :] = pltpu.roll(
                both_ropes.astype(F32), 64, 1
            ).astype(BF16)
        latent = latent_ref[...]
        rope = rope_ref[...]
        for n in range(4):
            kv[pl.ds(start, ROWS), n * 256 : n * 256 + 256] = mm(
                latent, ups[:, n * 256 : n * 256 + 256]
            ).astype(BF16)
        keys = kv[pl.ds(start, ROWS), :512]
        kxt[slot, :512, :] = keys.T
        kxt[slot, 512:, :] = rope.T
        flipped = latent.T
        for g in range(32):
            row = (g % 2) * 256 + (g // 2) * 16
            latt[row : row + 16, pl.ds(start, ROWS)] = flipped[g * 16 : g * 16 + 16, :]
        key_docs = jnp.sum(jnp.where(line == lane, docs[slot, 0:1, :], 0), axis=1, keepdims=True)
        past = jnp.logical_or(slot < 4, line <= lane)
        bias[...] = jnp.where(jnp.logical_and(key_docs == doc_row, past), 0.0, LOW)
        for h in range(HEADS_HERE):
            cols = slice(h * 256, h * 256 + 256)
            key = kv[pl.ds(start, ROWS), h * 128 : h * 128 + 128]
            value = kv[pl.ds(start, ROWS), 512 + h * 128 : 640 + h * 128]
            s = mm(jnp.concatenate([key, rope], axis=1), qx[:, cols], NT) + bias[...]
            top = jnp.max(s, axis=0, keepdims=True)
            p = jnp.exp2((s - top) * (SCALE * LOG2E))
            gp = mm(value, go_ref[:, h * 128 : h * 128 + 128], NT)
            probs[pl.ds(start, ROWS), cols] = p
            gprobs[pl.ds(start, ROWS), cols] = gp
            stats[0, pl.ds(slot, 1), cols] = top
            stats[1, pl.ds(slot, 1), cols] = jnp.sum(p, axis=0, keepdims=True)
            stats[2, pl.ds(slot, 1), cols] = jnp.sum(p * gp, axis=0, keepdims=True)
        return carry

    lax.fori_loop(0, SLOTS, scores, 0)

    tops = stats[0, 0:SLOTS, :]
    factor = jnp.exp2((tops - jnp.max(tops, axis=0, keepdims=True)) * (SCALE * LOG2E))
    total = jnp.sum(stats[1, 0:SLOTS, :] * factor, axis=0, keepdims=True)
    delta = jnp.sum(stats[2, 0:SLOTS, :] * factor, axis=0, keepdims=True) / total
    stats[0, 0:SLOTS, :] = factor / total
    stats[1, 0:1, :] = delta

    up_low = remote(sib_out.at[0], sib_in.at[0], s_sib.at[0], r_sib.at[0], sib)
    up_high = remote(sib_out.at[1], sib_in.at[1], s_sib.at[1], r_sib.at[1], sib)

    def share_of(by):
        return lax.rem(y + by + 8, 8)

    def hop(index, kind, way):
        side = 0 if way > 0 else 1
        by, dest = ((1, 1), (1, 3), (2, 4), (2, 2))[kind]
        rows = pl.ds(0, PACK)
        if kind == 2:
            rows = pl.ds(80, 64) if side else pl.ds(0, 80)
        return remote(
            ys_out.at[index, share_of(way * dest), rows, :], ys_in.at[index, side, kind, rows, :],
            s_ys.at[index, side, kind], r_ys.at[index, side, kind], at_y(way * by),
        )

    def relay(index):
        for way in (1, -1):
            side = 0 if way > 0 else 1
            hop(index, 1, way).wait_recv()
            hop(index, 2, way).wait_recv()
            dest = share_of(2 * way)
            more = ys_out[index, dest].astype(F32) + ys_in[index, side, 1].astype(F32)
            rows = slice(80, 144) if side else slice(0, 80)
            half = more[rows] + ys_in[index, side, 2, rows, :].astype(F32)
            ys_out[index, dest] = more.astype(BF16)
            ys_out[index, dest, rows, :] = half.astype(BF16)
            hop(index, 3, way).start()

    def grads(t, carry):
        slot = jnp.where(
            t == 0, 4 * core, jnp.where(t < 3, 2 * t - 1, jnp.where(t == 3, 2 - 2 * core, 4 - 2 * core))
        )
        start = pl.multiple_of(slot * ROWS, ROWS)
        rope_sum = jnp.zeros((ROWS, 128), F32)
        for h in range(HEADS_HERE):
            cols = slice(h * 256, h * 256 + 256)
            p = probs[pl.ds(start, ROWS), cols] * stats[0, pl.ds(slot, 1), cols]
            ds = (SCALE * p * (gprobs[pl.ds(start, ROWS), cols] - stats[1, 0:1, cols])).astype(BF16)
            dv = mm(p.astype(BF16), go_ref[:, h * 128 : h * 128 + 128])
            dk = mm(ds, qx[:, cols])
            dkv[pl.ds(start, ROWS), h * 128 : h * 128 + 128] = dk[:, :128].astype(BF16)
            dkv[pl.ds(start, ROWS), 512 + h * 128 : 640 + h * 128] = dv.astype(BF16)
            rope_sum = rope_sum + dk[:, 128:]
            key_t = jnp.concatenate(
                [kxt[slot, h * 128 : h * 128 + 128, :], kxt[slot, 512:, :]], axis=0
            )
            dqt[h] += mm(key_t, ds)
        part[:, LAT:] = rope_sum
        both = dkv[pl.ds(start, ROWS), :]
        for n in range(2):
            part[:, n * 256 : n * 256 + 256] = mm(both, ups[n * 256 : n * 256 + 256, :], NT)

        def add(which):
            part[...] += sib_in[which].astype(F32)

        def leave(index):
            for who in range(8):
                ys_out[index, who] = packed(part[who * 32 : who * 32 + 32, :]).astype(BF16)
            ys_own[index] = packed(part[pl.ds(pl.multiple_of(y * 32, 32), 32), :])
            for kind in (2, 1, 0):
                for way in (1, -1):
                    hop(index, kind, way).start()

        @pl.when(t == 0)
        def _():
            leave(0)

        @pl.when(t == 1)
        def _():
            sib_out[0] = part[...].astype(BF16)
            up_low.start()

        @pl.when(t == 2)
        def _():
            sib_out[1] = part[...].astype(BF16)
            up_high.start()

        @pl.when(t == 3)
        def _():
            up_low.wait_recv()
            add(0)
            leave(1)

        @pl.when(t == 4)
        def _():
            up_high.wait_recv()
            add(1)
            leave(2)
            relay(0)

        return carry

    lax.fori_loop(0, SLOTS, grads, 0)

    theirs = pl.multiple_of((1 - core) * 256, 256)
    mine = pl.multiple_of(core * 256, 256)
    to_sib = remote(g_out, g_in, s_g.at[0], r_g.at[0], sib)
    for n in range(4):
        g_out[:, n * 256 : n * 256 + 256] = mm(
            latt[pl.ds(theirs, 256), :], dkv[:, n * 256 : n * 256 + 256]
        ).astype(BF16)
    to_sib.start()
    for n in range(4):
        g_own[:, n * 256 : n * 256 + 256] = mm(
            latt[pl.ds(mine, 256), :], dkv[:, n * 256 : n * 256 + 256]
        )
    def to_owner(index, other, half):
        slot, rows = index * 2 + other, pl.ds(*HALVES[half])
        return remote(
            own_out.at[index, rows, :], own_in.at[slot, rows, :],
            s_own.at[slot], r_own.at[slot], owner(-4 + 2 * index, other),
        )

    def by_side(act):
        for mine_is in (0, 1):
            pl.when(zl == mine_is)(functools.partial(act, mine_is))

    def settle(index):
        which = lax.rem(index + 2 * core, 3)
        here = ys_own[index]
        for way in (1, -1):
            for kind in (0, 3):
                hop(index, kind, way).wait_recv()
                here = here + ys_in[index, 0 if way > 0 else 1, kind].astype(F32)
        own_out[which] = here.astype(BF16)

        @pl.when(which == 2)
        def _():
            own_keep[...] = here

        @pl.when(which < 2)
        def _():
            by_side(lambda side: to_owner(which, 0, side).start())

        by_side(lambda side: to_owner(which, 1, 1 - side).start())

    relay(1)
    relay(2)
    settle(0)

    for h in range(HEADS_HERE):
        dq = dqt[h].T
        dq_ref[:, h * 192 : h * 192 + 192] = dq[:, :192].astype(BF16)
    dq_out = pltpu.make_async_copy(dq_ref, dq_any, s_out.at[0])
    dq_out.start()
    settle(1)

    to_sib.wait_recv()
    g_own[...] += g_in[...].astype(F32)
    gx_out[...] = g_own[...].astype(BF16)

    def scatter_x(by):
        there = pl.multiple_of(lax.rem(x + by, 4) * 64, 64)
        return remote(
            gx_out.at[pl.ds(there, 64), :], gx_in.at[by - 1], s_gx.at[by - 1], r_gx.at[by - 1], at_x(by)
        )

    for by in (2, 1, 3):
        scatter_x(by).start()

    settle(2)

    pairs = [(index, other) for index in range(3) for other in (0, 1) if index < 2 or other]

    def to_all(by, half):
        mine_rows = all_rows.at[y, pl.ds(*HALVES[half]), :]
        return remote(mine_rows, mine_rows, s_ag.at[by - 1], r_ag.at[by - 1], at_dp(by))

    def other_zl(away, side):
        return (2 * away + 1 - 2 * side) % 16

    def gather(side):
        first, count = HALVES[side]
        rows = slice(first, first + count)
        for index, other in pairs:
            to_owner(index, other, side).wait_recv()
        final = own_keep[rows]
        for index, other in pairs:
            final = final + own_in[index * 2 + other, rows, :].astype(F32)
        all_rows[y, rows, :] = final.astype(BF16)
        for away in (4, 3, 5, 2, 6, 1, 7):
            to_all(2 * away, side).start()
            if away not in PASSED_ON:
                to_all(other_zl(away, side), side).start()
        to_all(other_zl(0, side), side).start()

    by_side(gather)

    def pass_on(side):
        for away in PASSED_ON:
            to_all(2 * away, side).wait_recv()
            piece = all_rows.at[lax.rem(y + 8 - away, 8), pl.ds(*HALVES[side]), :]
            at = other_zl(away, side) - 1
            remote(piece, piece, s_ag.at[at], r_ag.at[at], (mate, ctx)).start()


    for by in range(1, 4):
        scatter_x(by).wait_recv()
    g_sum = g_own[pl.ds(pl.multiple_of(x * 64, 64), 64), :]
    for by in range(1, 4):
        g_sum = g_sum + gx_in[by - 1].astype(F32)
    g_own[0:64, :] = g_sum
    gz_out[...] = g_sum.astype(BF16)

    def scatter_zh(by):
        there = pl.multiple_of(lax.rem(zh + by, 4) * 16, 16)
        return remote(
            gz_out.at[pl.ds(there, 16), :], gz_in.at[by - 1], s_gz.at[by - 1], r_gz.at[by - 1], at_zh(by)
        )

    for by in (2, 1, 3):
        scatter_zh(by).start()
    by_side(pass_on)

    for by in range(1, 4):
        scatter_zh(by).wait_recv()
    g_last = g_own[pl.ds(pl.multiple_of(zh * 16, 16), 16), :]
    for by in range(1, 4):
        g_last = g_last + gz_in[by - 1].astype(F32)
    dup_ref[...] = g_last
    dup_out = pltpu.make_async_copy(dup_ref, dup_any, s_out.at[1])
    dup_out.start()

    def gathered(side):
        for by in range(1, 16):
            if by % 2 or by // 2 not in PASSED_ON:
                to_all(by, (side + by) % 2).wait_recv()

    by_side(gathered)
    dlat_out = pltpu.make_async_copy(all_rows, dlat_any, s_out.at[2])
    dlat_out.start()

    for index in (0, 1):
        for half in (0, 1):
            along_z(index, half).wait_send()
        for j in range(6):
            along_y(index, j).wait_send()
    for index in (0, 1):
        tell(index).wait_send()
    fw_own.wait_send()
    fw_mid_low.wait_send()
    for index in range(3):
        for kind in range(4):
            for way in (1, -1):
                hop(index, kind, way).wait_send()
    up_low.wait_send()
    up_high.wait_send()
    to_sib.wait_send()
    for by in range(1, 4):
        scatter_x(by).wait_send()
        scatter_zh(by).wait_send()

    def left(side):
        for index, other in pairs:
            to_owner(index, other, (side + other) % 2).wait_send()
        for by in range(1, 16):
            to_all(by, side).wait_send()

    by_side(left)
    dq_out.wait()
    dup_out.wait()
    dlat_out.wait()


def write_out(dq_in, dlat_in, dup_in, dq_ref, dlat_ref, dupk_ref, dupv_ref, dlat, dup, wide, sem):
    copies = [
        pltpu.make_async_copy(src, dst, sem.at[i])
        for i, (src, dst) in enumerate(((dlat_in, dlat), (dup_in, dup), (dq_in, dq_ref)))
    ]
    for copy in copies:
        copy.start()
    copies[0].wait()
    for who in range(8):
        block = dlat[who].astype(F32)
        for n in range(4):
            wide[who * 32 : who * 32 + 32, n * 128 : n * 128 + 128] = block[n * 32 : n * 32 + 32]
        wide[who * 32 : who * 32 + 16, LAT:] = block[128:]
        wide[who * 32 + 16 : who * 32 + 32, LAT:] = pltpu.roll(block[128:], 64, 1)
    dlat_ref[...] = wide[...].T[: LAT + ROPE, :]
    copies[1].wait()
    dupk_ref[...] = dup[:, :512]
    dupv_ref[...] = dup[:, 512:]
    copies[2].wait()


def shards(queries, latent, grad_out, doc_ids, up_key, up_value):
    vmem = pl.BlockSpec(memory_space=pltpu.VMEM)
    anywhere = pl.BlockSpec(memory_space=pl.ANY)
    dma = pltpu.SemaphoreType.DMA
    shape = jax.ShapeDtypeStruct
    made = pl.pallas_call(
        kernel,
        out_shape=(shape((ROWS, 768), BF16), shape((8, PACK, 128), BF16), shape((16, 1024), F32)),
        in_specs=[anywhere] * 6,
        out_specs=(anywhere,) * 3,
        scratch_shapes=[
            pltpu.VMEM((ROWS, 768), BF16),
            pltpu.VMEM((8, PACK, 128), BF16),
            pltpu.VMEM((16, 1024), F32),
            pltpu.VMEM((ROWS, 768), BF16),
            pltpu.VMEM((LAT + ROPE, ROWS), BF16),
            pltpu.VMEM((ROWS, 512), BF16),
            pltpu.VMEM((SLOTS, 8, ROWS), jnp.int32),
            pltpu.VMEM((SLOTS, 8, PACK, 128), BF16),
            pltpu.VMEM((ROWS, LAT), BF16),
            pltpu.VMEM((ROWS, 128), BF16),
            pltpu.VMEM((ROWS, 1024), BF16),
            pltpu.VMEM((LAT, 1024), BF16),
            pltpu.VMEM((SLOTS * ROWS, 1024), BF16),
            pltpu.VMEM((SLOTS, WIDE, ROWS), BF16),
            pltpu.VMEM((LAT, SLOTS * ROWS), BF16),
            pltpu.VMEM((SLOTS * ROWS, 1024), F32),
            pltpu.VMEM((SLOTS * ROWS, 1024), F32),
            pltpu.VMEM((3, 8, 1024), F32),
            pltpu.VMEM((ROWS, ROWS), F32),
            pltpu.VMEM((HEADS_HERE, 256, ROWS), F32),
            pltpu.VMEM((SLOTS * ROWS, 1024), BF16),
            pltpu.VMEM((ROWS, WIDE), F32),
            pltpu.VMEM((2, ROWS, WIDE), BF16),
            pltpu.VMEM((2, ROWS, WIDE), BF16),
            pltpu.VMEM((3, 8, PACK, 128), BF16),
            pltpu.VMEM((3, PACK, 128), F32),
            pltpu.VMEM((3, 2, 4, PACK, 128), BF16),
            pltpu.VMEM((3, PACK, 128), BF16),
            pltpu.VMEM((6, PACK, 128), BF16),
            pltpu.VMEM((PACK, 128), F32),
            pltpu.VMEM((256, 1024), BF16),
            pltpu.VMEM((256, 1024), BF16),
            pltpu.VMEM((256, 1024), F32),
            pltpu.VMEM((256, 1024), BF16),
            pltpu.VMEM((3, 64, 1024), BF16),
            pltpu.VMEM((64, 1024), BF16),
            pltpu.VMEM((3, 16, 1024), BF16),
            dma((6,)),
            dma((3,)),
            dma((2,)), dma((2,)),
            dma((2, 2)), dma((2, 2)),
            dma((2, 6)), dma((2, 6)),
            dma((4,)), dma((4,)),
            dma((2,)), dma((2,)),
            dma((3, 2, 4)), dma((3, 2, 4)),
            dma((6,)), dma((6,)),
            dma((15,)), dma((15,)),
            dma((1,)), dma((1,)),
            dma((3,)), dma((3,)),
            dma((3,)), dma((3,)),
        ],
        compiler_params=pltpu.CompilerParams(
            collective_id=0, has_side_effects=True, vmem_limit_bytes=56 * 1024 * 1024
        ),
        name="mla_backward",
    )(queries, latent.T, grad_out, doc_ids.reshape(1, ROWS), up_key, up_value)
    grad_queries, grad_latent, grad_up_key, grad_up_value = pl.pallas_call(
        write_out,
        out_shape=(
            shape((ROWS, 768), BF16), shape((LAT + ROPE, ROWS), F32),
            shape((16, 512), F32), shape((16, 512), F32),
        ),
        in_specs=[anywhere] * 3,
        out_specs=(vmem,) * 4,
        scratch_shapes=[
            pltpu.VMEM((8, PACK, 128), BF16), pltpu.VMEM((16, 1024), F32),
            pltpu.VMEM((ROWS, WIDE), F32), dma((3,)),
        ],
        compiler_params=pltpu.CompilerParams(vmem_limit_bytes=63 * 1024 * 1024),
        name="write_out",
    )(*made)
    return grad_queries, grad_latent.T, grad_up_key, grad_up_value


def solution(mesh):
    return jax.shard_map(
        shards,
        mesh=mesh,
        in_specs=(P("ctx", "dp"), P("ctx", None), P("ctx", "dp"), P("ctx"), P(None, "dp"), P(None, "dp")),
        out_specs=(P("ctx", "dp"), P("ctx", None), P("ctx", "dp"), P("ctx", "dp")),
        check_vma=False,
    )
```

```python
import functools
import jax
import jax.numpy as jnp
from jax import lax
from jax.experimental import pallas as pl
from jax.experimental.pallas import tpu as pltpu
from jax.sharding import PartitionSpec as P

LAT = 512
ROPE = 64
NOPE = 128
ROWS = 256
HEADS_HERE = 4
WIDE = 640
PACK = 144
HALVES = ((0, 80), (80, 64))
SLOTS = 5
SCALE = (NOPE + ROPE) ** -0.5
LOG2E = 1.4426950408889634
LOW = -1e30
MESH = pl.DeviceIdType.MESH
F32 = jnp.float32
BF16 = jnp.bfloat16
NT = (((1,), (1,)), ((), ()))
NN = (((1,), (0,)), ((), ()))


def mm(a, b, dims=NN):
    return lax.dot_general(a, b, dims, preferred_element_type=F32)


def side_by_side(first, second):
    return first + pltpu.roll(second, 64, 1)


def packed(block):
    tiles = [block[:, n * 128 : n * 128 + 128] for n in range(4)]
    return jnp.concatenate(tiles + [side_by_side(block[:16, LAT:], block[16:, LAT:])], axis=0)


def kernel(
    q_any, lat_any, go_any, doc_any, upk_any, upv_any,
    dq_any, dlat_any, dup_any,
    dq_ref, all_rows, dup_ref, q_ref, lat_ref, go_ref, docs, win, latent_ref, rope_ref, qx, ups, kv, kxt, latt, probs, gprobs, stats, bias, dqt, dkv,
    part, sib_out, sib_in, ys_out, ys_own, ys_in, own_out, own_in, own_keep,
    g_out, g_in, g_own, gx_out, gx_in, gz_out, gz_in,
    s_in, s_out, s_doc, r_doc, s_z, r_z, s_y, r_y, s_fw, r_fw, s_sib, r_sib, s_ys, r_ys,
    s_own, r_own, s_ag, r_ag, s_g, r_g, s_gx, r_gx, s_gz, r_gz,
):
    dp = lax.axis_index("dp")
    ctx = lax.axis_index("ctx")
    y, zl = lax.div(dp, 2), lax.rem(dp, 2)
    x, zh, core = lax.div(ctx, 8), lax.rem(lax.div(ctx, 2), 4), lax.rem(ctx, 2)
    sib = (dp, ctx + 1 - 2 * core)
    mate = dp + 1 - 2 * zl

    def at_ctx(by):
        return lax.rem(ctx + by + 32, 32)

    def at_y(by):
        return (lax.rem(y + by + 8, 8) * 2 + zl, ctx)

    def at_dp(by):
        return (lax.rem(dp + by + 16, 16), ctx)

    def at_x(by):
        return (dp, lax.rem(x + by + 4, 4) * 8 + zh * 2 + core)

    def at_zh(by):
        return (dp, x * 8 + lax.rem(zh + by + 4, 4) * 2 + core)

    def owner(by, other):
        return (mate if other else dp, at_ctx(by))

    barrier = pltpu.get_barrier_semaphore()
    senders = [(mate, at_ctx(-4)), (dp, at_ctx(-2)), sib, (mate, ctx)]
    senders += [at_y(by) for by in (-2, 2, -1, 1)]
    senders += [at_x(-i) for i in range(1, 4)]
    senders += [at_zh(-1), at_zh(1)]
    for sender in senders:
        pl.semaphore_signal(barrier, inc=1, device_id=sender, device_id_type=MESH)

    loads = [
        pltpu.make_async_copy(src, dst, s_in.at[i])
        for i, (src, dst) in enumerate((
            (lat_any, lat_ref), (doc_any, docs.at[4, 0:1, :]), (upk_any, ups.at[:, :512]),
            (upv_any, ups.at[:, 512:]), (q_any, q_ref), (go_any, go_ref),
        ))
    ]
    for load in loads:
        load.start()

    def remote(src, dst, send, recv, to):
        return pltpu.make_async_remote_copy(
            src_ref=src, dst_ref=dst, send_sem=send, recv_sem=recv,
            device_id=to, device_id_type=MESH,
        )

    loads[0].wait()
    loads[1].wait()
    doc_row = docs[4, 0:1, :]
    line = lax.broadcasted_iota(jnp.int32, (ROWS, ROWS), 0)
    lane = lax.broadcasted_iota(jnp.int32, (ROWS, ROWS), 1)
    rows_of = lat_ref[:LAT, :].T
    tail = jnp.concatenate([lat_ref[LAT:, :].astype(F32), jnp.zeros((64, ROWS), F32)], axis=0).T
    for who in range(8):
        for n in range(4):
            win[4, who, n * 32 : n * 32 + 32, :] = rows_of[who * 32 : who * 32 + 32, n * 128 : n * 128 + 128]
        win[4, who, 128:, :] = side_by_side(
            tail[who * 32 : who * 32 + 16, :], tail[who * 32 + 16 : who * 32 + 32, :]
        ).astype(BF16)

    pl.semaphore_wait(barrier, len(senders))

    def shares(slot, who):
        return win.at[slot, who]

    def along_ctx(index):
        return (mate, at_ctx(4)) if index else (dp, at_ctx(2))

    def tell(index):
        return remote(
            docs.at[4], docs.at[2 - 2 * index], s_doc.at[index], r_doc.at[index], along_ctx(index)
        )

    def along_z(index, half):
        who = lax.rem(y + 4 * half, 8)
        return remote(
            shares(4, who), shares(2 - 2 * index, who), s_z.at[index, half], r_z.at[index, half],
            along_ctx(index),
        )

    for index in (0, 1):
        for half in (0, 1):
            along_z(index, half).start()
        tell(index).start()

    class Forward:
        def __init__(self, slot, to, at):
            self.copies = [
                remote(win.at[slot], win.at[to], s_fw.at[at], r_fw.at[at], sib),
                remote(docs.at[slot], docs.at[to], s_fw.at[2 + at], r_fw.at[2 + at], sib),
            ]

        def start(self):
            for copy in self.copies:
                copy.start()

        def wait_recv(self):
            for copy in self.copies:
                copy.wait_recv()

        def wait_send(self):
            for copy in self.copies:
                copy.wait_send()

    fw_own, fw_mid = Forward(4, 3, 0), Forward(2, 3, 0)
    fw_mid_low = Forward(2, 1, 1)

    def fw_far(who):
        remote(win.at[0, who], win.at[1, who], s_fw.at[1], r_fw.at[1], sib).start()


    @pl.when(core == 0)
    def _():
        fw_own.start()

    passes = ((2, 0, 0), (-2, 0, 0), (1, 0, 0), (-1, 0, 0), (1, 4, 1), (-1, 4, 1))

    def along_y(index, j):
        by, more, _ = passes[j]
        rows = shares(2 - 2 * index, lax.rem(y + more, 8))
        return remote(rows, rows, s_y.at[index, j], r_y.at[index, j], at_y(by))

    for load in loads[2:]:
        load.wait()

    for h in range(HEADS_HERE):
        qx[:, h * 256 : h * 256 + 128] = q_ref[:, h * 192 : h * 192 + 128]
        qx[:, h * 256 + 128 : h * 256 + 256] = jnp.concatenate(
            [q_ref[:, h * 192 + 128 : h * 192 + 192], jnp.zeros((ROWS, 64), BF16)], axis=1
        )
    dqt[...] = jnp.zeros_like(dqt)

    for index in (0, 1):
        for half in (0, 1):
            along_z(index, half).wait_recv()
            for j in range(6):
                if passes[j][2] == half:
                    along_y(index, j).start()
        tell(index).wait_recv()

    @pl.when(core == 1)
    def _():
        for half in (0, 1):
            fw_far(lax.rem(y + 4 * half, 8))
        remote(docs.at[0], docs.at[1], s_fw.at[3], r_fw.at[3], sib).start()

    def scores(t, carry):
        slot = jnp.where(
            t == 0, 4,
            jnp.where(t == 1, 2 + core, jnp.where(t == 2, 3 - core, jnp.where(t == 3, 0, 1))),
        )

        @pl.when(t == 1 + core)
        def _():
            for j in range(6):
                along_y(0, j).wait_recv()

            @pl.when(core == 0)
            def _():
                fw_mid_low.start()

            @pl.when(core == 1)
            def _():
                fw_mid.start()

        @pl.when(t == 3)
        def _():
            for j in (4, 5, 2, 3, 0, 1):
                along_y(1, j).wait_recv()
                by, more, _ = passes[j]

                @pl.when(core == 1)
                def _():
                    fw_far(lax.rem(y - by + more + 8, 8))

        @pl.when(t == 2 - core)
        def _():
            fw_own.wait_recv()

        @pl.when(t == 4)
        def _():
            fw_mid_low.wait_recv()

        start = pl.multiple_of(slot * ROWS, ROWS)
        for who in range(8):
            for n in range(4):
                latent_ref[who * 32 : who * 32 + 32, n * 128 : n * 128 + 128] = win[
                    slot, who, n * 32 : n * 32 + 32, :
                ]
            both_ropes = win[slot, who, 128:, :]
            rope_ref[who * 32 : who * 32 + 16, :] = both_ropes
            rope_ref[who * 32 + 16 : who * 32 + 32, :] = pltpu.roll(
                both_ropes.astype(F32), 64, 1
            ).astype(BF16)
        latent = latent_ref[...]
        rope = rope_ref[...]
        for n in range(4):
            kv[pl.ds(start, ROWS), n * 256 : n * 256 + 256] = mm(
                latent, ups[:, n * 256 : n * 256 + 256]
            ).astype(BF16)
        keys = kv[pl.ds(start, ROWS), :512]
        kxt[slot, :512, :] = keys.T
        kxt[slot, 512:, :] = rope.T
        flipped = latent.T
        for g in range(32):
            row = (g % 2) * 256 + (g // 2) * 16
            latt[row : row + 16, pl.ds(start, ROWS)] = flipped[g * 16 : g * 16 + 16, :]
        key_docs = jnp.sum(jnp.where(line == lane, docs[slot, 0:1, :], 0), axis=1, keepdims=True)
        past = jnp.logical_or(slot < 4, line <= lane)
        bias[...] = jnp.where(jnp.logical_and(key_docs == doc_row, past), 0.0, LOW)
        for h in range(HEADS_HERE):
            cols = slice(h * 256, h * 256 + 256)
            key = kv[pl.ds(start, ROWS), h * 128 : h * 128 + 128]
            value = kv[pl.ds(start, ROWS), 512 + h * 128 : 640 + h * 128]
            s = mm(jnp.concatenate([key, rope], axis=1), qx[:, cols], NT) + bias[...]
            top = jnp.max(s, axis=0, keepdims=True)
            p = jnp.exp2((s - top) * (SCALE * LOG2E))
            gp = mm(value, go_ref[:, h * 128 : h * 128 + 128], NT)
            probs[pl.ds(start, ROWS), cols] = p
            gprobs[pl.ds(start, ROWS), cols] = gp
            stats[0, pl.ds(slot, 1), cols] = top
            stats[1, pl.ds(slot, 1), cols] = jnp.sum(p, axis=0, keepdims=True)
            stats[2, pl.ds(slot, 1), cols] = jnp.sum(p * gp, axis=0, keepdims=True)
        return carry

    lax.fori_loop(0, SLOTS, scores, 0)

    tops = stats[0, 0:SLOTS, :]
    factor = jnp.exp2((tops - jnp.max(tops, axis=0, keepdims=True)) * (SCALE * LOG2E))
    total = jnp.sum(stats[1, 0:SLOTS, :] * factor, axis=0, keepdims=True)
    delta = jnp.sum(stats[2, 0:SLOTS, :] * factor, axis=0, keepdims=True) / total
    stats[0, 0:SLOTS, :] = factor / total
    stats[1, 0:1, :] = delta

    up_low = remote(sib_out.at[0], sib_in.at[0], s_sib.at[0], r_sib.at[0], sib)
    up_high = remote(sib_out.at[1], sib_in.at[1], s_sib.at[1], r_sib.at[1], sib)

    def share_of(by):
        return lax.rem(y + by + 8, 8)

    def hop(index, kind, way):
        side = 0 if way > 0 else 1
        by, dest = ((1, 1), (1, 3), (2, 4), (2, 2))[kind]
        rows = pl.ds(0, PACK)
        if kind == 2:
            rows = pl.ds(80, 64) if side else pl.ds(0, 80)
        return remote(
            ys_out.at[index, share_of(way * dest), rows, :], ys_in.at[index, side, kind, rows, :],
            s_ys.at[index, side, kind], r_ys.at[index, side, kind], at_y(way * by),
        )

    def relay(index):
        for way in (1, -1):
            side = 0 if way > 0 else 1
            hop(index, 1, way).wait_recv()
            hop(index, 2, way).wait_recv()
            dest = share_of(2 * way)
            more = ys_out[index, dest].astype(F32) + ys_in[index, side, 1].astype(F32)
            rows = slice(80, 144) if side else slice(0, 80)
            half = more[rows] + ys_in[index, side, 2, rows, :].astype(F32)
            ys_out[index, dest] = more.astype(BF16)
            ys_out[index, dest, rows, :] = half.astype(BF16)
            hop(index, 3, way).start()

    def grads(t, carry):
        slot = jnp.where(
            t == 0, 4 * core, jnp.where(t < 3, 2 * t - 1, jnp.where(t == 3, 2 - 2 * core, 4 - 2 * core))
        )
        start = pl.multiple_of(slot * ROWS, ROWS)
        rope_sum = jnp.zeros((ROWS, 128), F32)
        for h in range(HEADS_HERE):
            cols = slice(h * 256, h * 256 + 256)
            p = probs[pl.ds(start, ROWS), cols] * stats[0, pl.ds(slot, 1), cols]
            ds = (SCALE * p * (gprobs[pl.ds(start, ROWS), cols] - stats[1, 0:1, cols])).astype(BF16)
            dv = mm(p.astype(BF16), go_ref[:, h * 128 : h * 128 + 128])
            dk = mm(ds, qx[:, cols])
            dkv[pl.ds(start, ROWS), h * 128 : h * 128 + 128] = dk[:, :128].astype(BF16)
            dkv[pl.ds(start, ROWS), 512 + h * 128 : 640 + h * 128] = dv.astype(BF16)
            rope_sum = rope_sum + dk[:, 128:]
            key_t = jnp.concatenate(
                [kxt[slot, h * 128 : h * 128 + 128, :], kxt[slot, 512:, :]], axis=0
            )
            dqt[h] += mm(key_t, ds)
        part[:, LAT:] = rope_sum
        both = dkv[pl.ds(start, ROWS), :]
        for n in range(2):
            part[:, n * 256 : n * 256 + 256] = mm(both, ups[n * 256 : n * 256 + 256, :], NT)

        def add(which):
            part[...] += sib_in[which].astype(F32)

        def leave(index):
            for who in range(8):
                ys_out[index, who] = packed(part[who * 32 : who * 32 + 32, :]).astype(BF16)
            ys_own[index] = packed(part[pl.ds(pl.multiple_of(y * 32, 32), 32), :])
            for kind in (2, 1, 0):
                for way in (1, -1):
                    hop(index, kind, way).start()

        @pl.when(t == 0)
        def _():
            leave(0)

        @pl.when(t == 1)
        def _():
            sib_out[0] = part[...].astype(BF16)
            up_low.start()

        @pl.when(t == 2)
        def _():
            sib_out[1] = part[...].astype(BF16)
            up_high.start()

        @pl.when(t == 3)
        def _():
            up_low.wait_recv()
            add(0)
            leave(1)

        @pl.when(t == 4)
        def _():
            up_high.wait_recv()
            add(1)
            leave(2)
            relay(0)

        return carry

    lax.fori_loop(0, SLOTS, grads, 0)

    theirs = pl.multiple_of((1 - core) * 256, 256)
    mine = pl.multiple_of(core * 256, 256)
    to_sib = remote(g_out, g_in, s_g.at[0], r_g.at[0], sib)
    for n in range(4):
        g_out[:, n * 256 : n * 256 + 256] = mm(
            latt[pl.ds(theirs, 256), :], dkv[:, n * 256 : n * 256 + 256]
        ).astype(BF16)
    to_sib.start()
    relay(1)
    for n in range(4):
        g_own[:, n * 256 : n * 256 + 256] = mm(
            latt[pl.ds(mine, 256), :], dkv[:, n * 256 : n * 256 + 256]
        )
    def to_owner(index, other, half):
        slot, rows = index * 2 + other, pl.ds(*HALVES[half])
        return remote(
            own_out.at[index, rows, :], own_in.at[slot, rows, :],
            s_own.at[slot], r_own.at[slot], owner(-4 + 2 * index, other),
        )

    def by_side(act):
        for mine_is in (0, 1):
            pl.when(zl == mine_is)(functools.partial(act, mine_is))

    def settle(index):
        which = lax.rem(index + 2 * core, 3)
        here = ys_own[index]
        for way in (1, -1):
            for kind in (0, 3):
                hop(index, kind, way).wait_recv()
                here = here + ys_in[index, 0 if way > 0 else 1, kind].astype(F32)
        own_out[which] = here.astype(BF16)

        @pl.when(which == 2)
        def _():
            own_keep[...] = here

        @pl.when(which < 2)
        def _():
            by_side(lambda side: to_owner(which, 0, side).start())

        by_side(lambda side: to_owner(which, 1, 1 - side).start())

    relay(2)
    settle(0)

    for h in range(HEADS_HERE):
        dq = dqt[h].T
        dq_ref[:, h * 192 : h * 192 + 192] = dq[:, :192].astype(BF16)
    dq_out = pltpu.make_async_copy(dq_ref, dq_any, s_out.at[0])
    dq_out.start()
    settle(1)

    to_sib.wait_recv()
    g_own[...] += g_in[...].astype(F32)
    gx_out[...] = g_own[...].astype(BF16)

    def scatter_x(by):
        there = pl.multiple_of(lax.rem(x + by, 4) * 64, 64)
        return remote(
            gx_out.at[pl.ds(there, 64), :], gx_in.at[by - 1], s_gx.at[by - 1], r_gx.at[by - 1], at_x(by)
        )

    for by in (2, 1, 3):
        scatter_x(by).start()

    settle(2)

    pairs = [(index, other) for index in range(3) for other in (0, 1) if index < 2 or other]

    def to_all(by, half):
        mine_rows = all_rows.at[y, pl.ds(*HALVES[half]), :]
        return remote(mine_rows, mine_rows, s_ag.at[by - 1], r_ag.at[by - 1], at_dp(by))

    def gather(side):
        first, count = HALVES[side]
        rows = slice(first, first + count)
        for index, other in pairs:
            to_owner(index, other, side).wait_recv()
        final = own_keep[rows]
        for index, other in pairs:
            final = final + own_in[index * 2 + other, rows, :].astype(F32)
        all_rows[y, rows, :] = final.astype(BF16)
        for by in (8, 7 + 2 * side, 6, 10, 5, 11, 4, 12, 3, 13, 2, 14, 1, 15):
            to_all(by, side).start()

    by_side(gather)

    def pass_on(side):
        to_all(8, side).wait_recv()
        piece = all_rows.at[lax.rem(y + 4, 8), pl.ds(*HALVES[side]), :]
        at = 8 - 2 * side
        remote(piece, piece, s_ag.at[at], r_ag.at[at], (mate, ctx)).start()


    for by in range(1, 4):
        scatter_x(by).wait_recv()
    g_sum = g_own[pl.ds(pl.multiple_of(x * 64, 64), 64), :]
    for by in range(1, 4):
        g_sum = g_sum + gx_in[by - 1].astype(F32)
    g_own[0:64, :] = g_sum
    gz_out[...] = g_sum.astype(BF16)

    def scatter_zh(by):
        there = pl.multiple_of(lax.rem(zh + by, 4) * 16, 16)
        return remote(
            gz_out.at[pl.ds(there, 16), :], gz_in.at[by - 1], s_gz.at[by - 1], r_gz.at[by - 1], at_zh(by)
        )

    for by in (2, 1, 3):
        scatter_zh(by).start()
    by_side(pass_on)

    for by in range(1, 4):
        scatter_zh(by).wait_recv()
    g_last = g_own[pl.ds(pl.multiple_of(zh * 16, 16), 16), :]
    for by in range(1, 4):
        g_last = g_last + gz_in[by - 1].astype(F32)
    dup_ref[...] = g_last
    dup_out = pltpu.make_async_copy(dup_ref, dup_any, s_out.at[1])
    dup_out.start()

    def gathered(side):
        for by in range(1, 16):
            if by != 8:
                to_all(by, (side + by) % 2).wait_recv()

    by_side(gathered)
    dlat_out = pltpu.make_async_copy(all_rows, dlat_any, s_out.at[2])
    dlat_out.start()

    for index in (0, 1):
        for half in (0, 1):
            along_z(index, half).wait_send()
        for j in range(6):
            along_y(index, j).wait_send()
    for index in (0, 1):
        tell(index).wait_send()
    fw_own.wait_send()
    fw_mid_low.wait_send()
    for index in range(3):
        for kind in range(4):
            for way in (1, -1):
                hop(index, kind, way).wait_send()
    up_low.wait_send()
    up_high.wait_send()
    to_sib.wait_send()
    for by in range(1, 4):
        scatter_x(by).wait_send()
        scatter_zh(by).wait_send()

    def left(side):
        for index, other in pairs:
            to_owner(index, other, (side + other) % 2).wait_send()
        for by in range(1, 16):
            to_all(by, side).wait_send()

    by_side(left)
    dq_out.wait()
    dup_out.wait()
    dlat_out.wait()


def write_out(dq_in, dlat_in, dup_in, dq_any, dlat_ref, dupk_ref, dupv_ref, dlat, dup, wide, dq, sem):
    copies = [
        pltpu.make_async_copy(src, dst, sem.at[i])
        for i, (src, dst) in enumerate(((dlat_in, dlat), (dup_in, dup), (dq_in, dq)))
    ]
    for copy in copies:
        copy.start()
    dq_out = pltpu.make_async_copy(dq, dq_any, sem.at[3])
    copies[2].wait()
    dq_out.start()
    copies[0].wait()
    for who in range(8):
        block = dlat[who].astype(F32)
        for n in range(4):
            wide[who * 32 : who * 32 + 32, n * 128 : n * 128 + 128] = block[n * 32 : n * 32 + 32]
        wide[who * 32 : who * 32 + 16, LAT:] = block[128:]
        wide[who * 32 + 16 : who * 32 + 32, LAT:] = pltpu.roll(block[128:], 64, 1)
    dlat_ref[...] = wide[...].T[: LAT + ROPE, :]
    copies[1].wait()
    dupk_ref[...] = dup[:, :512]
    dupv_ref[...] = dup[:, 512:]
    dq_out.wait()


def shards(queries, latent, grad_out, doc_ids, up_key, up_value):
    vmem = pl.BlockSpec(memory_space=pltpu.VMEM)
    anywhere = pl.BlockSpec(memory_space=pl.ANY)
    dma = pltpu.SemaphoreType.DMA
    shape = jax.ShapeDtypeStruct
    made = pl.pallas_call(
        kernel,
        out_shape=(shape((ROWS, 768), BF16), shape((8, PACK, 128), BF16), shape((16, 1024), F32)),
        in_specs=[anywhere] * 6,
        out_specs=(anywhere,) * 3,
        scratch_shapes=[
            pltpu.VMEM((ROWS, 768), BF16),
            pltpu.VMEM((8, PACK, 128), BF16),
            pltpu.VMEM((16, 1024), F32),
            pltpu.VMEM((ROWS, 768), BF16),
            pltpu.VMEM((LAT + ROPE, ROWS), BF16),
            pltpu.VMEM((ROWS, 512), BF16),
            pltpu.VMEM((SLOTS, 8, ROWS), jnp.int32),
            pltpu.VMEM((SLOTS, 8, PACK, 128), BF16),
            pltpu.VMEM((ROWS, LAT), BF16),
            pltpu.VMEM((ROWS, 128), BF16),
            pltpu.VMEM((ROWS, 1024), BF16),
            pltpu.VMEM((LAT, 1024), BF16),
            pltpu.VMEM((SLOTS * ROWS, 1024), BF16),
            pltpu.VMEM((SLOTS, WIDE, ROWS), BF16),
            pltpu.VMEM((LAT, SLOTS * ROWS), BF16),
            pltpu.VMEM((SLOTS * ROWS, 1024), F32),
            pltpu.VMEM((SLOTS * ROWS, 1024), F32),
            pltpu.VMEM((3, 8, 1024), F32),
            pltpu.VMEM((ROWS, ROWS), F32),
            pltpu.VMEM((HEADS_HERE, 256, ROWS), F32),
            pltpu.VMEM((SLOTS * ROWS, 1024), BF16),
            pltpu.VMEM((ROWS, WIDE), F32),
            pltpu.VMEM((2, ROWS, WIDE), BF16),
            pltpu.VMEM((2, ROWS, WIDE), BF16),
            pltpu.VMEM((3, 8, PACK, 128), BF16),
            pltpu.VMEM((3, PACK, 128), F32),
            pltpu.VMEM((3, 2, 4, PACK, 128), BF16),
            pltpu.VMEM((3, PACK, 128), BF16),
            pltpu.VMEM((6, PACK, 128), BF16),
            pltpu.VMEM((PACK, 128), F32),
            pltpu.VMEM((256, 1024), BF16),
            pltpu.VMEM((256, 1024), BF16),
            pltpu.VMEM((256, 1024), F32),
            pltpu.VMEM((256, 1024), BF16),
            pltpu.VMEM((3, 64, 1024), BF16),
            pltpu.VMEM((64, 1024), BF16),
            pltpu.VMEM((3, 16, 1024), BF16),
            dma((6,)),
            dma((3,)),
            dma((2,)), dma((2,)),
            dma((2, 2)), dma((2, 2)),
            dma((2, 6)), dma((2, 6)),
            dma((4,)), dma((4,)),
            dma((2,)), dma((2,)),
            dma((3, 2, 4)), dma((3, 2, 4)),
            dma((6,)), dma((6,)),
            dma((15,)), dma((15,)),
            dma((1,)), dma((1,)),
            dma((3,)), dma((3,)),
            dma((3,)), dma((3,)),
        ],
        compiler_params=pltpu.CompilerParams(
            collective_id=0, has_side_effects=True, vmem_limit_bytes=56 * 1024 * 1024
        ),
        name="mla_backward",
    )(queries, latent.T, grad_out, doc_ids.reshape(1, ROWS), up_key, up_value)
    grad_queries, grad_latent, grad_up_key, grad_up_value = pl.pallas_call(
        write_out,
        out_shape=(
            shape((ROWS, 768), BF16), shape((LAT + ROPE, ROWS), F32),
            shape((16, 512), F32), shape((16, 512), F32),
        ),
        in_specs=[anywhere] * 3,
        out_specs=(anywhere, vmem, vmem, vmem),
        scratch_shapes=[
            pltpu.VMEM((8, PACK, 128), BF16), pltpu.VMEM((16, 1024), F32),
            pltpu.VMEM((ROWS, WIDE), F32), pltpu.VMEM((ROWS, 768), BF16), dma((4,)),
        ],
        compiler_params=pltpu.CompilerParams(vmem_limit_bytes=63 * 1024 * 1024),
        name="write_out",
    )(*made)
    return grad_queries, grad_latent.T, grad_up_key, grad_up_value


def solution(mesh):
    return jax.shard_map(
        shards,
        mesh=mesh,
        in_specs=(P("ctx", "dp"), P("ctx", None), P("ctx", "dp"), P("ctx"), P(None, "dp"), P(None, "dp")),
        out_specs=(P("ctx", "dp"), P("ctx", None), P("ctx", "dp"), P("ctx", "dp")),
        check_vma=False,
    )
```
